32 devices in a mesh: rows: 8 (over y, x, core), ffn: 4 (over z).
Axes of the slice: x: 2, y: 2, z: 4, core: 2. Of those that a mesh axis runs over, the one named last changes fastest.
Arguments:
- source: bfloat16 [16, 1024, 512], P('rows', 'ffn'), may hold values from -6 to 6
- target: bfloat16 [16, 1024, 512], P('rows', 'ffn'), may hold values from -6 to 6
- cotangent: bfloat16 [16, 1024, 512], P('rows', 'ffn'), may hold values from -6 to 6
- source_lengths: int32 [16], P('rows'), may hold values from 128 to 1024, as said below
- target_lengths: int32 [16], P('rows'), may hold values from 128 to 1024, as said below
- routes: int32 [3, 16, 1024, 2], P(None, 'rows', 'ffn'), may hold values from 0 to 7, all different within a row
- norm_gain: float32 [5, 512], replicated, may hold values from 0.5 to 1.5
- norm_shift: float32 [5, 512], replicated, may hold values from -0.9 to 0.9
- moa_router: bfloat16 [3, 512, 8], replicated, may hold values from -0.1875 to 0.1875
- moa_query: bfloat16 [3, 512, 512], replicated, may hold values from -0.5 to 0.5
- moa_keyval: bfloat16 [3, 512, 128], replicated, may hold values from -0.25 to 0.25
- moa_out: bfloat16 [3, 512, 512], replicated, may hold values from -4 to 4
- ffn_in: bfloat16 [2, 512, 2048], P(None, None, 'ffn'), may hold values from -0.25 to 0.25
- ffn_in_bias: bfloat16 [2, 2048], P(None, 'ffn'), may hold values from -0.8984375 to 0.8984375
- ffn_out: bfloat16 [2, 2048, 512], P(None, 'ffn'), may hold values from -0.125 to 0.125
- ffn_out_bias: bfloat16 [2, 512], replicated, may hold values from -0.8984375 to 0.8984375
Outputs:
- memory: float32 [16, 1024, 512], P('rows', 'ffn')
- decoded: float32 [16, 1024, 512], P('rows', 'ffn')
- source_grad: float32 [16, 1024, 512], P('rows', 'ffn')
- target_grad: float32 [16, 1024, 512], P('rows', 'ffn')
- memory_grad: float32 [16, 1024, 512], P('rows', 'ffn')
- gain_grad: float32 [4, 512], replicated
- shift_grad: float32 [4, 512], replicated
- final_norm_grad: float32 [2, 512], replicated
- router_grad: float32 [3, 512, 8], replicated
- query_grad: float32 [3, 512, 512], replicated
- keyval_grad: float32 [3, 512, 128], replicated
- out_grad: float32 [3, 512, 512], replicated
- ffn_in_grad: float32 [2, 512, 2048], P(None, None, 'ffn')
- ffn_in_bias_grad: float32 [2, 2048], P(None, 'ffn')
- ffn_out_grad: float32 [2, 2048, 512], P(None, 'ffn')
- ffn_out_bias_grad: float32 [2, 512], replicated
- routed_counts: int32 [3, 8], replicated
The draws below stay inside these ranges and needn't reach their ends.
Inputs may be any that keep to these rules, and one draw needn't show every extreme that they name: `source_lengths`: in each aligned pair of sequences, one has length 1024; some sequence has length 128. `target_lengths`: in each aligned pair of sequences, one has length 1024; some sequence has length 128.
All inputs are finite; a program needn't handle non-finite values.
Results may differ from the reference program's by a relative error of at most 0.039.
The reference program's roundings to bfloat16 on the way count: a program that leaves them out, or rounds other values in their place, can miss the bound.
Values may be sent and summed in bfloat16 or wider, within the bound.
No kernel may reach another device: no remote copies, remote signals or barrier semaphores. Data moves between devices by JAX's collectives and lax.ppermute only.
A program may use at most 128 MiB of HBM per device.

```python
import jax
import jax.numpy as jnp
from jax import lax

D = 512
HEAD = 64
EXPERTS = 8
FF = 2048
TOPK = 2
LEN = 1024
SEQS = 16


def lengths_from(key):
    pairs = SEQS // 2
    base_len = jax.random.randint(jax.random.fold_in(key, 1), (SEQS,), LEN // 8, LEN + 1)
    which_one = jax.random.randint(jax.random.fold_in(key, 2), (pairs,), 0, 2)
    member = jnp.arange(SEQS, dtype=jnp.int32) % 2
    pair_idx = jnp.arange(SEQS, dtype=jnp.int32) // 2
    full_len = member == which_one[pair_idx]
    least_len = (pair_idx == 0) & (member != which_one[0])
    return jnp.where(full_len, LEN, jnp.where(least_len, LEN // 8, base_len)).astype(jnp.int32)


def draw_source_lengths(key, part):
    key = jax.random.fold_in(key, 11)
    return lengths_from(key)


def draw_target_lengths(key, part):
    key = jax.random.fold_in(key, 12)
    return lengths_from(key)


def block_levels(stream_key, extent, cuts, least, high):
    loudness = 1.0
    for position, shards_of in cuts:
        heights = jax.random.uniform(jax.random.fold_in(jax.random.fold_in(stream_key, 6), position), (shards_of,), jnp.float32, least / len(cuts), high / len(cuts))
        loudness = loudness * jnp.repeat(jnp.exp(heights), extent[position] // shards_of).reshape((-1,) + (1,) * (len(extent) - 1 - position))
    return loudness


def different_ones(key, rows, count, top, lift):
    ranking = jax.random.permutation(jax.random.fold_in(key, 1), count)
    boost = ranking
    for power in range(3):
        boost = boost * boost // count
    boost = boost * lift // count
    tickets = jax.random.randint(jax.random.fold_in(key, 2), (rows, count), 0, 4096) + boost
    sure = jax.random.permutation(jax.random.fold_in(key, 3), rows)[jnp.arange(count) % rows]
    tickets = jnp.where(jnp.arange(rows)[:, None] == sure[None, :], 1 << 14, tickets)
    score = tickets * count + jnp.arange(count)
    return lax.top_k(score.astype(jnp.int32), top)[1].astype(jnp.int32)


def noise(stream_key, shape, scale, most, shards=(), kind=jnp.bfloat16):
    drawn = jax.random.normal(stream_key, shape, jnp.float32) * scale
    if len(shards) > 0:
        drawn = block_levels(stream_key, shape, shards, -0.22, 0.18) * drawn
    return jnp.clip(drawn, min=-most, max=most).astype(kind)


def setup_inputs(seed: int = 0) -> dict:
    key_of = jax.random.split(jax.random.key(seed), 17)
    source = noise(key_of[0], (SEQS, LEN, D), 1.0, 6.0, ((0, 8), (1, 4)))
    target = noise(key_of[1], (SEQS, LEN, D), 1.0, 6.0, ((0, 8), (1, 4)))
    cotangent = noise(key_of[2], (SEQS, LEN, D), 1.0, 6.0, ((0, 8), (1, 4)))
    source_lengths = draw_source_lengths(jax.random.fold_in(key_of[16], 71), 0)
    target_lengths = draw_target_lengths(jax.random.fold_in(key_of[16], 71), 0)
    routes = different_ones(key_of[5], 3 * SEQS * LEN, EXPERTS, TOPK, 2048).reshape((3, SEQS, LEN, TOPK))
    norm_gain = jnp.clip(1.0 + 0.1 * jax.random.normal(key_of[6], (5, D), jnp.float32), 0.5, 1.5)
    norm_shift = noise(key_of[7], (5, D), 0.15, 0.9, (), jnp.float32)
    moa_router = noise(key_of[8], (3, D, EXPERTS), (2 * D) ** -0.5, 0.1875)
    moa_query = noise(key_of[9], (3, D, EXPERTS * HEAD), (D // 4) ** -0.5, 0.5)
    moa_keyval = noise(key_of[10], (3, D, 2 * HEAD), D ** -0.5, 0.25)
    moa_out = noise(key_of[11], (3, EXPERTS * HEAD, D), 2 ** -0.5, 4.0)
    ffn_in = noise(key_of[12], (2, D, FF), D ** -0.5, 0.25, ((2, 4),))
    ffn_in_bias = noise(key_of[13], (2, FF), 0.15, 0.8984375, ((1, 4),))
    ffn_out = noise(key_of[14], (2, FF, D), FF ** -0.5, 0.125, ((1, 4),))
    ffn_out_bias = noise(key_of[15], (2, D), 0.15, 0.8984375)
    return dict(source=source, target=target, cotangent=cotangent, source_lengths=source_lengths, target_lengths=target_lengths, routes=routes, norm_gain=norm_gain, norm_shift=norm_shift, moa_router=moa_router, moa_query=moa_query, moa_keyval=moa_keyval, moa_out=moa_out, ffn_in=ffn_in, ffn_in_bias=ffn_in_bias, ffn_out=ffn_out, ffn_out_bias=ffn_out_bias)


EPS = 1e-05
PRECISE = lax.Precision.HIGHEST

@jax.custom_vjp
def low(v):
    return lax.optimization_barrier(v.astype(jnp.bfloat16)).astype(jnp.float32)

@jax.custom_vjp
def low_back(v):
    return v

def low_keep(v):
    return (low(v), None)

def low_pass(kept, grad):
    return (grad,)

def back_keep(v):
    return (v, None)

def back_low(kept, grad):
    return (low(grad),)
low.defvjp(low_keep, low_pass)
low_back.defvjp(back_keep, back_low)

def matmul(left, right):
    return jnp.dot(left, right, precision=PRECISE)

def softmax_last(values):
    maximum = lax.optimization_barrier(jnp.max(values, -1, keepdims=True))
    raised = jnp.exp(values - maximum)
    return raised / lax.optimization_barrier(jnp.sum(raised, -1, keepdims=True))

def layer_norm(values, gain_row, shift_row):
    center = values - lax.optimization_barrier(jnp.mean(values, -1, keepdims=True))
    spread = lax.optimization_barrier(jnp.mean(center * center, -1, keepdims=True))
    return center * lax.rsqrt(spread + EPS) * gain_row + shift_row

def attend(queries_in, keys_in, route_ids, allowed, router, query_proj, keyval, output):
    logits = matmul(queries_in, router)
    picked = (route_ids[:, :, None] == jnp.arange(EXPERTS, dtype=jnp.int32)[None, None, :]).astype(jnp.float32)
    gate_vals = softmax_last(lax.optimization_barrier(jnp.sum(picked * logits[:, None, :], -1)))
    queries = low(low_back(matmul(queries_in, query_proj))).reshape(LEN, EXPERTS, HEAD)
    slot_query = lax.optimization_barrier(jnp.sum(picked[:, :, :, None] * queries[:, None, :, :], 2))
    key_value = low(low_back(matmul(keys_in, keyval)))
    scores = low_back(jnp.einsum('lkd,md->lkm', slot_query, key_value[:, :HEAD], precision=PRECISE) * float(HEAD) ** (-0.5))
    weights = softmax_last(jnp.where(allowed, scores, -1e+30))
    attended = low_back(jnp.einsum('lkm,md->lkd', low(weights), key_value[:, HEAD:], precision=PRECISE))
    mixed_rows = low(lax.optimization_barrier(jnp.sum(picked[:, :, :, None] * (gate_vals[:, :, None] * attended)[:, :, None, :], 1))).reshape(LEN, EXPERTS * HEAD)
    return low_back(matmul(mixed_rows, output))

def feed(normed, weight_in, bias_in, weight_out):
    pre_act = low_back(matmul(normed, weight_in) + bias_in)
    return low_back(matmul(low(jax.nn.gelu(pre_act)), weight_out))

def pair_forward(params, source_seq, target_seq, memory_shift, source_len, target_len, route_ids):
    gain_rows, shift_rows, router, query_proj, keyval, output, weight_in, bias_in, weight_out, bias_out = params
    positions = jnp.arange(LEN, dtype=jnp.int32)
    source_ok = (positions < source_len)[None, None, :]
    target_ok = (positions < target_len)[None, None, :] & (positions[None, None, :] <= positions[:, None, None])
    hidden = low(layer_norm(source_seq, gain_rows[0], shift_rows[0]))
    state_now = source_seq + attend(hidden, hidden, route_ids[0], source_ok, router[0], query_proj[0], keyval[0], output[0])
    hidden = low(layer_norm(state_now, gain_rows[1], shift_rows[1]))
    memory = state_now + feed(hidden, weight_in[0], bias_in[0], weight_out[0]) + bias_out[0] + memory_shift
    hidden = low(layer_norm(target_seq, gain_rows[2], shift_rows[2]))
    state_now = target_seq + attend(hidden, hidden, route_ids[1], target_ok, router[1], query_proj[1], keyval[1], output[1])
    hidden = low(layer_norm(state_now, gain_rows[3], shift_rows[3]))
    state_now = state_now + attend(hidden, low(memory), route_ids[2], source_ok, router[2], query_proj[2], keyval[2], output[2])
    hidden = low(layer_norm(state_now, gain_rows[4], shift_rows[4]))
    decoded = state_now + feed(hidden, weight_in[1], bias_in[1], weight_out[1]) + bias_out[1]
    return (memory, decoded)

def reference(source, target, cotangent, source_lengths, target_lengths, routes, norm_gain, norm_shift, moa_router, moa_query, moa_keyval, moa_out, ffn_in, ffn_in_bias, ffn_out, ffn_out_bias):
    params = tuple((weight.astype(jnp.float32) for weight in (norm_gain, norm_shift, moa_router, moa_query, moa_keyval, moa_out, ffn_in, ffn_in_bias, ffn_out, ffn_out_bias)))
    positions = jnp.arange(LEN, dtype=jnp.int32)
    source_valid = positions[None, :] < source_lengths[:, None]
    target_valid = positions[None, :] < target_lengths[:, None]
    seed_grad = cotangent.astype(jnp.float32) * target_valid[:, :, None].astype(jnp.float32)
    routes_seq = jnp.moveaxis(routes, 1, 0)

    def forward(params, sources, targets, shifts):

        def single(item_set):
            return pair_forward(params, item_set[0], item_set[1], item_set[2], item_set[3], item_set[4], item_set[5])
        return lax.map(jax.checkpoint(single), (sources, targets, shifts, source_lengths, target_lengths, routes_seq))
    shifts = jnp.zeros(source.shape, jnp.float32)
    outputs, pullback = jax.vjp(forward, params, source.astype(jnp.float32), target.astype(jnp.float32), shifts)
    gradients = pullback((jnp.zeros_like(outputs[0]), seed_grad))
    param_grads = gradients[0]
    valid_rows = jnp.stack([source_valid, target_valid, target_valid])
    routed_hits = (routes[..., None] == jnp.arange(EXPERTS, dtype=jnp.int32)) & valid_rows[:, :, :, None, None]
    routed_counts = lax.optimization_barrier(jnp.sum(routed_hits.astype(jnp.int32), axis=(1, 2, 3)))
    final_norm_grad = jnp.stack([param_grads[0][4], param_grads[1][4]])
    return (outputs[0], outputs[1], gradients[1], gradients[2], gradients[3], param_grads[0][:4], param_grads[1][:4], final_norm_grad, param_grads[2], param_grads[3], param_grads[4], param_grads[5], param_grads[6], param_grads[7], param_grads[8], param_grads[9], routed_counts)
```

```python
import jax
import jax.numpy as jnp
from jax import lax
from jax.sharding import PartitionSpec as P

EPS = 1e-05
PRECISE = lax.Precision.HIGHEST


def softmax_last(values):
    maximum = jnp.max(values, -1, keepdims=True)
    raised = jnp.exp(values - maximum)
    return raised / jnp.sum(raised, -1, keepdims=True)


def norm_forward(values, gain_row, shift_row):
    center = values - jnp.mean(values, -1, keepdims=True)
    inverse = lax.rsqrt(jnp.mean(center * center, -1, keepdims=True) + EPS)
    normal = center * inverse
    return ((normal * gain_row + shift_row).astype(jnp.bfloat16), (normal, inverse))


def norm_backward(upstream, kept_items, gain_row):
    normal, inverse = kept_items
    scaled = upstream * gain_row
    result = inverse * (
        scaled
        - jnp.mean(scaled, -1, keepdims=True)
        - normal * jnp.mean(scaled * normal, -1, keepdims=True)
    )
    return (result, jnp.sum(upstream * normal, (0, 1)), jnp.sum(upstream, (0, 1)))


def attend_forward(query_in, key_in, route_ids, allowed, weights):
    router, query_proj, keyval, output = weights
    groups, row_count, model_width = query_in.shape
    tokens_here = groups * row_count
    experts = router.shape[1]
    head_dim = keyval.shape[1] // 2
    flat_query = query_in.reshape(tokens_here, model_width)
    flat_key = key_in.reshape(tokens_here, model_width)
    logits = jnp.dot(flat_query, router, preferred_element_type=jnp.float32)
    picked = (
        route_ids.reshape(tokens_here, 2)[:, :, None]
        == jnp.arange(experts, dtype=jnp.int32)[None, None, :]
    )
    gate_vals = softmax_last(jnp.sum(jnp.where(picked, logits[:, None, :], 0.0), -1))
    queries = (
        jnp.dot(flat_query, query_proj, preferred_element_type=jnp.float32)
        .astype(jnp.bfloat16)
        .reshape(tokens_here, experts, head_dim)
    )
    slot_query = jnp.sum(
        jnp.where(picked[:, :, :, None], queries[:, None, :, :], jnp.zeros((), jnp.bfloat16)), 2
    )
    key_value = (
        jnp.dot(flat_key, keyval, preferred_element_type=jnp.float32)
        .astype(jnp.bfloat16)
        .reshape(groups, row_count, 2 * head_dim)
    )
    gathered = gather_positions(key_value)
    query_rows = slot_query.reshape(groups, row_count * 2, head_dim)
    score_scale = float(head_dim) ** (-0.5)
    scores = (
        jnp.einsum(
            "gqd,gmd->gqm",
            query_rows,
            gathered[:, :, :head_dim],
            preferred_element_type=jnp.float32,
        )
        * score_scale
    )
    masked = jnp.where(allowed, scores, -1e30)
    maximum = jnp.max(masked, -1, keepdims=True)
    raised = jnp.exp(masked - maximum)
    totals = jnp.sum(raised, -1, keepdims=True)
    log_total = maximum + jnp.log(totals)
    weights_low = (raised / totals).astype(jnp.bfloat16)
    attended = jnp.einsum(
        "gqm,gmd->gqd", weights_low, gathered[:, :, head_dim:], preferred_element_type=jnp.float32
    ).reshape(tokens_here, 2, head_dim)
    mixed_rows = jnp.sum(
        jnp.where(picked[:, :, :, None], (gate_vals[:, :, None] * attended)[:, :, None, :], 0.0), 1
    )
    mixed_rows = mixed_rows.astype(jnp.bfloat16).reshape(tokens_here, experts * head_dim)
    result = jnp.dot(mixed_rows, output, preferred_element_type=jnp.float32).reshape(
        groups, row_count, model_width
    )
    return (
        result,
        (
            flat_query,
            flat_key,
            picked,
            gate_vals,
            query_rows,
            gathered,
            log_total,
            attended,
            mixed_rows,
        ),
    )


def attend_backward(upstream, kept_items, allowed, weights):
    router, query_proj, keyval, output = weights
    (
        flat_query,
        flat_key,
        picked,
        gate_vals,
        query_rows,
        gathered,
        log_total,
        attended,
        mixed_rows,
    ) = kept_items
    groups, row_count, model_width = upstream.shape
    tokens_here = groups * row_count
    experts = router.shape[1]
    head_dim = keyval.shape[1] // 2
    branch_grad = upstream.reshape(tokens_here, model_width).astype(jnp.bfloat16)
    output_grad = jnp.einsum(
        "ne,nd->ed", mixed_rows, branch_grad, preferred_element_type=jnp.float32
    )
    mixed_grad = jnp.einsum(
        "nd,ed->ne", branch_grad, output, preferred_element_type=jnp.float32
    ).reshape(tokens_here, experts, head_dim)
    slot_grad = jnp.sum(jnp.where(picked[:, :, :, None], mixed_grad[:, None, :, :], 0.0), 2)
    attended_grad = (
        (gate_vals[:, :, None] * slot_grad)
        .astype(jnp.bfloat16)
        .reshape(groups, row_count * 2, head_dim)
    )
    gate_grad = jnp.sum(attended * slot_grad, -1)
    chosen_grad = gate_vals * (gate_grad - jnp.sum(gate_vals * gate_grad, -1, keepdims=True))
    logit_grad = jnp.sum(jnp.where(picked, chosen_grad[:, :, None], 0.0), 1)
    router_grad = jnp.dot(flat_query.astype(jnp.float32).T, logit_grad, precision=PRECISE)
    input_grad = jnp.dot(logit_grad, router.astype(jnp.float32).T, precision=PRECISE)
    key_rows = gathered[:, :, :head_dim]
    value_rows = gathered[:, :, head_dim:]
    score_scale = float(head_dim) ** (-0.5)
    scores = (
        jnp.einsum("gqd,gmd->gqm", query_rows, key_rows, preferred_element_type=jnp.float32)
        * score_scale
    )
    weights_now = jnp.exp(jnp.where(allowed, scores, -1e30) - log_total)
    value_grad = jnp.einsum(
        "gqm,gqd->gmd",
        weights_now.astype(jnp.bfloat16),
        attended_grad,
        preferred_element_type=jnp.float32,
    )
    weight_grad = jnp.einsum(
        "gqd,gmd->gqm", attended_grad, value_rows, preferred_element_type=jnp.float32
    )
    score_grad = (
        weights_now * (weight_grad - jnp.sum(weights_now * weight_grad, -1, keepdims=True))
    ).astype(jnp.bfloat16)
    query_rows_grad = (
        jnp.einsum("gqm,gmd->gqd", score_grad, key_rows, preferred_element_type=jnp.float32)
        * score_scale
    )
    key_grad = (
        jnp.einsum("gqm,gqd->gmd", score_grad, query_rows, preferred_element_type=jnp.float32)
        * score_scale
    )
    joined = jnp.concatenate([key_grad, value_grad], -1)
    keyval_rows = scatter_positions(joined.astype(jnp.bfloat16)).reshape(
        tokens_here, 2 * head_dim
    )
    placed = jnp.where(
        picked[:, :, :, None], query_rows_grad.reshape(tokens_here, 2, 1, head_dim), 0.0
    )
    query_grad_rows = (
        jnp.sum(placed, 1).astype(jnp.bfloat16).reshape(tokens_here, experts * head_dim)
    )
    query_grad = jnp.einsum(
        "nd,ne->de", flat_query, query_grad_rows, preferred_element_type=jnp.float32
    )
    input_grad = input_grad + jnp.einsum(
        "ne,de->nd", query_grad_rows, query_proj, preferred_element_type=jnp.float32
    )
    keyval_grad = jnp.einsum("nd,ne->de", flat_key, keyval_rows, preferred_element_type=jnp.float32)
    source_part = jnp.einsum("ne,de->nd", keyval_rows, keyval, preferred_element_type=jnp.float32)
    shape_out = (groups, row_count, model_width)
    return (
        input_grad.reshape(shape_out),
        source_part.reshape(shape_out),
        (router_grad, query_grad, keyval_grad, output_grad),
    )


def swap(values, axis_name, bit):
    size = lax.axis_size(axis_name)
    return lax.ppermute(values, axis_name, [(i, i ^ bit) for i in range(size)])


def bits_of(axis_name):
    size = lax.axis_size(axis_name)
    return [1 << k for k in range(size.bit_length() - 1)]


def relative(values, axis_name):
    me = lax.axis_index(axis_name)
    size = values.shape[0]
    rest = values.shape[1:]
    for bit in bits_of(axis_name):
        split = values.reshape((size // (2 * bit), 2, bit) + rest)
        values = jnp.where((me & bit) != 0, split[:, ::-1], split).reshape((size,) + rest)
    return values


def gather_relative(values, axis_name):
    size = lax.axis_size(axis_name)
    return jnp.stack([values] + [swap(values, axis_name, k) for k in range(1, size)])


def gather_positions(key_value):
    groups, row_count, width = key_value.shape
    blocks = relative(gather_relative(key_value, "ffn"), "ffn")
    return jnp.swapaxes(blocks, 0, 1).reshape(groups, -1, width)


def scatter_positions(partial_rows):
    groups, length, width = partial_rows.shape
    size = lax.axis_size("ffn")
    blocks = jnp.swapaxes(partial_rows.reshape(groups, size, length // size, width), 0, 1)
    blocks = relative(blocks, "ffn")
    return scatter_relative(blocks, "ffn").astype(jnp.bfloat16)


def scatter_relative(blocks, axis_name):
    total = blocks[0].astype(jnp.float32)
    for k in range(1, blocks.shape[0]):
        total = total + swap(blocks[k].astype(jnp.bfloat16), axis_name, k).astype(jnp.float32)
    return total


def orders():
    bits = bits_of("rows")
    return bits[1:], bits[1:][::-1]


def rows_gather(values):
    half = values.shape[0] // 2
    size = lax.axis_size("rows")
    parts = []
    for order, part in zip(orders(), (values[:half], values[half:])):
        buffer, index = part[None], [0]
        for bit in order:
            buffer = jnp.concatenate([buffer, swap(buffer, "rows", bit)])
            index = index + [i ^ bit for i in index]
        parts.append((buffer, index))
    joined = jnp.concatenate(
        [buffer[jnp.array([index.index(2 * k) for k in range(size // 2)])] if index != [2 * k for k in range(size // 2)] else buffer for buffer, index in parts], 1
    )
    both = jnp.stack([joined, swap(joined, "rows", 1)], 1)
    return both.reshape((size,) + values.shape)


def rows_scatter(blocks):
    size, count = blocks.shape[:2]
    split = blocks.reshape((size // 2, 2) + blocks.shape[1:])
    kept = split[:, 0].astype(jnp.float32) + swap(
        split[:, 1].astype(jnp.bfloat16), "rows", 1
    ).astype(jnp.float32)
    half = count // 2
    results = []
    for order, part in zip(orders(), (kept[:, :half], kept[:, half:])):
        index = [2 * k for k in range(size // 2)]
        for bit in order[::-1]:
            keep = [n for n, i in enumerate(index) if not i & bit]
            send = [index.index(index[n] ^ bit) for n in keep]
            sent = jnp.stack([part[n] for n in send]).astype(jnp.bfloat16)
            received = swap(sent, "rows", bit)
            part = jnp.stack([part[n] for n in keep]) + received.astype(jnp.float32)
            index = [index[n] for n in keep]
        results.append(part[0])
    return jnp.concatenate(results)


def add_everywhere(values):
    for axis_name in ("rows", "ffn"):
        for bit in bits_of(axis_name):
            values = values + swap(values, axis_name, bit)
    return values


def gather_weights(weight_in, bias_in, weight_out):
    size = lax.axis_size("rows")
    hidden, width = weight_out.shape
    piece = hidden // size
    me = lax.axis_index("rows")
    bias_rows = jnp.zeros((size, 16, width), weight_out.dtype)
    bias_rows = bias_rows.at[:, 0, :piece].set(bias_in.reshape(size, piece))
    pieces = jnp.concatenate(
        [
            weight_in.T.reshape(size, piece, width),
            weight_out.reshape(size, piece, width),
            bias_rows,
        ],
        1,
    )
    mine = lax.dynamic_index_in_dim(pieces, me, 0, keepdims=False)
    crossed = gather_relative(mine, "ffn")
    planes = lax.axis_size("ffn")
    rows_here = mine.shape[0]
    full = rows_gather(crossed.reshape(planes * rows_here, width))
    full = full.reshape(size, planes, rows_here, width)
    first = full[:, :, :piece].reshape(-1, width)
    second = full[:, :, piece : 2 * piece].reshape(-1, width)
    bias = full[:, :, 2 * piece, :piece].reshape(-1)
    return first, second, bias


def reduce_feed(first_grad, second_grad, bias_grad):
    size, planes = lax.axis_size("rows"), lax.axis_size("ffn")
    width = first_grad.shape[1]
    piece = first_grad.shape[0] // (size * planes)
    bias_rows = jnp.zeros((size, planes, 16, width), jnp.float32)
    bias_rows = bias_rows.at[:, :, 0, :piece].set(bias_grad.reshape(size, planes, piece))
    pieces = jnp.concatenate(
        [
            first_grad.reshape(size, planes, piece, width),
            second_grad.reshape(size, planes, piece, width),
            bias_rows,
        ],
        2,
    )
    rows_here = pieces.shape[2]
    summed = rows_scatter(pieces.reshape(size, planes * rows_here, width))
    summed = scatter_relative(summed.reshape(planes, rows_here, width), "ffn")
    full = relative(rows_gather(summed.astype(jnp.bfloat16)), "rows").astype(jnp.float32)
    hidden = size * piece
    return (
        full[:, :piece].reshape(hidden, width).T,
        full[:, 2 * piece, :piece].reshape(hidden),
        full[:, piece : 2 * piece].reshape(hidden, width),
    )


def reduce_attention(query_grad, keyval_grad, output_grad):
    size, planes = lax.axis_size("rows"), lax.axis_size("ffn")
    width = query_grad.shape[1]
    stacked = jnp.concatenate([query_grad, output_grad, keyval_grad.T]).astype(jnp.bfloat16)
    count = stacked.shape[0] // size
    lanes = width // planes
    blocks = relative(stacked.reshape(size, count, width), "rows")
    summed = rows_scatter(blocks)
    by_plane = jnp.swapaxes(summed.reshape(count, planes, lanes), 0, 1)
    own = scatter_relative(relative(by_plane, "ffn"), "ffn").astype(jnp.bfloat16)
    planes_full = relative(gather_relative(own, "ffn"), "ffn")
    rows_here = jnp.swapaxes(planes_full, 0, 1).reshape(count, width)
    full = relative(rows_gather(rows_here), "rows").reshape(-1, width).astype(jnp.float32)
    model = query_grad.shape[0]
    return full[:model], full[2 * model :].T, full[model : 2 * model]


def feed_forward(normed, weights):
    first, second, bias = weights
    groups, row_count, model_width = normed.shape
    flat_rows = normed.reshape(-1, model_width)
    pre_act = jnp.einsum("nd,fd->nf", flat_rows, first, preferred_element_type=jnp.float32)
    pre_act = pre_act + bias.astype(jnp.float32)
    act_rows = jax.nn.gelu(pre_act).astype(jnp.bfloat16)
    result = jnp.dot(act_rows, second, preferred_element_type=jnp.float32).reshape(normed.shape)
    return (result, (flat_rows, pre_act, act_rows, first, second))


def feed_backward(upstream, kept_items):
    flat_rows, pre_act, act_rows, first, second = kept_items
    groups, row_count, model_width = upstream.shape
    rows_grad = upstream.astype(jnp.bfloat16).reshape(-1, model_width)
    act_grad = jnp.einsum("nd,fd->nf", rows_grad, second, preferred_element_type=jnp.float32)
    unused, pull_back = jax.vjp(jax.nn.gelu, pre_act)
    pre_grad = pull_back(act_grad)[0].astype(jnp.bfloat16)
    second_grad = jnp.einsum("nf,nd->fd", act_rows, rows_grad, preferred_element_type=jnp.float32)
    first_grad = jnp.einsum("nf,nd->fd", pre_grad, flat_rows, preferred_element_type=jnp.float32)
    bias_grad = jnp.sum(pre_grad.astype(jnp.float32), 0)
    normed_grad = jnp.dot(pre_grad, first, preferred_element_type=jnp.float32)
    reduced = reduce_feed(first_grad, second_grad, bias_grad)
    return (normed_grad.reshape(upstream.shape), reduced)


def body(
    source,
    target,
    cotangent,
    source_lengths,
    target_lengths,
    routes,
    norm_gain,
    norm_shift,
    moa_router,
    moa_query,
    moa_keyval,
    moa_out,
    ffn_in,
    ffn_in_bias,
    ffn_out,
    ffn_out_bias,
):
    groups, row_count, model_width = source.shape
    length = row_count * lax.axis_size("ffn")
    query_pos = lax.axis_index("ffn") * row_count + jnp.arange(row_count, dtype=jnp.int32)
    key_pos = jnp.arange(length, dtype=jnp.int32)
    source_keys = (key_pos[None, :] < source_lengths[:, None])[:, None, :]
    target_keys = (key_pos[None, :] < target_lengths[:, None])[:, None, :] & (
        key_pos[None, None, :] <= jnp.repeat(query_pos, 2)[None, :, None]
    )
    source_rows = query_pos[None, :] < source_lengths[:, None]
    target_rows = query_pos[None, :] < target_lengths[:, None]
    feed_weights = [
        gather_weights(ffn_in[layer], ffn_in_bias[layer], ffn_out[layer]) for layer in range(2)
    ]
    moa_weights = [
        (moa_router[layer_idx], moa_query[layer_idx], moa_keyval[layer_idx], moa_out[layer_idx])
        for layer_idx in range(3)
    ]
    source_f = source.astype(jnp.float32)
    normed, norm_zero = norm_forward(source_f, norm_gain[0], norm_shift[0])
    branch, attend_zero = attend_forward(normed, normed, routes[0], source_keys, moa_weights[0])
    middle = source_f + branch
    normed, norm_one = norm_forward(middle, norm_gain[1], norm_shift[1])
    branch, feed_zero = feed_forward(normed, feed_weights[0])
    memory = middle + branch + ffn_out_bias[0].astype(jnp.float32)
    memory_low = memory.astype(jnp.bfloat16)
    target_f = target.astype(jnp.float32)
    normed, norm_two = norm_forward(target_f, norm_gain[2], norm_shift[2])
    branch, attend_one = attend_forward(normed, normed, routes[1], target_keys, moa_weights[1])
    first_state = target_f + branch
    normed, norm_three = norm_forward(first_state, norm_gain[3], norm_shift[3])
    branch, attend_two = attend_forward(normed, memory_low, routes[2], source_keys, moa_weights[2])
    second = first_state + branch
    normed, norm_four = norm_forward(second, norm_gain[4], norm_shift[4])
    branch, feed_one = feed_forward(normed, feed_weights[1])
    decoded = second + branch + ffn_out_bias[1].astype(jnp.float32)
    upstream = cotangent.astype(jnp.float32) * target_rows[:, :, None].astype(jnp.float32)
    out_bias_one = jnp.sum(upstream, (0, 1))
    hidden_grad, feed_grads_one = feed_backward(upstream, feed_one)
    carried, gain_four, shift_four = norm_backward(hidden_grad, norm_four, norm_gain[4])
    second_grad = upstream + carried
    hidden_grad, memory_grad, cross_grads = attend_backward(
        second_grad, attend_two, source_keys, moa_weights[2]
    )
    carried, gain_three, shift_three = norm_backward(hidden_grad, norm_three, norm_gain[3])
    first_grad = second_grad + carried
    hidden_grad, self_part, self_grads = attend_backward(
        first_grad, attend_one, target_keys, moa_weights[1]
    )
    carried, gain_two, shift_two = norm_backward(hidden_grad + self_part, norm_two, norm_gain[2])
    target_grad = first_grad + carried
    out_bias_zero = jnp.sum(memory_grad, (0, 1))
    hidden_grad, feed_grads_zero = feed_backward(memory_grad, feed_zero)
    carried, gain_one, shift_one = norm_backward(hidden_grad, norm_one, norm_gain[1])
    middle_grad = memory_grad + carried
    hidden_grad, encoder_part, encoder_grads = attend_backward(
        middle_grad, attend_zero, source_keys, moa_weights[0]
    )
    carried, gain_zero, shift_zero = norm_backward(
        hidden_grad + encoder_part, norm_zero, norm_gain[0]
    )
    source_grad = middle_grad + carried
    experts = moa_router.shape[2]
    valid_rows = jnp.stack([source_rows, target_rows, target_rows])
    routed_hits = (routes[..., None] == jnp.arange(experts, dtype=jnp.int32)) & valid_rows[
        :, :, :, None, None
    ]
    counted = jnp.sum(jnp.where(routed_hits, 1.0, 0.0), (1, 2, 3))
    layer_grads = (encoder_grads, self_grads, cross_grads)
    small = jnp.concatenate(
        [
            jnp.stack([gain_zero, gain_one, gain_two, gain_three, gain_four]),
            jnp.stack([shift_zero, shift_one, shift_two, shift_three, shift_four]),
            jnp.stack([out_bias_zero, out_bias_one]),
            jnp.concatenate([grads_of[0].T for grads_of in layer_grads]),
            jnp.zeros((1, model_width)).at[0, : 3 * experts].set(counted.reshape(-1)),
        ]
    )
    small = add_everywhere(small)
    reduced = [reduce_attention(*grads_of[1:]) for grads_of in layer_grads]
    gains, shifts, out_biases = small[:5], small[5:10], small[10:12]
    routers = jnp.swapaxes(small[12 : 12 + 3 * experts].reshape(3, experts, model_width), 1, 2)
    counts = small[-1, : 3 * experts].reshape(3, experts)
    feeds = (feed_grads_zero, feed_grads_one)
    return (
        memory,
        decoded,
        source_grad,
        target_grad,
        memory_grad,
        gains[:4],
        shifts[:4],
        jnp.stack([gains[4], shifts[4]]),
        routers,
        jnp.stack([grads_of[0] for grads_of in reduced]),
        jnp.stack([grads_of[1] for grads_of in reduced]),
        jnp.stack([grads_of[2] for grads_of in reduced]),
        jnp.stack([grads_of[0] for grads_of in feeds]),
        jnp.stack([grads_of[1] for grads_of in feeds]),
        jnp.stack([grads_of[2] for grads_of in feeds]),
        out_biases,
        counts.astype(jnp.int32),
    )


def solution(mesh):
    in_specs = (
        P("rows", "ffn", None),
        P("rows", "ffn", None),
        P("rows", "ffn", None),
        P("rows"),
        P("rows"),
        P(None, "rows", "ffn", None),
        P(),
        P(),
        P(),
        P(),
        P(),
        P(),
        P(None, None, "ffn"),
        P(None, "ffn"),
        P(None, "ffn", None),
        P(),
    )
    out_specs = (
        P("rows", "ffn", None),
        P("rows", "ffn", None),
        P("rows", "ffn", None),
        P("rows", "ffn", None),
        P("rows", "ffn", None),
        P(),
        P(),
        P(),
        P(),
        P(),
        P(),
        P(),
        P(None, None, "ffn"),
        P(None, "ffn"),
        P(None, "ffn", None),
        P(),
        P(),
    )
    return jax.shard_map(body, mesh=mesh, in_specs=in_specs, out_specs=out_specs, check_vma=False)
```

```python
import functools
import jax
import jax.numpy as jnp
from jax import lax
from jax.experimental import pallas as pl
from jax.experimental.pallas import tpu as pltpu
from jax.sharding import PartitionSpec as P

EPS = 1e-05
LOW = jnp.bfloat16
FULL = jnp.float32
VMEM_BYTES = 56 * 1024 * 1024


def mm(left, right):
    return jnp.dot(left, right, preferred_element_type=FULL)


def mm_nt(left, right):
    return lax.dot_general(left, right, (((1,), (1,)), ((), ())), preferred_element_type=FULL)


def normalise(values):
    center = values - jnp.mean(values, -1, keepdims=True)
    inverse = lax.rsqrt(jnp.mean(center * center, -1, keepdims=True) + EPS)
    return center * inverse, inverse


def norm_back(upstream, normal, inverse, gain_row):
    scaled = upstream * gain_row
    return inverse * (
        scaled
        - jnp.mean(scaled, -1, keepdims=True)
        - normal * jnp.mean(scaled * normal, -1, keepdims=True)
    )


def split_low(values):
    high = values.astype(LOW)
    return high, (values - high.astype(FULL)).astype(LOW)


def gelu_parts(pre):
    c = 0.7978845608028654
    square = pre * pre
    t = jnp.tanh(c * pre * (1.0 + 0.044715 * square))
    half = 0.5 * (1.0 + t)
    act = pre * half
    slope = half + (0.5 * c) * pre * (1.0 - t * t) * (1.0 + 0.134145 * square)
    return act, slope


def call(body, out_shape, args, scratch=(), smem=1, flops=0, name=None):
    specs = [pl.BlockSpec(memory_space=pltpu.SMEM)] * smem + [
        pl.BlockSpec(memory_space=pltpu.VMEM)
    ] * (len(args) - smem)
    return pl.pallas_call(
        body,
        out_shape=out_shape,
        in_specs=specs,
        out_specs=jax.tree.map(lambda _: pl.BlockSpec(memory_space=pltpu.VMEM), out_shape),
        scratch_shapes=list(scratch),
        compiler_params=pltpu.CompilerParams(vmem_limit_bytes=VMEM_BYTES),
        cost_estimate=pl.CostEstimate(flops=flops, bytes_accessed=4 << 20, transcendentals=0),
        name=name,
    )(*args)


def like(shape, dtype):
    return jax.ShapeDtypeStruct(shape, dtype)


def prepare_kernel(meta, source, target, gain, shift, keyval, h_source, h_target, kv_source, kv_target):
    for value, row, h_out, kv_out in ((source, 0, h_source, kv_source), (target, 2, h_target, kv_target)):
        normal, _ = normalise(value[...].astype(FULL))
        h = (normal * gain[row : row + 1] + shift[row : row + 1]).astype(LOW)
        h_out[...] = h
        kv_out[...] = mm(h, keyval[row // 2]).astype(LOW)


def to_slots(values, groups):
    part = values.shape[1] // groups
    blocks = []
    for g in range(groups):
        block = values[:, g * part : (g + 1) * part]
        blocks += [block, block]
    return jnp.concatenate(blocks, 1)


def slot_queries(h, route, query_proj, router_t, groups, slot_out, gate_out):
    experts = router_t.shape[0]
    queries = mm(h, query_proj).astype(LOW)
    spread = to_slots(queries.T, groups)
    head = spread.shape[0] // experts
    chosen = jnp.zeros((head, spread.shape[1]), LOW)
    for e in range(experts):
        chosen = jnp.where(route == e, spread[e * head : (e + 1) * head], chosen)
    slot_out[...] = chosen * jnp.asarray(float(head) ** -0.5, LOW)
    logits = to_slots(mm_nt(router_t, h), groups)
    ids = lax.broadcasted_iota(jnp.int32, logits.shape, 0)
    picked = jnp.sum(jnp.where(ids == route, logits, 0.0), 0, keepdims=True)
    part = picked.shape[1] // (2 * groups)
    gates = []
    for g in range(groups):
        a = picked[:, 2 * g * part : (2 * g + 1) * part]
        b = picked[:, (2 * g + 1) * part : (2 * g + 2) * part]
        top = jnp.maximum(a, b)
        ea, eb = jnp.exp(a - top), jnp.exp(b - top)
        total = ea + eb
        gates += [ea / total, eb / total]
    gate_out[...] = jnp.concatenate(gates, 1)


def allowed_keys(shape, z, part, planes, length, causal):
    blocks = []
    for k in range(planes):
        position = (z ^ k) * part + lax.broadcasted_iota(jnp.int32, (part, shape[1]), 0)
        ok = position < length
        if causal:
            lane = lax.broadcasted_iota(jnp.int32, (part, shape[1]), 1)
            query = z * part + jnp.where(lane >= part, lane - part, lane)
            ok = ok & (position <= query)
        blocks.append(ok)
    return jnp.concatenate(blocks, 0)


def attend(meta, side, causal, slots, gates, route, kv_refs, out_proj, groups, experts, lse_out, att_out):
    z = meta[1]
    part = kv_refs[0].shape[0] // groups
    planes = len(kv_refs)
    head = slots.shape[0]
    lanes = 2 * part
    columns = []
    for g in range(groups):
        kv = jnp.concatenate([ref[g * part : (g + 1) * part, :] for ref in kv_refs], 0)
        q = slots[:, g * lanes : (g + 1) * lanes]
        padded = jnp.concatenate([q, jnp.zeros_like(q)], 0)
        scores = mm(kv, padded)
        ok = allowed_keys(scores.shape, z, part, planes, meta[2 + 2 * side + g], causal)
        scores = jnp.where(ok, scores, -1e30)
        top = jnp.max(scores, 0, keepdims=True)
        raised = jnp.exp(scores - top)
        total = jnp.sum(raised, 0, keepdims=True)
        lse_out[:, g * lanes : (g + 1) * lanes] = top + jnp.log(total)
        low = (raised * (1.0 / total)).astype(LOW)
        attended = mm(kv.T, low)[head:]
        att_out[:, g * lanes : (g + 1) * lanes] = attended
        gated = attended * gates[:, g * lanes : (g + 1) * lanes]
        ids = route[:, g * lanes : (g + 1) * lanes]
        rows = []
        for e in range(experts):
            first = jnp.where(ids[:, :part] == e, gated[:, :part], 0.0)
            rows.append(jnp.where(ids[:, part:] == e, gated[:, part:], first).astype(LOW))
        columns.append(jnp.concatenate(rows, 0))
    mixed = jnp.concatenate(columns, 1)
    return mixed, mm(mixed.T, out_proj)


def queries_kernel(groups, meta, h, route, query_proj, router_t, slot_out, gate_out):
    slot_queries(h[...], route[...], query_proj[...], router_t[...], groups, slot_out, gate_out)


def attend_kernel(groups, side, causal, planes, next_queries, meta, resid, slots, gates, route, *rest):
    kv_refs, rest = rest[:planes], rest[planes:]
    out_proj, rest = rest[0], rest[1:]
    if next_queries:
        (gain, shift, next_route, next_proj, next_router, new_resid, lse_out, att_out, mixed_out, next_slots, next_gates) = rest
    else:
        (new_resid, lse_out, att_out, mixed_out) = rest
    experts = out_proj.shape[0] // slots.shape[0]
    mixed, branch = attend(meta, side, causal, slots, gates, route, kv_refs, out_proj[...], groups, experts, lse_out, att_out)
    mixed_out[...] = mixed
    total = resid[...].astype(FULL) + branch
    new_resid[...] = total
    if next_queries:
        normal, _ = normalise(total)
        h = (normal * gain[3:4] + shift[3:4]).astype(LOW)
        slot_queries(h, next_route[...], next_proj[...], next_router[...], groups, next_slots, next_gates)


def place_weights(meta, own_first, own_second, pieces, first, second):
    r = meta[0]
    first[0] = own_first[...]
    second[0] = own_second[...]
    ways = len(pieces)
    rows = own_first.shape[0] // ways
    for j, piece in enumerate(pieces):
        at = pl.ds(pl.multiple_of((r ^ j) * rows, rows), rows)
        for k in range(1, first.shape[0]):
            first[k, at, :] = piece[k - 1, :rows]
            second[k, at, :] = piece[k - 1, rows : 2 * rows]


def feed_forward_kernel(ways, meta, state, gain, shift, out_bias, bias, keyval, own_first, own_second, *rest):
    pieces, (memory, low_out, kv_out, first, second) = rest[:ways], rest[ways:]
    place_weights(meta, own_first, own_second, pieces, first, second)
    value = state[...]
    normal, _ = normalise(value)
    h = (normal * gain[1:2] + shift[1:2]).astype(LOW)
    memory[...] = value + out_bias[0:1].astype(FULL)

    def step(k, carry):
        pre = mm(h, first[k]) + bias[k]
        act = jax.nn.gelu(pre).astype(LOW)
        memory[...] += mm_nt(act, second[k])
        return carry

    lax.fori_loop(0, first.shape[0], step, 0)
    low = memory[...].astype(LOW)
    low_out[...] = low
    kv_out[...] = mm(low, keyval[...]).astype(LOW)


def feed_backward_core(meta, h, upstream_low, ways, bias, first, second, grad, d_h, kept, sent, bias_grad, state):
    r, z = meta[0], meta[1]
    h_t = h.T
    up_t = upstream_low.T
    d_h[...] = jnp.zeros_like(d_h)
    rows = h.shape[1] // ways

    def step(k, carry):
        w_first, w_second = first[k], second[k]
        pre = mm(h, w_first) + bias[k]
        act, slope = gelu_parts(pre)
        act = act.astype(LOW)
        if state is not None:
            state[...] += mm_nt(act, w_second)
        d_pre_full = (mm(upstream_low, w_second) * slope).astype(LOW)
        d_h[...] += mm_nt(d_pre_full, w_first)
        bias_grad[z ^ k] = jnp.sum(d_pre_full.astype(FULL), 0, keepdims=True)
        for half, product in enumerate((mm(h_t, d_pre_full), mm(up_t, act))):
            grad[...] = product
            for j in range(ways):
                block = grad[pl.ds(pl.multiple_of((r ^ j) * rows, rows), rows), :].astype(LOW)
                target = sent if j & 1 else kept
                target[j // 2, k, half * rows : (half + 1) * rows, :] = block
        return carry

    lax.fori_loop(0, first.shape[0], step, 0)


def decoder_feed_kernel(ways, groups, meta, state_in, cotangent, gain, shift, out_bias, bias, own_first, own_second, *rest):
    pieces, (decoded, state_grad, kept, sent, bias_grad, sums, first, second, grad, d_h) = rest[:ways], rest[ways:]
    place_weights(meta, own_first, own_second, pieces, first, second)
    value = state_in[...]
    normal, inverse = normalise(value)
    h = (normal * gain[4:5] + shift[4:5]).astype(LOW)
    decoded[...] = value + out_bias[1:2].astype(FULL)
    part = value.shape[0] // groups
    seeds = []
    for g in range(groups):
        row = meta[1] * part + lax.broadcasted_iota(jnp.int32, (part, value.shape[1]), 0)
        seeds.append(jnp.where(row < meta[4 + g], cotangent[g * part : (g + 1) * part, :].astype(FULL), 0.0))
    seed = jnp.concatenate(seeds, 0)
    feed_backward_core(meta, h, seed.astype(LOW), ways, bias, first, second, grad, d_h, kept, sent, bias_grad, decoded)
    normal, inverse = normalise(state_in[...])
    upstream = d_h[...]
    state_grad[...] = seed + norm_back(upstream, normal, inverse, gain[4:5])
    sums[0:1] = jnp.sum(upstream * normal, 0, keepdims=True)
    sums[1:2] = jnp.sum(upstream, 0, keepdims=True)
    sums[2:3] = jnp.sum(seed, 0, keepdims=True)
    sums[3:8] = jnp.zeros((5, sums.shape[1]), FULL)


def total_of(blocks):
    total = blocks[0][...].astype(FULL)
    for block in blocks[1:]:
        total = total + block[...].astype(FULL)
    return total.astype(LOW)


def encoder_feed_kernel(ways, planes, meta, state_in, memory_low, gain, shift, bias, keyval, *rest):
    blocks, rest = rest[:planes], rest[planes:]
    own_first, own_second = rest[:2]
    pieces, rest = rest[2 : 2 + ways], rest[2 + ways :]
    (memory_grad, state_grad, keyval_grad, kept, sent, bias_grad, sums, first, second, grad, d_h) = rest
    place_weights(meta, own_first, own_second, pieces, first, second)
    d_kv = total_of(blocks)
    upstream_in = mm_nt(d_kv, keyval[...])
    memory_grad[...] = upstream_in
    keyval_grad[...] = mm(d_kv.T, memory_low[...])
    normal, inverse = normalise(state_in[...])
    h = (normal * gain[1:2] + shift[1:2]).astype(LOW)
    feed_backward_core(meta, h, upstream_in.astype(LOW), ways, bias, first, second, grad, d_h, kept, sent, bias_grad, None)
    normal, inverse = normalise(state_in[...])
    upstream = d_h[...]
    state_grad[...] = memory_grad[...] + norm_back(upstream, normal, inverse, gain[1:2])
    sums[0:1] = jnp.sum(upstream * normal, 0, keepdims=True)
    sums[1:2] = jnp.sum(upstream, 0, keepdims=True)
    sums[2:3] = jnp.sum(memory_grad[...], 0, keepdims=True)
    sums[3:8] = jnp.zeros((5, sums.shape[1]), FULL)


def attend_back_kernel(groups, side, causal, planes, ways, norm_row, finish, meta, upstream_ref, state, gain, shift, slots, gates, route, lse, att, mixed, *rest):
    kv_refs, rest = rest[:planes], rest[planes:]
    (query_proj, out_proj, router, result, kept, sent, router_grad, sums), rest = rest[:8], rest[8:]
    d_kv_out, scratch = rest[:planes], rest[planes:]
    (grad,) = scratch
    r, z = meta[0], meta[1]
    experts = router.shape[1]
    head = slots.shape[0]
    upstream = upstream_ref[...]
    branch_grad = upstream.astype(LOW)
    normal, inverse = normalise(state[...].astype(FULL))
    h = (normal * gain[norm_row : norm_row + 1] + shift[norm_row : norm_row + 1]).astype(LOW)
    part = h.shape[0] // groups
    lanes = 2 * part
    d_mixed = mm_nt(out_proj[...], branch_grad)
    out_grad = mm(mixed[...], branch_grad)
    query_columns, logit_columns = [], []
    for g in range(groups):
        here = slice(g * lanes, (g + 1) * lanes)
        ids = route[:, here]
        gate = gates[:, here]
        attended = att[:, here]
        mine = d_mixed[:, g * part : (g + 1) * part]
        spread = jnp.concatenate([mine, mine], 1)
        slot_grad = jnp.zeros((head, lanes), FULL)
        for e in range(experts):
            slot_grad = jnp.where(ids == e, spread[e * head : (e + 1) * head], slot_grad)
        gate_grad = jnp.sum(attended * slot_grad, 0, keepdims=True)
        weighted = gate * gate_grad
        both = weighted[:, :part] + weighted[:, part:]
        chosen_grad = gate * (gate_grad - jnp.concatenate([both, both], 1))
        att_grad = (gate * slot_grad).astype(LOW)
        inner = jnp.sum(att_grad.astype(FULL) * attended, 0, keepdims=True)
        q = slots[:, here]
        zeros = jnp.zeros_like(q)
        kv = jnp.concatenate([ref[g * part : (g + 1) * part, :] for ref in kv_refs], 0)
        scores = mm(kv, jnp.concatenate([q, zeros], 0))
        ok = allowed_keys(scores.shape, z, part, planes, meta[2 + 2 * side + g], causal)
        probs = jnp.exp(jnp.where(ok, scores, -1e30) - lse[:, here])
        probs_grad = mm(kv, jnp.concatenate([zeros, att_grad], 0))
        score_grad = (probs * (probs_grad - inner)).astype(LOW)
        d_kv = mm(score_grad, jnp.concatenate([q, zeros], 0).T) + mm(
            probs.astype(LOW), jnp.concatenate([zeros, att_grad], 0).T
        )
        for k in range(planes):
            d_kv_out[k][g * part : (g + 1) * part, :] = d_kv[k * part : (k + 1) * part].astype(LOW)
        slot_query_grad = mm(kv.T, score_grad)[:head] * (float(head) ** -0.5)
        rows = []
        for e in range(experts):
            first = jnp.where(ids[:, :part] == e, slot_query_grad[:, :part], 0.0)
            rows.append(jnp.where(ids[:, part:] == e, slot_query_grad[:, part:], first).astype(LOW))
        query_columns.append(jnp.concatenate(rows, 0))
        expert = lax.broadcasted_iota(jnp.int32, (experts, part), 0)
        first = jnp.where(ids[:, :part] == expert, chosen_grad[:, :part], 0.0)
        logit_columns.append(jnp.where(ids[:, part:] == expert, chosen_grad[:, part:], first))
    query_grad_rows = jnp.concatenate(query_columns, 1)
    logit_grad = jnp.concatenate(logit_columns, 1)
    high, low = split_low(logit_grad)
    router_grad[...] = mm(high, h) + mm(low, h)
    d_h = mm_nt(query_grad_rows.T, query_proj[...])
    d_h = d_h + mm_nt(high.T, router[...]) + mm_nt(low.T, router[...])
    rows_each = out_grad.shape[0] // ways
    for half in range(2):
        grad[...] = mm(query_grad_rows, h) if half == 0 else out_grad
        for j in range(ways):
            block = grad[pl.ds(pl.multiple_of((r ^ j) * rows_each, rows_each), rows_each), :].astype(LOW)
            place = sent if j & 1 else kept
            place[j // 2, half * rows_each : (half + 1) * rows_each, :] = block
    if finish:
        result[...] = upstream_ref[...] + norm_back(d_h, normal, inverse, gain[norm_row : norm_row + 1])
        sums[0:1] = jnp.sum(d_h * normal, 0, keepdims=True)
        sums[1:2] = jnp.sum(d_h, 0, keepdims=True)
        sums[2:8] = jnp.zeros((6, sums.shape[1]), FULL)
    else:
        result[...] = d_h
        sums[...] = jnp.zeros_like(sums)


def finish_kernel(planes, norm_row, meta, partial, upstream, state, gain, shift, keyval, *rest):
    blocks, (result, keyval_grad, sums) = rest[:planes], rest[planes:]
    d_kv = total_of(blocks)
    normal, inverse = normalise(state[...].astype(FULL))
    h = (normal * gain[norm_row : norm_row + 1] + shift[norm_row : norm_row + 1]).astype(LOW)
    keyval_grad[...] = mm(d_kv.T, h)
    d_h = partial[...] + mm_nt(d_kv, keyval[...])
    result[...] = upstream[...] + norm_back(d_h, normal, inverse, gain[norm_row : norm_row + 1])
    sums[0:1] = jnp.sum(d_h * normal, 0, keepdims=True)
    sums[1:2] = jnp.sum(d_h, 0, keepdims=True)
    sums[2:8] = jnp.zeros((6, sums.shape[1]), FULL)


def swap(values, axis_name, bits):
    size = lax.axis_size(axis_name)
    return lax.ppermute(values, axis_name, [(i, i ^ bits) for i in range(size)])


def ways_of():
    return min(lax.axis_size("rows"), 8)


def other_bits():
    size, ways = lax.axis_size("rows"), ways_of()
    bits = []
    while ways < size:
        bits.append(ways)
        ways *= 2
    return bits


def add_over(values, axis_name, bits):
    for bit in bits:
        values = values.astype(FULL) + swap(values, axis_name, bit).astype(FULL)
        values = values.astype(LOW)
    return values


def plane_bits():
    size, bits = lax.axis_size("ffn"), []
    while (1 << len(bits)) < size:
        bits.append(1 << len(bits))
    return bits


def gather_planes(values):
    return [values] + [swap(values, "ffn", k) for k in range(1, lax.axis_size("ffn"))]


def gather_weights(first, second, bias, device):
    ways = ways_of()
    rows = first.shape[0] // ways
    start = (device[0] % ways) * rows
    mine = jnp.concatenate(
        [
            lax.dynamic_slice_in_dim(first, start, rows, 0),
            lax.dynamic_slice_in_dim(second, start, rows, 0),
            jnp.broadcast_to(bias[None], (16,) + bias.shape),
        ]
    )
    crossed = [swap(mine, "ffn", k) for k in range(1, lax.axis_size("ffn"))]
    all_bias = jnp.stack([bias] + [part[2 * rows] for part in crossed])[:, None].astype(FULL)
    own = jnp.stack([part[: 2 * rows] for part in crossed])
    pieces = []
    for even in range(0, ways, 2):
        piece = own if even == 0 else swap(own, "rows", even)
        pieces += [piece, swap(piece, "rows", 1)]
    return all_bias, pieces


def scatter_rows(kept, sent):
    pairs = (kept.astype(FULL) + swap(sent, "rows", 1).astype(FULL)).astype(LOW)
    total = pairs[0].astype(FULL)
    for half in range(1, pairs.shape[0]):
        total = total + swap(pairs[half], "rows", 2 * half).astype(FULL)
    return total


def gather_rows(own):
    ways = ways_of()
    even = jnp.stack([own] + [swap(own, "rows", k) for k in range(2, ways, 2)])
    return even, swap(even, "rows", 1)


def reduce_feed(kept, sent):
    own = scatter_rows(kept, sent)
    total = own[0]
    low = own.astype(LOW)
    for k in range(1, own.shape[0]):
        total = total + swap(low[k], "ffn", k).astype(FULL)
    total = add_over(total.astype(LOW), "rows", other_bits())
    return gather_rows(total)


def reduce_attention(kept, sent):
    own = scatter_rows(kept, sent).astype(LOW)
    own = add_over(own, "ffn", plane_bits())
    own = add_over(own, "rows", other_bits())
    return gather_rows(own)


def add_small(values):
    for axis_name in ("rows", "ffn"):
        bit = 1
        while bit < lax.axis_size(axis_name):
            values = values + swap(values, axis_name, bit)
            bit *= 2
    return values


def add_tail(values):
    bits, bit = [], 1
    while bit < lax.axis_size("rows"):
        bits.append(bit)
        bit *= 2
    return add_over(add_over(values, "rows", bits), "ffn", plane_bits())


def place_kernel(layers, attentions, meta, *refs):
    feeds, refs = refs[: 2 * layers], refs[2 * layers :]
    moas, refs = refs[: 2 * attentions], refs[2 * attentions :]
    first_out, second_out, query_out, out_out, scratch = refs
    r = meta[0]
    for layer in range(layers):
        ways = 2 * feeds[2 * layer].shape[0]
        rows = feeds[2 * layer].shape[1] // 2
        for j in range(ways):
            piece = feeds[2 * layer + (j & 1)]
            at = pl.ds(pl.multiple_of(((r ^ j) & (ways - 1)) * rows, rows), rows)
            first_out[layer, at, :] = piece[j // 2, :rows].astype(FULL)
            scratch[at, :] = piece[j // 2, rows:].astype(FULL)
        second_out[layer] = scratch[...].T
    for item in range(attentions):
        ways = 2 * moas[2 * item].shape[0]
        rows = moas[2 * item].shape[1] // 2
        for j in range(ways):
            piece = moas[2 * item + (j & 1)]
            at = pl.ds(pl.multiple_of(((r ^ j) & (ways - 1)) * rows, rows), rows)
            scratch[at, :] = piece[j // 2, :rows].astype(FULL)
            out_out[item, at, :] = piece[j // 2, rows:].astype(FULL)
        query_out[item] = scratch[...].T


MICRO = 1 << 30


def body(
    source,
    target,
    cotangent,
    source_lengths,
    target_lengths,
    routes,
    norm_gain,
    norm_shift,
    moa_router,
    moa_query,
    moa_keyval,
    moa_out,
    ffn_in,
    ffn_in_bias,
    ffn_out,
    ffn_out_bias,
):
    groups, row_count, width = source.shape
    tokens = groups * row_count
    planes = lax.axis_size("ffn")
    ways = ways_of()
    experts = moa_router.shape[2]
    both = moa_keyval.shape[2]
    head = both // 2
    hidden = ffn_in.shape[2]
    slots_all = 2 * tokens
    row_index, plane_index = lax.axis_index("rows"), lax.axis_index("ffn")
    device = (row_index, plane_index)
    meta = jnp.concatenate(
        [
            jnp.stack([row_index % ways, plane_index]).astype(jnp.int32),
            source_lengths,
            target_lengths,
        ]
    )
    flat = lambda values: values.reshape(tokens, width)
    source, target, cotangent = flat(source), flat(target), flat(cotangent)
    route_rows = jnp.swapaxes(routes, 2, 3).reshape(3, 1, slots_all)
    router_t = jnp.swapaxes(moa_router, 1, 2)
    second_weights = [ffn_out[layer].T for layer in range(2)]

    bias_zero, pieces_zero = gather_weights(ffn_in[0], second_weights[0], ffn_in_bias[0], device)
    rows_like = like((tokens, width), FULL)
    low_like = like((tokens, width), LOW)
    kv_like = like((tokens, both), LOW)
    h_source, h_target, kv_source, kv_target = call(
        prepare_kernel,
        [low_like, low_like, kv_like, kv_like],
        (meta, source, target, norm_gain, norm_shift, moa_keyval),
        flops=3 * MICRO,
        name="prepare",
    )
    kv_zero = gather_planes(kv_source)
    kv_one = gather_planes(kv_target)
    bias_one, pieces_one = gather_weights(ffn_in[1], second_weights[1], ffn_in_bias[1], device)
    slot_like = [like((head, slots_all), LOW), like((1, slots_all), FULL)]
    slots_zero, slots_one = (
        call(
            functools.partial(queries_kernel, groups),
            slot_like,
            (meta, h, route_rows[j], moa_query[j], router_t[j]),
            flops=2 * MICRO,
            name="queries",
        )
        for j, h in ((0, h_source), (1, h_target))
    )
    kept_like = [
        rows_like,
        like((1, slots_all), FULL),
        like((head, slots_all), FULL),
        like((experts * head, tokens), LOW),
    ]

    def attention(j, side, causal, resid, slots, kv_blocks, following):
        extra, more = (), []
        if following:
            extra = (norm_gain, norm_shift, route_rows[2], moa_query[2], router_t[2])
            more = slot_like
        return call(
            functools.partial(attend_kernel, groups, side, causal, planes, following),
            kept_like + more,
            (meta, resid, *slots, route_rows[j], *kv_blocks, moa_out[j], *extra),
            flops=5 * MICRO,
            name="attend",
        )

    middle, *saved_zero = attention(0, 0, False, source, slots_zero, kv_zero, False)
    weight_scratch = [pltpu.VMEM((planes, width, hidden), LOW)] * 2
    memory, memory_low, kv_memory = call(
        functools.partial(feed_forward_kernel, ways),
        [rows_like, low_like, kv_like],
        (meta, middle, norm_gain, norm_shift, ffn_out_bias, bias_zero, moa_keyval[2])
        + (ffn_in[0], second_weights[0], *pieces_zero),
        weight_scratch,
        flops=8 * MICRO,
        name="encoder_feed",
    )
    kv_two = gather_planes(kv_memory)
    first_state, *saved_one, next_slots, next_gates = attention(
        1, 1, True, target, slots_one, kv_one, True
    )
    slots_two = (next_slots, next_gates)
    second_state, *saved_two = attention(2, 0, False, first_state, slots_two, kv_two, False)

    back_scratch = weight_scratch + [pltpu.VMEM((width, hidden), FULL), pltpu.VMEM((tokens, width), FULL)]
    feed_like = [like((ways // 2, planes, 2 * width // ways, hidden), LOW)] * 2
    feed_like += [like((planes, 1, hidden), FULL), like((8, width), FULL)]
    decoded, second_grad, kept, sent, bias_grad_one, sums_four = call(
        functools.partial(decoder_feed_kernel, ways, groups),
        [rows_like, rows_like] + feed_like,
        (meta, second_state, cotangent, norm_gain, norm_shift, ffn_out_bias, bias_one)
        + (ffn_in[1], second_weights[1], *pieces_one),
        back_scratch,
        flops=15 * MICRO,
        name="decoder_feed",
    )
    feed_one = reduce_feed(kept, sent)

    moa_like = [like((ways // 2, 2 * width // ways, width), LOW)] * 2
    moa_like += [like((experts, width), FULL), like((8, width), FULL)] + [kv_like] * planes

    def attention_back(j, side, causal, norm_row, finish, upstream, state, slots, saved, kv_blocks):
        return call(
            functools.partial(
                attend_back_kernel, groups, side, causal, planes, ways, norm_row, finish
            ),
            [rows_like] + moa_like,
            (meta, upstream, state, norm_gain, norm_shift, *slots, route_rows[j], *saved)
            + (*kv_blocks, moa_query[j], moa_out[j], moa_router[j]),
            [pltpu.VMEM((width, width), FULL)],
            flops=8 * MICRO,
            name="attend_back",
        )

    def home(blocks):
        return [blocks[0]] + [swap(blocks[k], "ffn", k) for k in range(1, planes)]

    first_grad, kept_two, sent_two, router_two, sums_three, *d_kv_two = attention_back(
        2, 0, False, 3, True, second_grad, first_state, slots_two, saved_two, kv_two
    )
    d_kv_two = home(d_kv_two)
    self_grad, kept_one, sent_one, router_one, unused, *d_kv_one = attention_back(
        1, 1, True, 2, False, first_grad, target, slots_one, saved_one, kv_one
    )
    d_kv_one = home(d_kv_one)
    memory_grad, middle_grad, keyval_two, kept, sent, bias_grad_zero, sums_one = call(
        functools.partial(encoder_feed_kernel, ways, planes),
        [rows_like, rows_like, like((both, width), FULL)] + feed_like,
        (meta, middle, memory_low, norm_gain, norm_shift, bias_zero, moa_keyval[2], *d_kv_two)
        + (ffn_in[0], second_weights[0], *pieces_zero),
        back_scratch,
        flops=15 * MICRO,
        name="encoder_feed_back",
    )
    feed_zero = reduce_feed(kept, sent)
    moa_later = reduce_attention(
        jnp.concatenate([kept_two, kept_one], 1), jnp.concatenate([sent_two, sent_one], 1)
    )
    encoder_grad, kept_zero, sent_zero, router_zero, unused, *d_kv_zero = attention_back(
        0, 0, False, 0, False, middle_grad, source, slots_zero, saved_zero, kv_zero
    )
    d_kv_zero = home(d_kv_zero)
    moa_first = reduce_attention(kept_zero, sent_zero)

    def finish(j, norm_row, partial, upstream, state, blocks):
        return call(
            functools.partial(finish_kernel, planes, norm_row),
            [rows_like, like((both, width), FULL), like((8, width), FULL)],
            (meta, partial, upstream, state, norm_gain, norm_shift, moa_keyval[j], *blocks),
            flops=4 * MICRO,
            name="finish",
        )

    target_grad, keyval_one, sums_two = finish(1, 2, self_grad, first_grad, target, d_kv_one)
    source_grad, keyval_zero, sums_zero = finish(
        0, 0, encoder_grad, middle_grad, source, d_kv_zero
    )

    position = plane_index * row_count + jnp.arange(row_count, dtype=jnp.int32)
    source_rows = position[None, :] < source_lengths[:, None]
    target_rows = position[None, :] < target_lengths[:, None]
    valid = jnp.stack([source_rows, target_rows, target_rows])
    hits = (routes[..., None] == jnp.arange(experts, dtype=jnp.int32)) & valid[..., None, None]
    counted = jnp.sum(jnp.where(hits, 1.0, 0.0), (1, 2, 3)).reshape(-1)
    small = jnp.concatenate(
        [
            sums_one[:3],
            sums_two[:2],
            sums_three[:2],
            sums_four[:3],
            router_zero,
            router_one,
            router_two,
            bias_grad_zero[:, 0],
            bias_grad_one[:, 0],
            jnp.zeros((1, width), FULL).at[0, : counted.shape[0]].set(counted),
        ]
    )
    small = add_small(small)
    tail = jnp.concatenate([keyval_zero, keyval_one, keyval_two, sums_zero, sums_zero])
    tail = add_tail(tail.astype(LOW)).astype(FULL)

    moa_parts = []
    for pair in (
        moa_first,
        [part[:, 2 * width // ways :] for part in moa_later],
        [part[:, : 2 * width // ways] for part in moa_later],
    ):
        moa_parts += list(pair)
    first_grads, second_grads, query_grads, out_grads = call(
        functools.partial(place_kernel, 2, 3),
        [like((2, width, hidden), FULL), like((2, hidden, width), FULL)]
        + [like((3, width, experts * head), FULL), like((3, experts * head, width), FULL)],
        (meta, *feed_zero, *feed_one, *moa_parts),
        [pltpu.VMEM((width, width), FULL)],
        flops=4 * MICRO,
        name="place",
    )
    keyval_grads = jnp.swapaxes(tail[: 3 * both].reshape(3, both, width), 1, 2)
    gain_zero, shift_zero = tail[3 * both], tail[3 * both + 1]
    gain_one, shift_one, out_zero, gain_two, shift_two = (small[i] for i in range(5))
    gain_three, shift_three, gain_four, shift_four, out_one = (small[i] for i in range(5, 10))
    routers = jnp.swapaxes(small[10 : 10 + 3 * experts].reshape(3, experts, width), 1, 2)
    rest = small[10 + 3 * experts :]
    bias_grads = lax.dynamic_index_in_dim(
        rest[: 2 * planes].reshape(2, planes, hidden), plane_index, 1, keepdims=False
    )
    counts = rest[-1, : 3 * experts].reshape(3, experts).astype(jnp.int32)
    whole = lambda values: values.reshape(groups, row_count, width)
    return (
        whole(memory),
        whole(decoded),
        whole(source_grad),
        whole(target_grad),
        whole(memory_grad),
        jnp.stack([gain_zero, gain_one, gain_two, gain_three]),
        jnp.stack([shift_zero, shift_one, shift_two, shift_three]),
        jnp.stack([gain_four, shift_four]),
        routers,
        query_grads,
        keyval_grads,
        out_grads,
        first_grads,
        bias_grads,
        second_grads,
        jnp.stack([out_zero, out_one]),
        counts,
    )


def solution(mesh):
    in_specs = (
        P("rows", "ffn", None),
        P("rows", "ffn", None),
        P("rows", "ffn", None),
        P("rows"),
        P("rows"),
        P(None, "rows", "ffn", None),
        P(),
        P(),
        P(),
        P(),
        P(),
        P(),
        P(None, None, "ffn"),
        P(None, "ffn"),
        P(None, "ffn", None),
        P(),
    )
    out_specs = (
        P("rows", "ffn", None),
        P("rows", "ffn", None),
        P("rows", "ffn", None),
        P("rows", "ffn", None),
        P("rows", "ffn", None),
        P(),
        P(),
        P(),
        P(),
        P(),
        P(),
        P(),
        P(None, None, "ffn"),
        P(None, "ffn"),
        P(None, "ffn", None),
        P(),
        P(),
    )
    return jax.shard_map(body, mesh=mesh, in_specs=in_specs, out_specs=out_specs, check_vma=False)
```

```python
import functools
import jax
import jax.numpy as jnp
from jax import lax
from jax.experimental import pallas as pl
from jax.experimental.pallas import tpu as pltpu
from jax.sharding import PartitionSpec as P

EPS = 1e-05
LOW = jnp.bfloat16
FULL = jnp.float32
VMEM_BYTES = 56 * 1024 * 1024
MICRO = 1 << 20
COSTS = {"cut": 2, "prepare": 2.4, "queries": 2.4, "attend": 5, "encoder_feed": 8, "decoder_feed": 15}
COSTS.update({"attend_back": 6.3, "project_back": 4.8, "encoder_feed_back": 14, "finish": 4})
COSTS.update({"pack": 2, "unpack": 2.4, "place": 4.5})


class Meta:
    def __init__(self, source_lengths, target_lengths):
        self.lengths = (source_lengths, target_lengths)

    def __getitem__(self, n):
        if n == 0:
            return lax.rem(lax.axis_index("rows"), ways_of())
        if n == 1:
            return lax.axis_index("ffn")
        groups = self.lengths[0].shape[0]
        return self.lengths[(n - 2) // groups][(n - 2) % groups]


def mm(left, right):
    return jnp.dot(left, right, preferred_element_type=FULL)


def mm_nt(left, right):
    return lax.dot_general(left, right, (((1,), (1,)), ((), ())), preferred_element_type=FULL)


def normalise(values):
    center = values - jnp.mean(values, -1, keepdims=True)
    inverse = lax.rsqrt(jnp.mean(center * center, -1, keepdims=True) + EPS)
    return center * inverse, inverse


def norm_back(upstream, normal, inverse, gain_row):
    scaled = upstream * gain_row
    return inverse * (
        scaled
        - jnp.mean(scaled, -1, keepdims=True)
        - normal * jnp.mean(scaled * normal, -1, keepdims=True)
    )


def split_low(values):
    high = values.astype(LOW)
    return high, (values - high.astype(FULL)).astype(LOW)


def gelu_parts(pre):
    c = 0.7978845608028654
    square = pre * pre
    t = jnp.tanh(c * pre * (1.0 + 0.044715 * square))
    half = 0.5 * (1.0 + t)
    act = pre * half
    slope = half + (0.5 * c) * pre * (1.0 - t * t) * (1.0 + 0.134145 * square)
    return act, slope


def call(body, out_shape, args, scratch=(), after=(), name=None, whole=(), alias=None, out_specs=None):
    arrays, specs = [], []
    for n, arg in enumerate(args):
        if isinstance(arg, tuple):
            array, entry = arg
            rest = array.shape[1:]
            specs.append(
                pl.BlockSpec(
                    (None,) + rest,
                    lambda step, entry=entry, rest=rest: (entry,) + (0,) * len(rest),
                    pipeline_mode=pl.Buffered(1),
                )
            )
        else:
            array = arg
            space = pltpu.SMEM if n < 2 else pl.ANY if n in whole else pltpu.VMEM
            specs.append(pl.BlockSpec(memory_space=space))
        arrays.append(array)
    taken, skipped = len(arrays), len(after)

    def run(*refs):
        body(Meta(*refs[:2]), *refs[2:taken], *refs[taken + skipped :])

    return pl.pallas_call(
        run,
        grid=(1,),
        out_shape=out_shape,
        in_specs=specs + [pl.BlockSpec(memory_space=pl.ANY)] * skipped,
        out_specs=out_specs
        or jax.tree.map(lambda _: pl.BlockSpec(memory_space=pltpu.VMEM), out_shape),
        scratch_shapes=list(scratch),
        input_output_aliases=alias or {},
        compiler_params=pltpu.CompilerParams(vmem_limit_bytes=VMEM_BYTES),
        cost_estimate=pl.CostEstimate(
            flops=int(COSTS[name] * MICRO), bytes_accessed=1 << 16, transcendentals=0
        ),
        name=name,
    )(*arrays, *after)


def like(shape, dtype):
    return jax.ShapeDtypeStruct(shape, dtype)


def prepare_kernel(row, meta, value, gain, shift, keyval, h_out, kv_out):
    normal, _ = normalise(value[...].astype(FULL))
    h = (normal * gain[row : row + 1] + shift[row : row + 1]).astype(LOW)
    h_out[...] = h
    kv_out[...] = mm(h, keyval[...]).astype(LOW)


def cut_kernel(ways, layer, meta, first, second, bias, mine, semaphores):
    rows = first.shape[1] // ways
    at = pl.ds(pl.multiple_of(meta[0] * rows, rows), rows)
    copies = [
        pltpu.make_async_copy(weight.at[layer, at, :], mine.at[pl.ds(n * rows, rows), :], semaphores.at[n])
        for n, weight in enumerate((first, second))
    ]
    for copy in copies:
        copy.start()
    mine[2 * rows :] = jnp.broadcast_to(bias[layer : layer + 1, :], (16, bias.shape[1]))
    for copy in copies:
        copy.wait()


def to_slots(values, groups):
    part = values.shape[1] // groups
    blocks = []
    for g in range(groups):
        block = values[:, g * part : (g + 1) * part]
        blocks += [block, block]
    return jnp.concatenate(blocks, 1)


def slot_queries(h, route, query_proj, router_t, groups, slot_out, gate_out):
    experts = router_t.shape[0]
    queries = mm(h, query_proj).astype(LOW)
    spread = to_slots(queries.T, groups)
    head = spread.shape[0] // experts
    chosen = jnp.zeros((head, spread.shape[1]), LOW)
    for e in range(experts):
        chosen = jnp.where(route == e, spread[e * head : (e + 1) * head], chosen)
    slot_out[...] = chosen * jnp.asarray(float(head) ** -0.5, LOW)
    logits = to_slots(mm_nt(router_t, h), groups)
    ids = lax.broadcasted_iota(jnp.int32, logits.shape, 0)
    picked = jnp.sum(jnp.where(ids == route, logits, 0.0), 0, keepdims=True)
    part = picked.shape[1] // (2 * groups)
    gates = []
    for g in range(groups):
        a = picked[:, 2 * g * part : (2 * g + 1) * part]
        b = picked[:, (2 * g + 1) * part : (2 * g + 2) * part]
        top = jnp.maximum(a, b)
        ea, eb = jnp.exp(a - top), jnp.exp(b - top)
        total = ea + eb
        gates += [ea / total, eb / total]
    gate_out[...] = jnp.concatenate(gates, 1)


def allowed_keys(shape, z, part, planes, length, causal):
    blocks = []
    for k in range(planes):
        position = (z ^ k) * part + lax.broadcasted_iota(jnp.int32, (part, shape[1]), 0)
        ok = position < length
        if causal:
            lane = lax.broadcasted_iota(jnp.int32, (part, shape[1]), 1)
            query = z * part + jnp.where(lane >= part, lane - part, lane)
            ok = ok & (position <= query)
        blocks.append(ok)
    return jnp.concatenate(blocks, 0)


def attend(meta, side, causal, slots, gates, route, kv_refs, out_proj, groups, experts, lse_out, att_out):
    z = meta[1]
    part = kv_refs[0].shape[0] // groups
    planes = len(kv_refs)
    head = slots.shape[0]
    lanes = 2 * part
    columns = []
    for g in range(groups):
        kv = jnp.concatenate([ref[g * part : (g + 1) * part, :] for ref in kv_refs], 0)
        q = slots[:, g * lanes : (g + 1) * lanes]
        padded = jnp.concatenate([q, jnp.zeros_like(q)], 0)
        scores = mm(kv, padded)
        ok = allowed_keys(scores.shape, z, part, planes, meta[2 + 2 * side + g], causal)
        scores = jnp.where(ok, scores, -1e30)
        top = jnp.max(scores, 0, keepdims=True)
        raised = jnp.exp(scores - top)
        total = jnp.sum(raised, 0, keepdims=True)
        lse_out[:, g * lanes : (g + 1) * lanes] = top + jnp.log(total)
        low = (raised * (1.0 / total)).astype(LOW)
        attended = mm(kv.T, low)[head:]
        att_out[:, g * lanes : (g + 1) * lanes] = attended
        gated = attended * gates[:, g * lanes : (g + 1) * lanes]
        ids = route[:, g * lanes : (g + 1) * lanes]
        rows = []
        for e in range(experts):
            first = jnp.where(ids[:, :part] == e, gated[:, :part], 0.0)
            rows.append(jnp.where(ids[:, part:] == e, gated[:, part:], first).astype(LOW))
        columns.append(jnp.concatenate(rows, 0))
    mixed = jnp.concatenate(columns, 1)
    return mixed, mm(mixed.T, out_proj)


def queries_kernel(groups, meta, h, route, query_proj, router_t, slot_out, gate_out):
    slot_queries(h[...], route[...], query_proj[...], router_t[...], groups, slot_out, gate_out)


def attend_kernel(groups, side, causal, planes, next_queries, meta, resid, slots, gates, route, *rest):
    kv_refs, rest = rest[:planes], rest[planes:]
    out_proj, rest = rest[0], rest[1:]
    if next_queries:
        (gain, shift, next_route, next_proj, next_router, new_resid, lse_out, att_out, mixed_out, next_slots, next_gates) = rest
    else:
        (new_resid, lse_out, att_out, mixed_out) = rest
    experts = out_proj.shape[0] // slots.shape[0]
    mixed, branch = attend(meta, side, causal, slots, gates, route, kv_refs, out_proj[...], groups, experts, lse_out, att_out)
    mixed_out[...] = mixed
    total = resid[...].astype(FULL) + branch
    new_resid[...] = total
    if next_queries:
        normal, _ = normalise(total)
        h = (normal * gain[3:4] + shift[3:4]).astype(LOW)
        slot_queries(h, next_route[...], next_proj[...], next_router[...], groups, next_slots, next_gates)


def place_weights(meta, own_first, own_second, pieces, first, second):
    r = meta[0]
    first[0] = own_first[...]
    second[0] = own_second[...]
    ways = len(pieces)
    rows = own_first.shape[0] // ways
    for j, piece in enumerate(pieces):
        at = pl.ds(pl.multiple_of((r ^ j) * rows, rows), rows)
        for k in range(1, first.shape[0]):
            first[k, at, :] = piece[k - 1, :rows]
            second[k, at, :] = piece[k - 1, rows:]


def feed_forward_kernel(ways, meta, state, gain, shift, out_bias, bias, keyval, own_first, own_second, *rest):
    pieces, (memory, low_out, kv_out, first, second) = rest[:ways], rest[ways:]
    place_weights(meta, own_first, own_second, pieces, first, second)
    value = state[...]
    normal, _ = normalise(value)
    h = (normal * gain[1:2] + shift[1:2]).astype(LOW)
    memory[...] = value + out_bias[0:1].astype(FULL)

    def step(k, carry):
        pre = mm(h, first[k]) + bias[k]
        act = jax.nn.gelu(pre).astype(LOW)
        memory[...] += mm(act, second[k])
        return carry

    lax.fori_loop(0, first.shape[0], step, 0)
    low = memory[...].astype(LOW)
    low_out[...] = low
    kv_out[...] = mm(low, keyval[...]).astype(LOW)


def feed_backward_core(meta, h, upstream_low, ways, bias, first, second, grad, d_h, kept, sent, bias_grad, state):
    r, z = meta[0], meta[1]
    h_t = h.T
    up_t = upstream_low.T
    d_h[...] = jnp.zeros_like(d_h)
    rows = h.shape[1] // ways

    def step(k, carry):
        w_first, w_second = first[k], second[k]
        pre = mm(h, w_first) + bias[k]
        act, slope = gelu_parts(pre)
        act = act.astype(LOW)
        if state is not None:
            state[...] += mm(act, w_second)
        d_pre_full = (mm_nt(upstream_low, w_second) * slope).astype(LOW)
        d_h[...] += mm_nt(d_pre_full, w_first)
        bias_grad[z ^ k] = jnp.sum(d_pre_full.astype(FULL), 0, keepdims=True)
        for half, product in enumerate((mm(h_t, d_pre_full), mm(up_t, act))):
            grad[...] = product
            for j in range(ways):
                block = grad[pl.ds(pl.multiple_of((r ^ j) * rows, rows), rows), :].astype(LOW)
                target = sent if j & 1 else kept
                target[j // 2, k, half * rows : (half + 1) * rows, :] = block
        return carry

    lax.fori_loop(0, first.shape[0], step, 0)


def decoder_feed_kernel(ways, groups, meta, state_in, cotangent, gain, shift, out_bias, bias, own_first, own_second, *rest):
    pieces, (decoded, state_grad, kept, sent, bias_grad, sums, first, second, grad, d_h) = rest[:ways], rest[ways:]
    place_weights(meta, own_first, own_second, pieces, first, second)
    value = state_in[...]
    normal, inverse = normalise(value)
    h = (normal * gain[4:5] + shift[4:5]).astype(LOW)
    decoded[...] = value + out_bias[1:2].astype(FULL)
    part = value.shape[0] // groups
    seeds = []
    for g in range(groups):
        row = meta[1] * part + lax.broadcasted_iota(jnp.int32, (part, value.shape[1]), 0)
        seeds.append(jnp.where(row < meta[4 + g], cotangent[g * part : (g + 1) * part, :].astype(FULL), 0.0))
    seed = jnp.concatenate(seeds, 0)
    feed_backward_core(meta, h, seed.astype(LOW), ways, bias, first, second, grad, d_h, kept, sent, bias_grad, decoded)
    normal, inverse = normalise(state_in[...])
    upstream = d_h[...]
    state_grad[...] = seed + norm_back(upstream, normal, inverse, gain[4:5])
    sums[0:1] = jnp.sum(upstream * normal, 0, keepdims=True)
    sums[1:2] = jnp.sum(upstream, 0, keepdims=True)
    sums[2:3] = jnp.sum(seed, 0, keepdims=True)
    sums[3:8] = jnp.zeros((5, sums.shape[1]), FULL)


def total_of(blocks):
    total = blocks[0][...].astype(FULL)
    for block in blocks[1:]:
        total = total + block[...].astype(FULL)
    return total.astype(LOW)


def write_pieces(meta, ways, values, scratch, kept, sent):
    scratch[...] = values
    rows = values.shape[0] // ways
    for j in range(ways):
        at = pl.ds(pl.multiple_of((meta[0] ^ j) * rows, rows), rows)
        place = sent if j & 1 else kept
        place[j // 2] = scratch[at, :].astype(LOW)


def encoder_feed_kernel(ways, planes, meta, state_in, memory_low, gain, shift, bias, keyval, *rest):
    blocks, rest = rest[:planes], rest[planes:]
    own_first, own_second = rest[:2]
    pieces, rest = rest[2 : 2 + ways], rest[2 + ways :]
    (memory_grad, state_grad, keyval_kept, keyval_sent, kept, sent, bias_grad, sums, first, second, grad, d_h, keyval_grad) = rest
    place_weights(meta, own_first, own_second, pieces, first, second)
    d_kv = total_of(blocks)
    upstream_in = mm_nt(d_kv, keyval[...])
    memory_grad[...] = upstream_in
    write_pieces(meta, ways, mm(d_kv.T, memory_low[...]), keyval_grad, keyval_kept, keyval_sent)
    normal, inverse = normalise(state_in[...])
    h = (normal * gain[1:2] + shift[1:2]).astype(LOW)
    feed_backward_core(meta, h, upstream_in.astype(LOW), ways, bias, first, second, grad, d_h, kept, sent, bias_grad, None)
    normal, inverse = normalise(state_in[...])
    upstream = d_h[...]
    state_grad[...] = memory_grad[...] + norm_back(upstream, normal, inverse, gain[1:2])
    sums[0:1] = jnp.sum(upstream * normal, 0, keepdims=True)
    sums[1:2] = jnp.sum(upstream, 0, keepdims=True)
    sums[2:3] = jnp.sum(memory_grad[...], 0, keepdims=True)
    sums[3:8] = jnp.zeros((5, sums.shape[1]), FULL)


def attend_back_kernel(groups, side, causal, planes, experts, meta, upstream, slots, gates, route, lse, att, *rest):
    kv_refs, rest = rest[:planes], rest[planes:]
    out_proj, d_kv_kept, d_kv_sent, query_rows_out, logit_out = rest
    z = meta[1]
    head = slots.shape[0]
    branch_grad = upstream[...].astype(LOW)
    part = branch_grad.shape[0] // groups
    lanes = 2 * part
    d_mixed = mm_nt(out_proj[...], branch_grad)
    query_columns, logit_columns = [], []
    for g in range(groups):
        here = slice(g * lanes, (g + 1) * lanes)
        ids = route[:, here]
        gate = gates[:, here]
        attended = att[:, here]
        mine = d_mixed[:, g * part : (g + 1) * part]
        spread = jnp.concatenate([mine, mine], 1)
        slot_grad = jnp.zeros((head, lanes), FULL)
        for e in range(experts):
            slot_grad = jnp.where(ids == e, spread[e * head : (e + 1) * head], slot_grad)
        gate_grad = jnp.sum(attended * slot_grad, 0, keepdims=True)
        weighted = gate * gate_grad
        both = weighted[:, :part] + weighted[:, part:]
        chosen_grad = gate * (gate_grad - jnp.concatenate([both, both], 1))
        att_grad = (gate * slot_grad).astype(LOW)
        inner = jnp.sum(att_grad.astype(FULL) * attended, 0, keepdims=True)
        q = slots[:, here]
        zeros = jnp.zeros_like(q)
        kv = jnp.concatenate([ref[g * part : (g + 1) * part, :] for ref in kv_refs], 0)
        scores = mm(kv, jnp.concatenate([q, zeros], 0))
        ok = allowed_keys(scores.shape, z, part, planes, meta[2 + 2 * side + g], causal)
        probs = jnp.exp(jnp.where(ok, scores, -1e30) - lse[:, here])
        probs_grad = mm(kv, jnp.concatenate([zeros, att_grad], 0))
        score_grad = (probs * (probs_grad - inner)).astype(LOW)
        d_kv = mm(score_grad, jnp.concatenate([q, zeros], 0).T) + mm(
            probs.astype(LOW), jnp.concatenate([zeros, att_grad], 0).T
        )
        for k in range(planes):
            place = d_kv_sent if k & 1 else d_kv_kept
            place[k // 2, g * part : (g + 1) * part, :] = d_kv[k * part : (k + 1) * part].astype(LOW)
        slot_query_grad = mm(kv.T, score_grad)[:head] * (float(head) ** -0.5)
        rows = []
        for e in range(experts):
            first = jnp.where(ids[:, :part] == e, slot_query_grad[:, :part], 0.0)
            rows.append(jnp.where(ids[:, part:] == e, slot_query_grad[:, part:], first).astype(LOW))
        query_columns.append(jnp.concatenate(rows, 0))
        expert = lax.broadcasted_iota(jnp.int32, (experts, part), 0)
        first = jnp.where(ids[:, :part] == expert, chosen_grad[:, :part], 0.0)
        logit_columns.append(jnp.where(ids[:, part:] == expert, chosen_grad[:, part:], first))
    query_rows_out[...] = jnp.concatenate(query_columns, 1)
    logit_out[...] = jnp.concatenate(logit_columns, 1)


def project_back_kernel(ways, norm_row, finish, meta, upstream, state, gain, shift, mixed, query_rows, logit_grad, query_proj, router, result, kept, sent, router_grad, sums, grad):
    normal, inverse = normalise(state[...].astype(FULL))
    h = (normal * gain[norm_row : norm_row + 1] + shift[norm_row : norm_row + 1]).astype(LOW)
    query_grad_rows = query_rows[...]
    high, low = split_low(logit_grad[...])
    router_grad[...] = mm(high, h) + mm(low, h)
    d_h = mm_nt(query_grad_rows.T, query_proj[...])
    d_h = d_h + mm_nt(high.T, router[...]) + mm_nt(low.T, router[...])
    rows_each = grad.shape[0] // ways
    for half in range(2):
        if half == 0:
            grad[...] = mm(query_grad_rows, h)
        else:
            grad[...] = mm(mixed[...], upstream[...].astype(LOW))
        for j in range(ways):
            at = pl.ds(pl.multiple_of((meta[0] ^ j) * rows_each, rows_each), rows_each)
            place = sent if j & 1 else kept
            place[j // 2, half * rows_each : (half + 1) * rows_each, :] = grad[at, :].astype(LOW)
    if finish:
        result[...] = upstream[...] + norm_back(d_h, normal, inverse, gain[norm_row : norm_row + 1])
        sums[0:1] = jnp.sum(d_h * normal, 0, keepdims=True)
        sums[1:2] = jnp.sum(d_h, 0, keepdims=True)
        sums[2:8] = jnp.zeros((6, sums.shape[1]), FULL)
    else:
        result[...] = d_h
        sums[...] = jnp.zeros_like(sums)


def finish_kernel(planes, ways, norm_row, pieces, meta, partial, upstream, state, gain, shift, keyval, *rest):
    blocks, rest = rest[:planes], rest[planes:]
    d_kv = total_of(blocks)
    normal, inverse = normalise(state[...].astype(FULL))
    h = (normal * gain[norm_row : norm_row + 1] + shift[norm_row : norm_row + 1]).astype(LOW)
    keyval_grad = mm(d_kv.T, h)
    if pieces:
        result, keyval_kept, keyval_sent, sums, scratch = rest
        write_pieces(meta, ways, keyval_grad, scratch, keyval_kept, keyval_sent)
    else:
        result, keyval_out, sums = rest
        keyval_out[...] = keyval_grad
    d_h = partial[...] + mm_nt(d_kv, keyval[...])
    result[...] = upstream[...] + norm_back(d_h, normal, inverse, gain[norm_row : norm_row + 1])
    sums[0:1] = jnp.sum(d_h * normal, 0, keepdims=True)
    sums[1:2] = jnp.sum(d_h, 0, keepdims=True)
    sums[2:8] = jnp.zeros((6, sums.shape[1]), FULL)


def pack_kernel(groups, meta, routes, sums_zero, sums_one, sums_two, sums_three, sums_four, router_zero, router_one, router_two, bias_zero, bias_one, keyval_zero, out):
    experts = router_zero.shape[0]
    planes = bias_zero.shape[0]
    head = keyval_zero.shape[0]
    width = out.shape[1]
    slots_all = routes.shape[2]
    part = slots_all // (2 * groups)
    out[:head] = keyval_zero[...].astype(LOW)
    out[head : head + 40] = jnp.concatenate(
        [sums_zero[...], sums_one[...], sums_two[...], sums_three[...], sums_four[...]], 0
    ).astype(LOW)
    at = head + 40
    expert = lax.broadcasted_iota(jnp.int32, (experts, slots_all), 0)
    lane = lax.broadcasted_iota(jnp.int32, (experts, slots_all), 1)
    position = meta[1] * part + lane % part
    hits = []
    for j in range(3):
        inside = jnp.zeros((experts, slots_all), jnp.bool_)
        for g in range(groups):
            mine = (lane // (2 * part)) == g
            inside = inside | (mine & (position < meta[2 + g + (groups if j else 0)]))
        hits.append(jnp.where((routes[j] == expert) & inside, 1.0, 0.0))
    hits.append(jnp.zeros((128 - 3 * experts, slots_all), FULL))
    hits = jnp.concatenate(hits, 0).astype(LOW)
    counts = mm_nt(jnp.ones((16, slots_all), LOW), hits).astype(jnp.int32)
    bit = lax.broadcasted_iota(jnp.int32, counts.shape, 0)
    digits = (lax.shift_right_logical(counts, bit) & 1).astype(FULL)
    out[at : at + 16, 128:] = jnp.zeros((16, width - 128), LOW)
    out[at : at + 16, :128] = digits.astype(LOW)
    at += 16
    rows = [router_zero[...], router_one[...], router_two[...]]
    rows += [bias_zero[k] for k in range(planes)] + [bias_one[k] for k in range(planes)]
    rows = jnp.concatenate(rows, 0)
    rows = jnp.concatenate([rows, jnp.zeros((out.shape[0] - at - rows.shape[0], width), FULL)], 0)
    out[at:] = rows.astype(LOW)


def unpack_kernel(planes, experts, meta, total, gain_out, shift_out, final_out, router_out, keyval_out, bias_out, out_bias_out, counts_out, scratch, turned, semaphore):
    head = turned.shape[1]
    scratch[...] = total[...].astype(FULL)
    turned[...] = scratch[:head].T
    copy = pltpu.make_async_copy(turned, keyval_out.at[0], semaphore)
    copy.start()
    sums = [scratch[head + 8 * n : head + 8 * n + 8] for n in range(5)]
    gain_out[...] = jnp.concatenate([sums[n][0:1] for n in range(4)], 0)
    shift_out[...] = jnp.concatenate([sums[n][1:2] for n in range(4)], 0)
    final_out[...] = sums[4][0:2]
    out_bias_out[...] = jnp.concatenate([sums[1][2:3], sums[4][2:3]], 0)
    at = head + 40
    digits = scratch[at : at + 16, :128]
    weight = lax.shift_left(jnp.int32(1), lax.broadcasted_iota(jnp.int32, digits.shape, 0))
    value = jnp.sum(digits * weight.astype(FULL), 0, keepdims=True).astype(jnp.int32)
    for j in range(3):
        counts_out[j : j + 1, :] = value[:, j * experts : (j + 1) * experts]
    at += 16
    for j in range(3):
        router_out[j] = scratch[at + j * experts : at + (j + 1) * experts]
    at += 3 * experts
    for layer in range(2):
        bias_out[layer : layer + 1, :] = scratch[pl.ds(at + layer * planes + meta[1], 1), :]
    copy.wait()


def swap(values, axis_name, bits):
    size = lax.axis_size(axis_name)
    return lax.ppermute(values, axis_name, [(i, i ^ bits) for i in range(size)])


def ways_of():
    return min(lax.axis_size("rows"), 8)


def bits_of(axis_name, first=1):
    bits, bit = [], first
    while bit < lax.axis_size(axis_name):
        bits.append(bit)
        bit *= 2
    return bits


def entry_of(item):
    return item[0][item[1]] if isinstance(item, tuple) else item


def first_planes(values):
    have = {0: values}
    have.update({bit: swap(values, "ffn", bit) for bit in bits_of("ffn")[::-1]})
    return have


def other_planes(have, received):
    for bit in bits_of("ffn")[::-1]:
        known = {k: part for k, part in received.items() if k & (bit - 1) == 0 and k & ~(2 * bit - 1)}
        received.update({k | bit: swap(part, "ffn", bit) for k, part in known.items() if k | bit not in received})
    return [{**have, **received}[k] for k in range(lax.axis_size("ffn"))]


def even_rows(own):
    return [own] + [swap(own, "rows", k) for k in range(2, ways_of(), 2)]


def all_rows(even):
    return [part for piece in even for part in (piece, swap(piece, "rows", 1))]


def cross_rows(parts):
    return [swap(part, "rows", 2 * half + 2) for half, part in enumerate(parts)]


def place_kernel(ways, layer, entries, small, meta, *refs):
    pieces = refs[:ways]
    first_out, second_out, query_out, out_out, keyval_out, plain, turned, turn, narrow, semaphores = refs[-10:]
    r = meta[0]
    rows = turn.shape[0] // ways
    copies = []

    def send(source, place):
        copies.append(pltpu.make_async_copy(source, place, semaphores.at[len(copies)]))
        copies[-1].start()

    for n in range(1 + len(entries)):
        for j, piece in enumerate(pieces):
            at = pl.ds(pl.multiple_of((r ^ j) * rows, rows), rows)
            base = 2 * rows * n
            halves = [piece[base : base + rows].astype(FULL), piece[base + rows : base + 2 * rows].astype(FULL)]
            plain[n, at, :] = halves[1 if n else 0]
            turn[at, :] = halves[0 if n else 1]
        turned[n] = turn[...].T
        if n:
            send(plain.at[n], out_out.at[entries[n - 1]])
            send(turned.at[n], query_out.at[entries[n - 1]])
        else:
            send(plain.at[0], first_out.at[layer])
            send(turned.at[0], second_out.at[layer])
    few = turn.shape[1] // 4 // ways
    for n in range(len(small)):
        for j, piece in enumerate(pieces):
            at = pl.ds(pl.multiple_of((r ^ j) * few, few), few)
            base = 2 * rows * (1 + len(entries)) + few * n
            turn[at, :] = piece[base : base + few].astype(FULL)
        narrow[n] = turn[: few * ways].T
        send(narrow.at[n], keyval_out.at[small[n]])
    for copy in copies:
        copy.wait()


def body(
    source,
    target,
    cotangent,
    source_lengths,
    target_lengths,
    routes,
    norm_gain,
    norm_shift,
    moa_router,
    moa_query,
    moa_keyval,
    moa_out,
    ffn_in,
    ffn_in_bias,
    ffn_out,
    ffn_out_bias,
):
    groups, row_count, width = source.shape
    tokens = groups * row_count
    planes = lax.axis_size("ffn")
    ways = ways_of()
    experts = moa_router.shape[2]
    both = moa_keyval.shape[2]
    head = both // 2
    hidden = ffn_in.shape[2]
    slots_all = 2 * tokens
    meta = (source_lengths, target_lengths)
    flat = lambda values: values.reshape(tokens, width)
    source, target, cotangent = flat(source), flat(target), flat(cotangent)
    route_rows = jnp.swapaxes(routes, 2, 3).reshape(3, 1, slots_all)
    router_t = jnp.swapaxes(moa_router, 1, 2)
    norms = (norm_gain, norm_shift)

    rows_like = like((tokens, width), FULL)
    low_like = like((tokens, width), LOW)
    kv_like = like((tokens, both), LOW)
    sums_like = like((8, width), FULL)
    slot_like = [like((head, slots_all), LOW), like((1, slots_all), FULL)]

    last = []

    def run(body, out_shape, args, scratch=(), after=(), **more):
        after = tuple(after) + tuple(last)
        results = call(body, out_shape, args, scratch, after, **more)
        flat_results = jax.tree.leaves(results)
        last[:] = [min(flat_results, key=lambda array: array.size)]
        return results

    def hold(*arrays):
        held = lax.optimization_barrier((arrays, tuple(last)))[0]
        return held if len(arrays) > 1 else held[0]

    def mark(*arrays):
        last.extend(jax.tree.leaves(arrays))

    def relay(have):
        keys = [k for k in have if k]
        held = hold(*(have[k] for k in keys))
        mark(held)
        return other_planes(have, dict(zip(keys, held)))

    def sums(*outs):
        results = []
        for slots in outs:
            parts = []
            for slot in slots:
                parts.append(sum(entry_of(arg).astype(FULL) for arg in slot).astype(LOW))
            results.append(parts[0] if len(parts) == 1 else jnp.concatenate(parts))
        return results

    piece_rows = 2 * width // ways

    def cut(layer, after=()):
        return run(
            functools.partial(cut_kernel, ways, layer),
            like((piece_rows + 16, hidden), LOW),
            (*meta, ffn_in, ffn_out, ffn_in_bias),
            [pltpu.SemaphoreType.DMA((2,))],
            after,
            name="cut",
            whole=(2, 3),
        )

    def join(parts):
        biases = jnp.stack([part[piece_rows] for part in parts])[:, None].astype(FULL)
        return jnp.stack([part[:piece_rows] for part in parts[1:]]), biases

    def prepare(j, row, value, after=()):
        return run(
            functools.partial(prepare_kernel, row),
            [low_like, kv_like],
            (*meta, value, *norms, (moa_keyval, j)),
            after=after,
            name="prepare",
        )

    def queries(j, h, after=()):
        return run(
            functools.partial(queries_kernel, groups),
            slot_like,
            (*meta, h, (route_rows, j), (moa_query, j), (router_t, j)),
            after=after,
            name="queries",
        )

    kept_like = [
        rows_like,
        like((1, slots_all), FULL),
        like((head, slots_all), FULL),
        like((experts * head, tokens), LOW),
    ]

    def attention(j, side, causal, resid, slots, kv_blocks, following, after=()):
        extra, more = (), []
        if following:
            extra = (*norms, (route_rows, 2), (moa_query, 2), (router_t, 2))
            more = slot_like
        return run(
            functools.partial(attend_kernel, groups, side, causal, planes, following),
            kept_like + more,
            (*meta, resid, *slots, (route_rows, j), *kv_blocks, (moa_out, j), *extra),
            after=after,
            name="attend",
        )

    def attention_back(j, side, causal, upstream, slots, saved, kv_blocks, after=()):
        lse, att, mixed = saved
        return run(
            functools.partial(attend_back_kernel, groups, side, causal, planes, experts),
            [like((planes // 2, tokens, both), LOW)] * 2
            + [like((experts * head, tokens), LOW), like((experts, tokens), FULL)],
            (*meta, upstream, *slots, (route_rows, j), lse, att, *kv_blocks, (moa_out, j)),
            after=after,
            name="attend_back",
        )

    def project_back(j, norm_row, finish, upstream, state, saved, rows, after=()):
        return run(
            functools.partial(project_back_kernel, ways, norm_row, finish),
            [rows_like]
            + [like((ways // 2, piece_rows, width), LOW)] * 2
            + [like((experts, width), FULL), sums_like],
            (*meta, upstream, state, *norms, saved[2], *rows, (moa_query, j), (moa_router, j)),
            [pltpu.VMEM((width, width), FULL)],
            after=after,
            name="project_back",
        )

    keyval_like = [like((ways // 2, both // ways, width), LOW)] * 2
    keyval_scratch = [pltpu.VMEM((both, width), FULL)]

    def finish(j, norm_row, partial, upstream, state, blocks, pieces, after=()):
        return run(
            functools.partial(finish_kernel, len(blocks), ways, norm_row, pieces),
            [rows_like] + (keyval_like if pieces else [like((both, width), FULL)]) + [sums_like],
            (*meta, partial, upstream, state, *norms, (moa_keyval, j), *blocks),
            keyval_scratch if pieces else [],
            after=after,
            name="finish",
        )

    halves = range(ways // 2)
    near_planes = list(range(1, planes, 2))
    flat_pieces = lambda values: values.reshape(ways // 2, planes * piece_rows, hidden)
    by_plane = lambda values: values.reshape(planes, piece_rows, hidden)
    two = lambda values: values.reshape(planes // 2, -1, values.shape[-1])

    def pairs(*items):
        kept = hold(*(kept for kept, received in items), *(received for kept, received in items))
        kept, received = kept[: len(items)], kept[len(items) :]
        own, *parts = sums(*([[(k, h), (r, h)] for k, r in zip(kept, received)] for h in halves))
        mark(own, parts)
        return [own] + cross_rows(parts)

    def feed_pairs(kept, received):
        return pairs((flat_pieces(kept), flat_pieces(received)))

    def feed_near(arrays):
        arrays = [by_plane(values) for values in hold(*arrays)]
        slot = lambda k: [(array, k) for array in arrays]
        near, kept = sums([slot(k) for k in near_planes], [slot(k - 1) for k in near_planes])
        mark(near, kept)
        return two(kept), two(swap(near, "ffn", 1))

    def planes_far(kept, near):
        kept, near = hold(kept, near)
        (far,) = sums([[(kept, k), (near, k)] for k in range(1, planes // 2)])
        mark(far)
        rows_each = kept.shape[1]
        return [(kept, 0), (near, 0)] + [
            swap(far[(k - 1) * rows_each : k * rows_each], "ffn", 2 * k) for k in range(1, planes // 2)
        ]

    def total(*slots):
        flat_slots = [arg for slot in slots for arg in slot]
        arrays = hold(*(arg[0] if isinstance(arg, tuple) else arg for arg in flat_slots))
        arrays = [
            (array, arg[1]) if isinstance(arg, tuple) else array
            for array, arg in zip(arrays, flat_slots)
        ]
        taken = []
        for slot in slots:
            taken.append(arrays[: len(slot)])
            arrays = arrays[len(slot) :]
        (result,) = sums(taken)
        mark(result)
        return result

    def over_more_rows(values):
        for bit in bits_of("rows", ways):
            values = total([values, swap(values, "rows", bit)])
        return values

    def join(have):
        parts = hold(*have)
        biases = jnp.stack([part[piece_rows] for part in parts])[:, None].astype(FULL)
        own = jnp.stack([part[:piece_rows] for part in parts[1:]])
        mark(own)
        return even_rows(own), biases

    def core(even):
        even = hold(*even)
        mark(even)
        return all_rows(even)

    weights_zero = first_planes(cut(0))
    h_source, kv_source = prepare(0, 0, source)
    kv_zero = first_planes(kv_source)
    slots_zero = queries(0, h_source)
    weights_zero = relay(weights_zero)
    h_target, kv_target = prepare(1, 2, target)
    kv_zero = relay(kv_zero)
    kv_one = first_planes(hold(kv_target))
    weights_one = cut(1)
    even_zero, bias_zero = join(weights_zero)
    slots_one = queries(1, h_target)
    kv_one = relay(kv_one)
    middle, *saved_zero = attention(0, 0, False, source, slots_zero, kv_zero, False)
    weights_one = first_planes(hold(weights_one))
    first_state, *saved_one, next_slots, next_gates = attention(
        1, 1, True, target, slots_one, kv_one, True
    )
    slots_two = (next_slots, next_gates)
    weights_one = relay(weights_one)
    pieces_zero = core(even_zero)
    even_one, bias_one = join(weights_one)
    weight_scratch = [pltpu.VMEM((planes, width, hidden), LOW), pltpu.VMEM((planes, hidden, width), LOW)]
    memory, memory_low, kv_memory = run(
        functools.partial(feed_forward_kernel, ways),
        [rows_like, low_like, kv_like],
        (*meta, middle, *norms, ffn_out_bias, bias_zero, (moa_keyval, 2))
        + ((ffn_in, 0), (ffn_out, 0), *pieces_zero),
        weight_scratch,
        name="encoder_feed",
    )
    kv_two = relay(first_planes(kv_memory))
    pieces_one = core(even_one)
    second_state, *saved_two = attention(2, 0, False, first_state, slots_two, kv_two, False)

    back_scratch = weight_scratch + [pltpu.VMEM((width, hidden), FULL), pltpu.VMEM((tokens, width), FULL)]
    feed_like = [like((ways // 2, planes, piece_rows, hidden), LOW)] * 2
    feed_like += [like((planes, 1, hidden), FULL), sums_like]
    decoded, second_grad, one_kept, one_sent, bias_grad_one, sums_four = run(
        functools.partial(decoder_feed_kernel, ways, groups),
        [rows_like, rows_like] + feed_like,
        (*meta, second_state, cotangent, *norms, ffn_out_bias, bias_one)
        + ((ffn_in, 1), (ffn_out, 1), *pieces_one),
        back_scratch,
        name="decoder_feed",
    )
    one_received = swap(one_sent, "rows", 1)
    d_kv_kept_two, d_kv_sent, *rows_two = attention_back(
        2, 0, False, second_grad, slots_two, saved_two, kv_two
    )
    d_kv_near_two = swap(d_kv_sent, "ffn", 1)
    one = feed_pairs(one_kept, one_received)
    first_grad, kept_two, sent_two, router_two, sums_three = project_back(
        2, 3, True, second_grad, first_state, saved_two, rows_two
    )
    received_two = swap(sent_two, "rows", 1)
    d_kv_two = planes_far(d_kv_kept_two, d_kv_near_two)
    received_two = hold(received_two)
    mark(received_two)
    d_kv_kept_one, d_kv_sent, *rows_one = attention_back(
        1, 1, True, first_grad, slots_one, saved_one, kv_one
    )
    d_kv_near_one = swap(d_kv_sent, "ffn", 1)
    self_grad, kept_one, sent_one, router_one, unused = project_back(
        1, 2, False, first_grad, target, saved_one, rows_one
    )
    received_one = swap(sent_one, "rows", 1)
    one_kept, one_near = feed_near(one)
    d_kv_one = planes_far(d_kv_kept_one, d_kv_near_one)
    later = pairs((kept_one, received_one), (kept_two, received_two))
    (memory_grad, middle_grad, keyval_kept_two, keyval_sent_two, zero_kept, zero_sent, bias_grad_zero, sums_one) = run(
        functools.partial(encoder_feed_kernel, ways, len(d_kv_two)),
        [rows_like, rows_like] + keyval_like + feed_like,
        (*meta, middle, memory_low, *norms, bias_zero, (moa_keyval, 2), *d_kv_two)
        + ((ffn_in, 0), (ffn_out, 0), *pieces_zero),
        back_scratch + keyval_scratch,
        name="encoder_feed_back",
    )
    zero_received = swap(zero_sent, "rows", 1)
    one_parts = planes_far(one_kept, one_near)
    d_kv_kept_zero, d_kv_sent, *rows_zero = attention_back(
        0, 0, False, middle_grad, slots_zero, saved_zero, kv_zero
    )
    d_kv_near_zero = swap(d_kv_sent, "ffn", 1)
    zero = feed_pairs(zero_kept, zero_received)
    encoder_grad, kept_zero, sent_zero, router_zero, unused = project_back(
        0, 0, False, middle_grad, source, saved_zero, rows_zero
    )
    d_kv_zero = planes_far(d_kv_kept_zero, d_kv_near_zero)
    later = total(later)
    later_next = swap(later, "ffn", 1)
    target_grad, keyval_kept_one, keyval_sent_one, sums_two = finish(
        1, 2, self_grad, first_grad, target, d_kv_one, True
    )
    sent_zero, keyval_sent_one, keyval_sent_two = hold(sent_zero, keyval_sent_one, keyval_sent_two)
    first_sent = jnp.concatenate([sent_zero, keyval_sent_one, keyval_sent_two], 1)
    mark(first_sent)
    first_received = swap(first_sent, "rows", 1)
    later = total([later, later_next])
    later_next = swap(later, "ffn", 2)
    source_grad, keyval_zero, sums_zero = finish(
        0, 0, encoder_grad, middle_grad, source, d_kv_zero, False
    )
    few = both + 40 + 16 + 3 * experts + 2 * planes
    few = (few + 15) // 16 * 16
    packed = run(
        functools.partial(pack_kernel, groups),
        like((few, width), LOW),
        (*meta, route_rows, sums_zero, sums_one, sums_two, sums_three, sums_four)
        + (router_zero, router_one, router_two, bias_grad_zero, bias_grad_one, keyval_zero),
        name="pack",
    )
    stages = [("rows", bit) for bit in bits_of("rows")] + [("ffn", bit) for bit in bits_of("ffn")]

    def advance(count):
        nonlocal packed, packed_next
        for unused in range(count):
            if packed_next is not None:
                packed = total([packed, packed_next])
            packed_next = swap(packed, *stages.pop(0)) if stages else None

    packed_next = None
    advance(1)
    zero_kept, zero_near = feed_near(zero)
    advance(1)
    first_kept = jnp.concatenate([kept_zero, keyval_kept_one, keyval_kept_two], 1)
    first_part = pairs((first_kept, first_received))
    advance(1)
    zero_parts = planes_far(zero_kept, zero_near)
    first_part = total(first_part)
    first_next = swap(first_part, "ffn", 1)
    later = total(one_parts, [later, later_next])
    later_even = even_rows(over_more_rows(later))
    advance(len(stages) - 1)
    first_part = total([first_part, first_next])
    first_next = swap(first_part, "ffn", 2)
    advance(1)
    first_part = total(zero_parts, [first_part, first_next])
    first_even = even_rows(over_more_rows(first_part))
    later_pieces = core(later_even)
    grads_like = [like((2, width, hidden), FULL), like((2, hidden, width), FULL)]
    grads_like += [like((3, width, experts * head), FULL), like((3, experts * head, width), FULL)]
    stay = pl.BlockSpec(memory_space=pl.ANY)
    lies = pl.BlockSpec(memory_space=pltpu.VMEM)

    def place(layer, entries, small, pieces, given):
        count = 1 + len(entries)
        return run(
            functools.partial(place_kernel, ways, layer, entries, small),
            grads_like + [like((3, width, both), FULL)],
            (*meta, *pieces, *given),
            [pltpu.VMEM((count, width, width), FULL)] * 2
            + [pltpu.VMEM((width, width), FULL), pltpu.VMEM((2, width, both), FULL)]
            + [pltpu.SemaphoreType.DMA((2 * count + 2,))],
            name="place",
            whole=range(2 + ways, 2 + ways + len(given)),
            alias={2 + ways + n: n for n in range(len(given))},
            out_specs=[stay] * 5,
        )

    *grads, unused = place(1, (1, 2), (), later_pieces, ())
    first_pieces = core(first_even)
    advance(1)
    gains, shifts, final, routers, keyval_grads, bias_grads, out_biases, counts = run(
        functools.partial(unpack_kernel, planes, experts),
        [like((4, width), FULL), like((4, width), FULL), like((2, width), FULL)]
        + [like((3, experts, width), FULL), like((3, width, both), FULL), like((2, hidden), FULL)]
        + [like((2, width), FULL), like((3, experts), jnp.int32)],
        (*meta, packed),
        [pltpu.VMEM((few, width), FULL), pltpu.VMEM((width, both), FULL), pltpu.SemaphoreType.DMA],
        name="unpack",
        out_specs=[lies] * 4 + [stay] + [lies] * 3,
    )
    first_grads, second_grads, query_grads, out_grads, keyval_grads = place(
        0, (0,), (1, 2), first_pieces, (*grads, keyval_grads)
    )
    whole = lambda values: values.reshape(groups, row_count, width)
    return (
        whole(memory),
        whole(decoded),
        whole(source_grad),
        whole(target_grad),
        whole(memory_grad),
        gains,
        shifts,
        final,
        jnp.swapaxes(routers, 1, 2),
        query_grads,
        keyval_grads,
        out_grads,
        first_grads,
        bias_grads,
        second_grads,
        out_biases,
        counts,
    )


def solution(mesh):
    in_specs = (
        P("rows", "ffn", None),
        P("rows", "ffn", None),
        P("rows", "ffn", None),
        P("rows"),
        P("rows"),
        P(None, "rows", "ffn", None),
        P(),
        P(),
        P(),
        P(),
        P(),
        P(),
        P(None, None, "ffn"),
        P(None, "ffn"),
        P(None, "ffn", None),
        P(),
    )
    out_specs = (
        P("rows", "ffn", None),
        P("rows", "ffn", None),
        P("rows", "ffn", None),
        P("rows", "ffn", None),
        P("rows", "ffn", None),
        P(),
        P(),
        P(),
        P(),
        P(),
        P(),
        P(),
        P(None, None, "ffn"),
        P(None, "ffn"),
        P(None, "ffn", None),
        P(),
        P(),
    )
    return jax.shard_map(body, mesh=mesh, in_specs=in_specs, out_specs=out_specs, check_vma=False)
```

```python
import functools
import jax
import jax.numpy as jnp
from jax import lax
from jax.experimental import pallas as pl
from jax.experimental.pallas import tpu as pltpu
from jax.sharding import PartitionSpec as P

EPS = 1e-05
LOW = jnp.bfloat16
FULL = jnp.float32
VMEM_BYTES = 22 * 1024 * 1024
MICRO = 1 << 30
COSTS = {"cut": 1, "prepare": 1.1, "queries": 1.1, "attend": 3, "encoder_feed": 6, "decoder_feed": 12}
COSTS.update({"attend_back": 4.3, "project_back": 2.8, "encoder_feed_back": 10, "finish": 2.7})
COSTS.update({"finish_pack": 3.5, "prepare_queries": 2, "place": 4})


class Meta:
    def __init__(self, *lengths):
        self.lengths = lengths

    def __getitem__(self, n):
        if n == 0:
            return lax.rem(lax.axis_index("rows"), ways_of())
        if n == 1:
            return lax.axis_index("ffn")
        groups = self.lengths[0].shape[0]
        return self.lengths[(n - 2) // groups][(n - 2) % groups]


def mm(left, right):
    return jnp.dot(left, right, preferred_element_type=FULL)


def mm_nt(left, right):
    return lax.dot_general(left, right, (((1,), (1,)), ((), ())), preferred_element_type=FULL)


def normalise(values):
    center = values - jnp.mean(values, -1, keepdims=True)
    inverse = lax.rsqrt(jnp.mean(center * center, -1, keepdims=True) + EPS)
    return center * inverse, inverse


def norm_back(upstream, normal, inverse, gain_row):
    scaled = upstream * gain_row
    return inverse * (
        scaled
        - jnp.mean(scaled, -1, keepdims=True)
        - normal * jnp.mean(scaled * normal, -1, keepdims=True)
    )


def split_low(values):
    high = values.astype(LOW)
    return high, (values - high.astype(FULL)).astype(LOW)


def gelu_parts(pre):
    c = 0.7978845608028654
    square = pre * pre
    t = jnp.tanh(c * pre * (1.0 + 0.044715 * square))
    half = 0.5 * (1.0 + t)
    act = pre * half
    slope = half + (0.5 * c) * pre * (1.0 - t * t) * (1.0 + 0.134145 * square)
    return act, slope


def call(body, out_shape, args, scratch=(), after=(), name=None, whole=(), alias=None, out_specs=None, smem=0):
    arrays, specs = [], []
    for n, arg in enumerate(args):
        if isinstance(arg, tuple):
            array, entry = arg
            rest = array.shape[1:]
            specs.append(
                pl.BlockSpec(
                    (None,) + rest,
                    lambda step, entry=entry, rest=rest: (entry,) + (0,) * len(rest),
                    pipeline_mode=pl.Buffered(1),
                )
            )
        else:
            array = arg
            space = pltpu.SMEM if n < smem else pltpu.HBM if n in whole else pltpu.VMEM
            specs.append(pl.BlockSpec(memory_space=space))
        arrays.append(array)
    taken, skipped = len(arrays), len(after)

    def run(*refs):
        body(Meta(*refs[:smem]), *refs[smem:taken], *refs[taken + skipped :])

    return pl.pallas_call(
        run,
        grid=(1,),
        out_shape=out_shape,
        in_specs=specs + [pl.BlockSpec(memory_space=pl.ANY)] * skipped,
        out_specs=out_specs
        or jax.tree.map(lambda _: pl.BlockSpec(memory_space=pltpu.VMEM), out_shape),
        scratch_shapes=list(scratch),
        input_output_aliases=alias or {},
        compiler_params=pltpu.CompilerParams(vmem_limit_bytes=VMEM_BYTES),
        cost_estimate=pl.CostEstimate(
            flops=int(COSTS[name] * MICRO), bytes_accessed=1 << 16, transcendentals=0
        ),
        name=name,
    )(*arrays, *after)


def like(shape, dtype):
    return jax.ShapeDtypeStruct(shape, dtype)


def prepare_kernel(row, meta, value, gain, shift, keyval, h_out, kv_out):
    normal, _ = normalise(value[...].astype(FULL))
    h = (normal * gain[row : row + 1] + shift[row : row + 1]).astype(LOW)
    h_out[...] = h
    kv_out[...] = mm(h, keyval[...]).astype(LOW)


def cut_kernel(ways, layer, meta, first, second, bias, mine, biases, semaphores):
    rows = first.shape[1] // ways
    at = pl.ds(pl.multiple_of(meta[0] * rows, rows), rows)
    copies = [
        pltpu.make_async_copy(weight.at[layer, at, :], mine.at[pl.ds(n * rows, rows), :], semaphores.at[n])
        for n, weight in enumerate((first, second))
    ]
    copies.append(pltpu.make_async_copy(bias, biases, semaphores.at[2]))
    for copy in copies:
        copy.start()
    for copy in copies:
        copy.wait()
    mine[2 * rows :] = jnp.broadcast_to(biases[layer : layer + 1, :], (16, biases.shape[1]))


def to_slots(values, groups):
    part = values.shape[1] // groups
    blocks = []
    for g in range(groups):
        block = values[:, g * part : (g + 1) * part]
        blocks += [block, block]
    return jnp.concatenate(blocks, 1)


def slot_queries(h, route, query_proj, router_t, groups, slot_out, gate_out):
    experts = router_t.shape[0]
    queries = mm(h, query_proj).astype(LOW)
    spread = to_slots(queries.T, groups)
    head = spread.shape[0] // experts
    chosen = jnp.zeros((head, spread.shape[1]), LOW)
    for e in range(experts):
        chosen = jnp.where(route == e, spread[e * head : (e + 1) * head], chosen)
    slot_out[...] = chosen * jnp.asarray(float(head) ** -0.5, LOW)
    logits = to_slots(mm_nt(router_t, h), groups)
    ids = lax.broadcasted_iota(jnp.int32, logits.shape, 0)
    picked = jnp.sum(jnp.where(ids == route, logits, 0.0), 0, keepdims=True)
    part = picked.shape[1] // (2 * groups)
    gates = []
    for g in range(groups):
        a = picked[:, 2 * g * part : (2 * g + 1) * part]
        b = picked[:, (2 * g + 1) * part : (2 * g + 2) * part]
        top = jnp.maximum(a, b)
        ea, eb = jnp.exp(a - top), jnp.exp(b - top)
        total = ea + eb
        gates += [ea / total, eb / total]
    gate_out[...] = jnp.concatenate(gates, 1)


def allowed_keys(shape, z, part, planes, length, causal):
    blocks = []
    for k in range(planes):
        position = (z ^ k) * part + lax.broadcasted_iota(jnp.int32, (part, shape[1]), 0)
        ok = position < length
        if causal:
            lane = lax.broadcasted_iota(jnp.int32, (part, shape[1]), 1)
            query = z * part + jnp.where(lane >= part, lane - part, lane)
            ok = ok & (position <= query)
        blocks.append(ok)
    return jnp.concatenate(blocks, 0)


def attend(meta, side, causal, slots, gates, route, kv_refs, out_proj, groups, experts, lse_out, att_out):
    z = meta[1]
    part = kv_refs[0].shape[0] // groups
    planes = len(kv_refs)
    head = slots.shape[0]
    lanes = 2 * part
    columns = []
    for g in range(groups):
        kv = jnp.concatenate([ref[g * part : (g + 1) * part, :] for ref in kv_refs], 0)
        q = slots[:, g * lanes : (g + 1) * lanes]
        padded = jnp.concatenate([q, jnp.zeros_like(q)], 0)
        scores = mm(kv, padded)
        ok = allowed_keys(scores.shape, z, part, planes, meta[2 + 2 * side + g], causal)
        scores = jnp.where(ok, scores, -1e30)
        top = jnp.max(scores, 0, keepdims=True)
        raised = jnp.exp(scores - top)
        total = jnp.sum(raised, 0, keepdims=True)
        lse_out[:, g * lanes : (g + 1) * lanes] = top + jnp.log(total)
        low = (raised * (1.0 / total)).astype(LOW)
        attended = mm(kv.T, low)[head:]
        att_out[:, g * lanes : (g + 1) * lanes] = attended
        gated = attended * gates[:, g * lanes : (g + 1) * lanes]
        ids = route[:, g * lanes : (g + 1) * lanes]
        rows = []
        for e in range(experts):
            first = jnp.where(ids[:, :part] == e, gated[:, :part], 0.0)
            rows.append(jnp.where(ids[:, part:] == e, gated[:, part:], first).astype(LOW))
        columns.append(jnp.concatenate(rows, 0))
    mixed = jnp.concatenate(columns, 1)
    return mixed, mm(mixed.T, out_proj)


def prepare_queries_kernel(groups, row, meta, value, gain, shift, keyval, route, query_proj, router_t, kv_out, slot_out, gate_out):
    normal, _ = normalise(value[...].astype(FULL))
    h = (normal * gain[row : row + 1] + shift[row : row + 1]).astype(LOW)
    kv_out[...] = mm(h, keyval[...]).astype(LOW)
    slot_queries(h, route[...], query_proj[...], router_t[...], groups, slot_out, gate_out)


def queries_kernel(groups, meta, h, route, query_proj, router_t, slot_out, gate_out):
    slot_queries(h[...], route[...], query_proj[...], router_t[...], groups, slot_out, gate_out)


def attend_kernel(groups, side, causal, planes, next_queries, meta, resid, slots, gates, route, *rest):
    kv_refs, rest = rest[:planes], rest[planes:]
    out_proj, rest = rest[0], rest[1:]
    if next_queries:
        (gain, shift, next_route, next_proj, next_router, new_resid, lse_out, att_out, mixed_out, next_slots, next_gates) = rest
    else:
        (new_resid, lse_out, att_out, mixed_out) = rest
    experts = out_proj.shape[0] // slots.shape[0]
    mixed, branch = attend(meta, side, causal, slots, gates, route, kv_refs, out_proj[...], groups, experts, lse_out, att_out)
    mixed_out[...] = mixed
    total = resid[...].astype(FULL) + branch
    new_resid[...] = total
    if next_queries:
        normal, _ = normalise(total)
        h = (normal * gain[3:4] + shift[3:4]).astype(LOW)
        slot_queries(h, next_route[...], next_proj[...], next_router[...], groups, next_slots, next_gates)


def place_weights(meta, own_first, own_second, pieces, first, second):
    r = meta[0]
    first[0] = own_first[...]
    second[0] = own_second[...]
    ways = len(pieces)
    rows = own_first.shape[0] // ways
    for j, piece in enumerate(pieces):
        at = pl.ds(pl.multiple_of((r ^ j) * rows, rows), rows)
        for k in range(1, first.shape[0]):
            first[k, at, :] = piece[k - 1, :rows]
            second[k, at, :] = piece[k - 1, rows:]


def feed_forward_kernel(ways, meta, state, gain, shift, out_bias, bias, keyval, own_first, own_second, *rest):
    pieces, (memory, low_out, kv_out, first, second) = rest[:ways], rest[ways:]
    place_weights(meta, own_first, own_second, pieces, first, second)
    value = state[...]
    normal, _ = normalise(value)
    h = (normal * gain[1:2] + shift[1:2]).astype(LOW)
    memory[...] = value + out_bias[0:1].astype(FULL)

    def step(k, carry):
        pre = mm(h, first[k]) + bias[k]
        act = jax.nn.gelu(pre).astype(LOW)
        memory[...] += mm(act, second[k])
        return carry

    lax.fori_loop(0, first.shape[0], step, 0)
    low = memory[...].astype(LOW)
    low_out[...] = low
    kv_out[...] = mm(low, keyval[...]).astype(LOW)


def feed_backward_core(meta, h, upstream_low, ways, bias, first, second, grad, d_h, kept, sent, bias_grad, state):
    r, z = meta[0], meta[1]
    h_t = h.T
    up_t = upstream_low.T
    d_h[...] = jnp.zeros_like(d_h)
    rows = h.shape[1] // ways

    def step(k, carry):
        w_first, w_second = first[k], second[k]
        pre = mm(h, w_first) + bias[k]
        act, slope = gelu_parts(pre)
        act = act.astype(LOW)
        if state is not None:
            state[...] += mm(act, w_second)
        d_pre_full = (mm_nt(upstream_low, w_second) * slope).astype(LOW)
        d_h[...] += mm_nt(d_pre_full, w_first)
        bias_grad[z ^ k] = jnp.sum(d_pre_full.astype(FULL), 0, keepdims=True)
        for half, product in enumerate((mm(h_t, d_pre_full), mm(up_t, act))):
            grad[...] = product
            for j in range(ways):
                block = grad[pl.ds(pl.multiple_of((r ^ j) * rows, rows), rows), :].astype(LOW)
                target = sent if j & 1 else kept
                target[j // 2, k, half * rows : (half + 1) * rows, :] = block
        return carry

    lax.fori_loop(0, first.shape[0], step, 0)


def decoder_feed_kernel(ways, groups, meta, state_in, cotangent, gain, shift, out_bias, bias, own_first, own_second, *rest):
    pieces, (decoded, state_grad, kept, sent, bias_grad, sums, first, second, grad, d_h) = rest[:ways], rest[ways:]
    place_weights(meta, own_first, own_second, pieces, first, second)
    value = state_in[...]
    normal, inverse = normalise(value)
    h = (normal * gain[4:5] + shift[4:5]).astype(LOW)
    decoded[...] = value + out_bias[1:2].astype(FULL)
    part = value.shape[0] // groups
    seeds = []
    for g in range(groups):
        row = meta[1] * part + lax.broadcasted_iota(jnp.int32, (part, value.shape[1]), 0)
        seeds.append(jnp.where(row < meta[4 + g], cotangent[g * part : (g + 1) * part, :].astype(FULL), 0.0))
    seed = jnp.concatenate(seeds, 0)
    feed_backward_core(meta, h, seed.astype(LOW), ways, bias, first, second, grad, d_h, kept, sent, bias_grad, decoded)
    normal, inverse = normalise(state_in[...])
    upstream = d_h[...]
    state_grad[...] = seed + norm_back(upstream, normal, inverse, gain[4:5])
    sums[0:1] = jnp.sum(upstream * normal, 0, keepdims=True)
    sums[1:2] = jnp.sum(upstream, 0, keepdims=True)
    sums[2:3] = jnp.sum(seed, 0, keepdims=True)
    sums[3:8] = jnp.zeros((5, sums.shape[1]), FULL)


def total_of(blocks):
    total = blocks[0][...].astype(FULL)
    for block in blocks[1:]:
        total = total + block[...].astype(FULL)
    return total.astype(LOW)


def write_pieces(meta, ways, values, scratch, kept, sent):
    scratch[...] = values
    rows = values.shape[0] // ways
    for j in range(ways):
        at = pl.ds(pl.multiple_of((meta[0] ^ j) * rows, rows), rows)
        place = sent if j & 1 else kept
        place[j // 2] = scratch[at, :].astype(LOW)


def encoder_feed_kernel(ways, planes, meta, state_in, memory_low, gain, shift, bias, keyval, *rest):
    blocks, rest = rest[:planes], rest[planes:]
    own_first, own_second = rest[:2]
    pieces, rest = rest[2 : 2 + ways], rest[2 + ways :]
    (memory_grad, state_grad, keyval_kept, keyval_sent, kept, sent, bias_grad, sums, first, second, grad, d_h, keyval_grad) = rest
    place_weights(meta, own_first, own_second, pieces, first, second)
    d_kv = total_of(blocks)
    upstream_in = mm_nt(d_kv, keyval[...])
    memory_grad[...] = upstream_in
    write_pieces(meta, ways, mm(d_kv.T, memory_low[...]), keyval_grad, keyval_kept, keyval_sent)
    normal, inverse = normalise(state_in[...])
    h = (normal * gain[1:2] + shift[1:2]).astype(LOW)
    feed_backward_core(meta, h, upstream_in.astype(LOW), ways, bias, first, second, grad, d_h, kept, sent, bias_grad, None)
    normal, inverse = normalise(state_in[...])
    upstream = d_h[...]
    state_grad[...] = memory_grad[...] + norm_back(upstream, normal, inverse, gain[1:2])
    sums[0:1] = jnp.sum(upstream * normal, 0, keepdims=True)
    sums[1:2] = jnp.sum(upstream, 0, keepdims=True)
    sums[2:3] = jnp.sum(memory_grad[...], 0, keepdims=True)
    sums[3:8] = jnp.zeros((5, sums.shape[1]), FULL)


def attend_back_kernel(groups, side, causal, planes, experts, meta, upstream, slots, gates, route, lse, att, *rest):
    kv_refs, rest = rest[:planes], rest[planes:]
    out_proj, d_kv_kept, d_kv_sent, query_rows_out, logit_out = rest
    z = meta[1]
    head = slots.shape[0]
    branch_grad = upstream[...].astype(LOW)
    part = branch_grad.shape[0] // groups
    lanes = 2 * part
    d_mixed = mm_nt(out_proj[...], branch_grad)
    query_columns, logit_columns = [], []
    for g in range(groups):
        here = slice(g * lanes, (g + 1) * lanes)
        ids = route[:, here]
        gate = gates[:, here]
        attended = att[:, here]
        mine = d_mixed[:, g * part : (g + 1) * part]
        spread = jnp.concatenate([mine, mine], 1)
        slot_grad = jnp.zeros((head, lanes), FULL)
        for e in range(experts):
            slot_grad = jnp.where(ids == e, spread[e * head : (e + 1) * head], slot_grad)
        gate_grad = jnp.sum(attended * slot_grad, 0, keepdims=True)
        weighted = gate * gate_grad
        both = weighted[:, :part] + weighted[:, part:]
        chosen_grad = gate * (gate_grad - jnp.concatenate([both, both], 1))
        att_grad = (gate * slot_grad).astype(LOW)
        inner = jnp.sum(att_grad.astype(FULL) * attended, 0, keepdims=True)
        q = slots[:, here]
        zeros = jnp.zeros_like(q)
        kv = jnp.concatenate([ref[g * part : (g + 1) * part, :] for ref in kv_refs], 0)
        scores = mm(kv, jnp.concatenate([q, zeros], 0))
        ok = allowed_keys(scores.shape, z, part, planes, meta[2 + 2 * side + g], causal)
        probs = jnp.exp(jnp.where(ok, scores, -1e30) - lse[:, here])
        probs_grad = mm(kv, jnp.concatenate([zeros, att_grad], 0))
        score_grad = (probs * (probs_grad - inner)).astype(LOW)
        d_kv = mm(score_grad, jnp.concatenate([q, zeros], 0).T) + mm(
            probs.astype(LOW), jnp.concatenate([zeros, att_grad], 0).T
        )
        for k in range(planes):
            place = d_kv_sent if k & 1 else d_kv_kept
            place[k // 2, g * part : (g + 1) * part, :] = d_kv[k * part : (k + 1) * part].astype(LOW)
        slot_query_grad = mm(kv.T, score_grad)[:head] * (float(head) ** -0.5)
        rows = []
        for e in range(experts):
            first = jnp.where(ids[:, :part] == e, slot_query_grad[:, :part], 0.0)
            rows.append(jnp.where(ids[:, part:] == e, slot_query_grad[:, part:], first).astype(LOW))
        query_columns.append(jnp.concatenate(rows, 0))
        expert = lax.broadcasted_iota(jnp.int32, (experts, part), 0)
        first = jnp.where(ids[:, :part] == expert, chosen_grad[:, :part], 0.0)
        logit_columns.append(jnp.where(ids[:, part:] == expert, chosen_grad[:, part:], first))
    query_rows_out[...] = jnp.concatenate(query_columns, 1)
    logit_out[...] = jnp.concatenate(logit_columns, 1)


def project_back_kernel(ways, norm_row, finish, meta, upstream, state, gain, shift, mixed, query_rows, logit_grad, query_proj, router, result, kept, sent, router_grad, sums, grad):
    normal, inverse = normalise(state[...].astype(FULL))
    h = (normal * gain[norm_row : norm_row + 1] + shift[norm_row : norm_row + 1]).astype(LOW)
    query_grad_rows = query_rows[...]
    high, low = split_low(logit_grad[...])
    router_grad[...] = mm(high, h) + mm(low, h)
    d_h = mm_nt(query_grad_rows.T, query_proj[...])
    d_h = d_h + mm(high.T, router[...]) + mm(low.T, router[...])
    rows_each = grad.shape[0] // ways
    for half in range(2):
        if half == 0:
            grad[...] = mm(query_grad_rows, h)
        else:
            grad[...] = mm(mixed[...], upstream[...].astype(LOW))
        for j in range(ways):
            at = pl.ds(pl.multiple_of((meta[0] ^ j) * rows_each, rows_each), rows_each)
            place = sent if j & 1 else kept
            place[j // 2, half * rows_each : (half + 1) * rows_each, :] = grad[at, :].astype(LOW)
    if finish:
        result[...] = upstream[...] + norm_back(d_h, normal, inverse, gain[norm_row : norm_row + 1])
        sums[0:1] = jnp.sum(d_h * normal, 0, keepdims=True)
        sums[1:2] = jnp.sum(d_h, 0, keepdims=True)
        sums[2:8] = jnp.zeros((6, sums.shape[1]), FULL)
    else:
        result[...] = d_h
        sums[...] = jnp.zeros_like(sums)


def finish_kernel(planes, ways, norm_row, pieces, meta, partial, upstream, state, gain, shift, keyval, *rest):
    blocks, rest = rest[:planes], rest[planes:]
    d_kv = total_of(blocks)
    normal, inverse = normalise(state[...].astype(FULL))
    h = (normal * gain[norm_row : norm_row + 1] + shift[norm_row : norm_row + 1]).astype(LOW)
    keyval_grad = mm(d_kv.T, h)
    if pieces:
        result, keyval_kept, keyval_sent, sums, scratch = rest
        write_pieces(meta, ways, keyval_grad, scratch, keyval_kept, keyval_sent)
    else:
        result, keyval_out, sums = rest
        keyval_out[...] = keyval_grad
    d_h = partial[...] + mm_nt(d_kv, keyval[...])
    result[...] = upstream[...] + norm_back(d_h, normal, inverse, gain[norm_row : norm_row + 1])
    sums[0:1] = jnp.sum(d_h * normal, 0, keepdims=True)
    sums[1:2] = jnp.sum(d_h, 0, keepdims=True)
    sums[2:8] = jnp.zeros((6, sums.shape[1]), FULL)


def finish_pack_kernel(planes, groups, ways, norm_row, meta, partial, upstream, state, gain, shift, keyval, *rest):
    blocks, rest = rest[:planes], rest[planes:]
    (routes, sums_one, sums_two, sums_three, sums_four, router_zero, router_one, router_two, bias_zero, bias_one) = rest[:10]
    result, keyval_kept, keyval_sent, small_kept, small_sent, sums, keyval_scratch, out = rest[10:]
    finish_kernel(planes, ways, norm_row, True, meta, partial, upstream, state, gain, shift, keyval, *blocks, result, keyval_kept, keyval_sent, sums, keyval_scratch)
    experts = router_zero.shape[0]
    count = bias_zero.shape[0]
    width = out.shape[1]
    slots_all = routes.shape[2]
    part = slots_all // (2 * groups)
    for n, ref in enumerate((sums, sums_one, sums_two, sums_three, sums_four)):
        out[8 * n : 8 * n + 8] = ref[...]
    at = 40
    expert = lax.broadcasted_iota(jnp.int32, (experts, slots_all), 0)
    lane = lax.broadcasted_iota(jnp.int32, (experts, slots_all), 1)
    position = meta[1] * part + lane % part
    hits = []
    for j in range(3):
        inside = jnp.zeros((experts, slots_all), jnp.bool_)
        for g in range(groups):
            mine = (lane // (2 * part)) == g
            inside = inside | (mine & (position < meta[2 + g + (groups if j else 0)]))
        hits.append(jnp.where((routes[j] == expert) & inside, 1.0, 0.0))
    hits.append(jnp.zeros((128 - 3 * experts, slots_all), FULL))
    hits = jnp.concatenate(hits, 0).astype(LOW)
    counts = mm_nt(jnp.ones((16, slots_all), LOW), hits).astype(jnp.int32)
    bit = lax.broadcasted_iota(jnp.int32, counts.shape, 0)
    digits = (lax.shift_right_logical(counts, bit) & 1).astype(FULL)
    out[at : at + 16, 128:] = jnp.zeros((16, width - 128), FULL)
    out[at : at + 16, :128] = digits
    at += 16
    rows = [router_zero[...], router_one[...], router_two[...]]
    rows += [bias_zero[k] for k in range(count)] + [bias_one[k] for k in range(count)]
    rows = jnp.concatenate(rows, 0)
    out[at : at + rows.shape[0]] = rows
    at += rows.shape[0]
    out[at:] = jnp.zeros((out.shape[0] - at, width), FULL)
    write_pieces(meta, ways, out[...], out, small_kept, small_sent)


def unpack(meta, total, planes, experts, gain_out, shift_out, final_out, router_out, bias_out, out_bias_out, counts_out):
    sums = [total[8 * n : 8 * n + 8] for n in range(5)]
    gain_out[...] = jnp.concatenate([sums[n][0:1] for n in range(4)], 0)
    shift_out[...] = jnp.concatenate([sums[n][1:2] for n in range(4)], 0)
    final_out[...] = sums[4][0:2]
    out_bias_out[...] = jnp.concatenate([sums[1][2:3], sums[4][2:3]], 0)
    at = 40
    digits = total[at : at + 16, :128]
    weight = lax.shift_left(jnp.int32(1), lax.broadcasted_iota(jnp.int32, digits.shape, 0))
    value = jnp.sum(digits * weight.astype(FULL), 0, keepdims=True).astype(jnp.int32)
    for j in range(3):
        counts_out[j : j + 1, :] = value[:, j * experts : (j + 1) * experts]
    at += 16
    for j in range(3):
        router_out[j] = total[at + j * experts : at + (j + 1) * experts]
    at += 3 * experts
    for layer in range(2):
        bias_out[layer : layer + 1, :] = total[pl.ds(at + layer * planes + meta[1], 1), :]


def swap(values, axis_name, bits):
    size = lax.axis_size(axis_name)
    return lax.ppermute(values, axis_name, [(i, i ^ bits) for i in range(size)])


def ways_of():
    return min(lax.axis_size("rows"), 8)


def bits_of(axis_name, first=1):
    bits, bit = [], first
    while bit < lax.axis_size(axis_name):
        bits.append(bit)
        bit *= 2
    return bits


def entry_of(item):
    return item[0][item[1]] if isinstance(item, tuple) else item


def first_planes(values):
    have = {0: values}
    have.update({bit: swap(values, "ffn", bit) for bit in bits_of("ffn")[::-1]})
    return have


def other_planes(have, received):
    for bit in bits_of("ffn")[::-1]:
        known = {k: part for k, part in received.items() if k & (bit - 1) == 0 and k & ~(2 * bit - 1)}
        received.update({k | bit: swap(part, "ffn", bit) for k, part in known.items() if k | bit not in received})
    return [{**have, **received}[k] for k in range(lax.axis_size("ffn"))]


def even_rows(own):
    return [own] + [swap(own, "rows", k) for k in range(2, ways_of(), 2)]


def all_rows(even):
    return [part for piece in even for part in (piece, swap(piece, "rows", 1))]


def cross_rows(parts):
    return [swap(part, "rows", 2 * half + 2) for half, part in enumerate(parts)]


def place_kernel(ways, layer, entries, small, small_rows, planes, experts, given, meta, *refs):
    pieces, refs = refs[:ways], refs[ways + given :]
    plain, turned, turn, narrow, semaphores = refs[-5:]
    first_out, second_out, query_out, out_out, *more = refs[:-5]
    r = meta[0]
    rows = turn.shape[0] // ways
    copies = []

    def send(source, place):
        copies.append(pltpu.make_async_copy(source, place, semaphores.at[len(copies)]))
        copies[-1].start()

    for n in range(1 + len(entries)):
        for j, piece in enumerate(pieces):
            at = pl.ds(pl.multiple_of((r ^ j) * rows, rows), rows)
            base = 2 * rows * n
            halves = [piece[base : base + rows].astype(FULL), piece[base + rows : base + 2 * rows].astype(FULL)]
            plain[n, at, :] = halves[1 if n else 0]
            turn[at, :] = halves[0 if n else 1]
        turned[n] = turn[...].T
        if n:
            send(plain.at[n], out_out.at[entries[n - 1]])
            send(turned.at[n], query_out.at[entries[n - 1]])
        else:
            send(plain.at[0], first_out.at[layer])
            send(turned.at[0], second_out.at[layer])
    base = 2 * rows * (1 + len(entries))

    def collect(few):
        for j, piece in enumerate(pieces):
            at = pl.ds(pl.multiple_of((r ^ j) * few, few), few)
            turn[at, :] = piece[base : base + few].astype(FULL)

    for n, entry in enumerate(small):
        few = narrow.shape[2] // ways
        collect(few)
        base += few
        narrow[n] = turn[: narrow.shape[2]].T
        send(narrow.at[n], more[0].at[entry])
    if small_rows:
        collect(small_rows // ways)
        unpack(meta, turn, planes, experts, *more[1:])
    for copy in copies:
        copy.wait()


def body(
    source,
    target,
    cotangent,
    source_lengths,
    target_lengths,
    routes,
    norm_gain,
    norm_shift,
    moa_router,
    moa_query,
    moa_keyval,
    moa_out,
    ffn_in,
    ffn_in_bias,
    ffn_out,
    ffn_out_bias,
):
    groups, row_count, width = source.shape
    tokens = groups * row_count
    planes = lax.axis_size("ffn")
    ways = ways_of()
    experts = moa_router.shape[2]
    both = moa_keyval.shape[2]
    head = both // 2
    hidden = ffn_in.shape[2]
    slots_all = 2 * tokens
    meta = (source_lengths, target_lengths)
    flat = lambda values: values.reshape(tokens, width)
    source, target, cotangent = flat(source), flat(target), flat(cotangent)
    route_rows = jnp.swapaxes(routes, 2, 3).reshape(3, 1, slots_all)
    router_t = jnp.swapaxes(moa_router, 1, 2)
    norms = (norm_gain, norm_shift)

    rows_like = like((tokens, width), FULL)
    low_like = like((tokens, width), LOW)
    kv_like = like((tokens, both), LOW)
    sums_like = like((8, width), FULL)
    slot_like = [like((head, slots_all), LOW), like((1, slots_all), FULL)]

    last = []

    def run(body, out_shape, args, scratch=(), after=(), **more):
        after = tuple(after) + tuple(last)
        results = call(body, out_shape, args, scratch, after, **more)
        flat_results = jax.tree.leaves(results)
        last[:] = [min(flat_results, key=lambda array: array.size)]
        return results

    def hold(*arrays):
        held = lax.optimization_barrier((arrays, tuple(last)))[0]
        return held if len(arrays) > 1 else held[0]

    def mark(*arrays):
        last.extend(jax.tree.leaves(arrays))

    def relay(have):
        keys = [k for k in have if k]
        held = hold(*(have[k] for k in keys))
        mark(held)
        return other_planes(have, dict(zip(keys, held)))

    def sums(*outs):
        results = []
        for slots in outs:
            parts = []
            for slot in slots:
                parts.append(sum(entry_of(arg).astype(FULL) for arg in slot).astype(LOW))
            results.append(parts[0] if len(parts) == 1 else jnp.concatenate(parts))
        return results

    piece_rows = 2 * width // ways

    def cut(layer, after=()):
        return run(
            functools.partial(cut_kernel, ways, layer),
            like((piece_rows + 16, hidden), LOW),
            (ffn_in, ffn_out, ffn_in_bias),
            [pltpu.VMEM(ffn_in_bias.shape, LOW), pltpu.SemaphoreType.DMA((3,))],
            after,
            name="cut",
            whole=(0, 1, 2),
        )

    def join(parts):
        biases = jnp.stack([part[piece_rows] for part in parts])[:, None].astype(FULL)
        return jnp.stack([part[:piece_rows] for part in parts[1:]]), biases

    def prepare(j, row, value, after=()):
        return run(
            functools.partial(prepare_kernel, row),
            [low_like, kv_like],
            (value, *norms, (moa_keyval, j)),
            after=after,
            name="prepare",
        )

    def prepare_queries(j, row, value):
        kv, *slots = run(
            functools.partial(prepare_queries_kernel, groups, row),
            [kv_like] + slot_like,
            (value, *norms, (moa_keyval, j), (route_rows, j), (moa_query, j), (router_t, j)),
            name="prepare_queries",
        )
        return kv, slots

    def queries(j, h, after=()):
        return run(
            functools.partial(queries_kernel, groups),
            slot_like,
            (h, (route_rows, j), (moa_query, j), (router_t, j)),
            after=after,
            name="queries",
        )

    kept_like = [
        rows_like,
        like((1, slots_all), FULL),
        like((head, slots_all), FULL),
        like((experts * head, tokens), LOW),
    ]

    def attention(j, side, causal, resid, slots, kv_blocks, following, after=()):
        extra, more = (), []
        if following:
            extra = (*norms, (route_rows, 2), (moa_query, 2), (router_t, 2))
            more = slot_like
        return run(
            functools.partial(attend_kernel, groups, side, causal, planes, following),
            kept_like + more,
            (*meta, resid, *slots, (route_rows, j), *kv_blocks, (moa_out, j), *extra),
            after=after,
            smem=2,
            name="attend",
        )

    def attention_back(j, side, causal, upstream, slots, saved, kv_blocks, after=()):
        lse, att, mixed = saved
        return run(
            functools.partial(attend_back_kernel, groups, side, causal, planes, experts),
            [like((planes // 2, tokens, both), LOW)] * 2
            + [like((experts * head, tokens), LOW), like((experts, tokens), FULL)],
            (*meta, upstream, *slots, (route_rows, j), lse, att, *kv_blocks, (moa_out, j)),
            after=after,
            smem=2,
            name="attend_back",
        )

    def project_back(j, norm_row, finish, upstream, state, saved, rows, after=()):
        return run(
            functools.partial(project_back_kernel, ways, norm_row, finish),
            [rows_like]
            + [like((ways // 2, piece_rows, width), LOW)] * 2
            + [like((experts, width), FULL), sums_like],
            (upstream, state, *norms, saved[2], *rows, (moa_query, j), (router_t, j)),
            [pltpu.VMEM((width, width), FULL)],
            after=after,
            name="project_back",
        )

    keyval_like = [like((ways // 2, both // ways, width), LOW)] * 2
    keyval_scratch = [pltpu.VMEM((both, width), FULL)]

    def finish(j, norm_row, partial, upstream, state, blocks, pieces, after=()):
        return run(
            functools.partial(finish_kernel, len(blocks), ways, norm_row, pieces),
            [rows_like] + (keyval_like if pieces else [like((both, width), FULL)]) + [sums_like],
            (partial, upstream, state, *norms, (moa_keyval, j), *blocks),
            keyval_scratch if pieces else [],
            after=after,
            name="finish",
        )

    halves = range(ways // 2)
    near_planes = list(range(1, planes, 2))
    flat_pieces = lambda values: values.reshape(ways // 2, planes * piece_rows, hidden)
    by_plane = lambda values: values.reshape(planes, piece_rows, hidden)
    two = lambda values: values.reshape(planes // 2, -1, values.shape[-1])

    def pairs(*items):
        kept = hold(*(kept for kept, received in items), *(received for kept, received in items))
        kept, received = kept[: len(items)], kept[len(items) :]
        own, *parts = sums(*([[(k, h), (r, h)] for k, r in zip(kept, received)] for h in halves))
        mark(own, parts)
        return [own] + cross_rows(parts)

    def halve(items, bits):
        arrays = hold(*(array for item in items for array in item))
        parts = [arrays[n : n + 2] for n in range(0, len(arrays), 2)]
        count = parts[0][0].shape[0] // 2
        outs = []
        for at in (0, count):
            slots = [[[(k, n), (r, n)] for k, r in parts] for n in range(at, at + count)]
            rows_each = sum(k.shape[1] for k, r in parts)
            joined = [sums(slot)[0] for slot in slots]
            outs.append(jnp.concatenate(joined).reshape(count, rows_each, -1))
        mark(outs)
        return outs[0], swap(outs[1], "rows", bits)

    def feed_pairs(kept, received):
        return pairs((flat_pieces(kept), flat_pieces(received)))

    def feed_near(arrays):
        arrays = hold(*arrays) if len(arrays) > 1 else [hold(arrays[0])]
        arrays = [by_plane(values) for values in arrays]
        slot = lambda k: [(array, k) for array in arrays]
        near, kept = sums([slot(k) for k in near_planes], [slot(k - 1) for k in near_planes])
        mark(near, kept)
        return two(kept), two(swap(near, "ffn", 1))

    def planes_far(kept, near):
        kept, near = hold(kept, near)
        (far,) = sums([[(kept, k), (near, k)] for k in range(1, planes // 2)])
        mark(far)
        rows_each = kept.shape[1]
        return [(kept, 0), (near, 0)] + [
            swap(far[(k - 1) * rows_each : k * rows_each], "ffn", 2 * k) for k in range(1, planes // 2)
        ]

    def total(*slots):
        flat_slots = [arg for slot in slots for arg in slot]
        arrays = hold(*(arg[0] if isinstance(arg, tuple) else arg for arg in flat_slots))
        arrays = [
            (array, arg[1]) if isinstance(arg, tuple) else array
            for array, arg in zip(arrays, flat_slots)
        ]
        taken = []
        for slot in slots:
            taken.append(arrays[: len(slot)])
            arrays = arrays[len(slot) :]
        (result,) = sums(taken)
        mark(result)
        return result

    def over_more_rows(values):
        for bit in bits_of("rows", ways):
            values = total([values, swap(values, "rows", bit)])
        return values

    def join(have):
        parts = hold(*have)
        biases = jnp.stack([part[piece_rows] for part in parts])[:, None].astype(FULL)
        own = jnp.stack([part[:piece_rows] for part in parts[1:]])
        mark(own)
        return even_rows(own), biases

    def core(even):
        even = hold(*even)
        mark(even)
        return all_rows(even)

    weights_zero = first_planes(cut(0))
    h_source, kv_source = prepare(0, 0, source)
    kv_zero = first_planes(kv_source)
    weights_zero = relay(weights_zero)
    slots_zero = queries(0, h_source)
    kv_zero = relay(kv_zero)
    even_zero, bias_zero = join(weights_zero)
    mine_one = cut(1)
    weights_one = first_planes(mine_one)
    kv_target, slots_one = prepare_queries(1, 2, target)
    middle, *saved_zero = attention(0, 0, False, source, slots_zero, kv_zero, False)
    weights_one = relay(weights_one)
    kv_one = first_planes(hold(kv_target))
    pieces_zero = core(even_zero)
    even_one, bias_one = join(weights_one)
    weight_scratch = [pltpu.VMEM((planes, width, hidden), LOW), pltpu.VMEM((planes, hidden, width), LOW)]
    memory, memory_low, kv_memory = run(
        functools.partial(feed_forward_kernel, ways),
        [rows_like, low_like, kv_like],
        (middle, *norms, ffn_out_bias, bias_zero, (moa_keyval, 2))
        + ((ffn_in, 0), (ffn_out, 0), *pieces_zero),
        weight_scratch,
        name="encoder_feed",
    )
    kv_one = relay(kv_one)
    kv_two = first_planes(kv_memory)
    first_state, *saved_one, next_slots, next_gates = attention(
        1, 1, True, target, slots_one, kv_one, True
    )
    slots_two = (next_slots, next_gates)
    kv_two = relay(kv_two)
    pieces_one = core(even_one)
    second_state, *saved_two = attention(2, 0, False, first_state, slots_two, kv_two, False)

    back_scratch = weight_scratch + [pltpu.VMEM((width, hidden), FULL), pltpu.VMEM((tokens, width), FULL)]
    feed_like = [like((ways // 2, planes, piece_rows, hidden), LOW)] * 2
    feed_like += [like((planes, 1, hidden), FULL), sums_like]
    decoded, second_grad, one_kept, one_sent, bias_grad_one, sums_four = run(
        functools.partial(decoder_feed_kernel, ways, groups),
        [rows_like, rows_like] + feed_like,
        (*meta, second_state, cotangent, *norms, ffn_out_bias, bias_one)
        + ((ffn_in, 1), (ffn_out, 1), *pieces_one),
        back_scratch,
        smem=2,
        name="decoder_feed",
    )
    flat_one = flat_pieces(one_kept), flat_pieces(swap(one_sent, "rows", 1))
    d_kv_kept_two, d_kv_sent, *rows_two = attention_back(
        2, 0, False, second_grad, slots_two, saved_two, kv_two
    )
    d_kv_near_two = swap(d_kv_sent, "ffn", 1)
    one = halve([flat_one], 4)
    first_grad, kept_two, sent_two, router_two, sums_three = project_back(
        2, 3, True, second_grad, first_state, saved_two, rows_two
    )
    d_kv_two = planes_far(d_kv_kept_two, d_kv_near_two)
    d_kv_kept_one, d_kv_sent, *rows_one = attention_back(
        1, 1, True, first_grad, slots_one, saved_one, kv_one
    )
    d_kv_near_one = swap(d_kv_sent, "ffn", 1)
    self_grad, kept_one, sent_one, router_one, unused = project_back(
        1, 2, False, first_grad, target, saved_one, rows_one
    )
    later_sent = jnp.concatenate([sent_one, sent_two], 1)
    mark(later_sent)
    later_received = swap(later_sent, "rows", 1)
    one = halve([one], 2)
    (memory_grad, middle_grad, keyval_kept_two, keyval_sent_two, zero_kept, zero_sent, bias_grad_zero, sums_one) = run(
        functools.partial(encoder_feed_kernel, ways, len(d_kv_two)),
        [rows_like, rows_like] + keyval_like + feed_like,
        (middle, memory_low, *norms, bias_zero, (moa_keyval, 2), *d_kv_two)
        + ((ffn_in, 0), (ffn_out, 0), *pieces_zero),
        back_scratch + keyval_scratch,
        name="encoder_feed_back",
    )
    zero_received = swap(zero_sent, "rows", 1)
    d_kv_kept_zero, d_kv_sent, *rows_zero = attention_back(
        0, 0, False, middle_grad, slots_zero, saved_zero, kv_zero
    )
    d_kv_near_zero = swap(d_kv_sent, "ffn", 1)
    d_kv_one = planes_far(d_kv_kept_one, d_kv_near_one)
    zero = feed_pairs(zero_kept, zero_received)
    encoder_grad, kept_zero, sent_zero, router_zero, unused = project_back(
        0, 0, False, middle_grad, source, saved_zero, rows_zero
    )
    d_kv_zero = planes_far(d_kv_kept_zero, d_kv_near_zero)
    later = halve([(jnp.concatenate([kept_one, kept_two], 1), later_received)], 4)
    target_grad, keyval_kept_one, keyval_sent_one, sums_two = finish(
        1, 2, self_grad, first_grad, target, d_kv_one, True
    )
    small_rows = 40 + 16 + 3 * experts + 2 * planes
    small_rows = (small_rows + 127) // 128 * 128
    small_like = [like((ways // 2, small_rows // ways, width), LOW)] * 2
    (source_grad, keyval_kept_zero, keyval_sent_zero, small_kept, small_sent, sums_zero) = run(
        functools.partial(finish_pack_kernel, len(d_kv_zero), groups, ways, 0),
        [rows_like] + keyval_like + small_like + [sums_like],
        (*meta, encoder_grad, middle_grad, source, *norms, (moa_keyval, 0), *d_kv_zero)
        + (route_rows, sums_one, sums_two, sums_three, sums_four)
        + (router_zero, router_one, router_two, bias_grad_zero, bias_grad_one),
        keyval_scratch + [pltpu.VMEM((small_rows, width), FULL)],
        name="finish_pack",
        smem=2,
    )
    first_sent = jnp.concatenate(
        [sent_zero, keyval_sent_zero, keyval_sent_one, keyval_sent_two, small_sent], 1
    )
    first_kept = jnp.concatenate(
        [kept_zero, keyval_kept_zero, keyval_kept_one, keyval_kept_two, small_kept], 1
    )
    mark(first_sent)
    first_received = swap(first_sent, "rows", 1)
    zero_kept, zero_near = feed_near(zero)
    first_part = pairs((first_kept, first_received))
    later = halve([later], 2)
    one = total([(one[0], 0), (one[1], 0)])
    one_kept, one_near = feed_near([one])
    zero_parts = planes_far(zero_kept, zero_near)
    first_part = total(first_part)
    first_next = swap(first_part, "ffn", 1)
    later = total([(later[0], 0), (later[1], 0)])
    later_next = swap(later, "ffn", 1)
    one_parts = planes_far(one_kept, one_near)
    first_part = total([first_part, first_next])
    first_next = swap(first_part, "ffn", 2)
    later = total([later, later_next])
    later_next = swap(later, "ffn", 2)
    first_part = total(zero_parts, [first_part, first_next])
    first_even = even_rows(over_more_rows(first_part))
    later = total(one_parts, [later, later_next])
    later_even = even_rows(over_more_rows(later))
    first_pieces = core(first_even)
    grads_like = [like((2, width, hidden), FULL), like((2, hidden, width), FULL)]
    grads_like += [like((3, width, experts * head), FULL), like((3, experts * head, width), FULL)]
    grads_like += [like((3, width, both), FULL)]
    small_outs = [like((4, width), FULL), like((4, width), FULL), like((2, width), FULL)]
    small_outs += [like((3, experts, width), FULL), like((2, hidden), FULL), like((2, width), FULL)]
    small_outs += [like((3, experts), jnp.int32)]
    stay = pl.BlockSpec(memory_space=pl.ANY)
    lies = pl.BlockSpec(memory_space=pltpu.VMEM)

    def place(layer, entries, small, small_rows, pieces, given):
        count = 1 + len(entries)
        outs = grads_like + small_outs if small else grads_like[:4]
        return run(
            functools.partial(
                place_kernel, ways, layer, entries, small, small_rows, planes, experts, len(given)
            ),
            outs,
            (*pieces, *given),
            [pltpu.VMEM((count, width, width), FULL)] * 2
            + [pltpu.VMEM((width, width), FULL), pltpu.VMEM((3, width, both), FULL)]
            + [pltpu.SemaphoreType.DMA((2 * count + 3,))],
            name="place",
            whole=range(ways, ways + len(given)),
            alias={ways + n: n for n in range(len(given))},
            out_specs=[stay] * (5 if small else 4) + [lies] * (len(outs) - 5 if small else 0),
        )

    (first_grads, second_grads, query_grads, out_grads, keyval_grads, *smalls) = place(
        0, (0,), (0, 1, 2), small_rows, first_pieces, ()
    )
    gains, shifts, final, routers, bias_grads, out_biases, counts = smalls
    later_pieces = core(later_even)
    first_grads, second_grads, query_grads, out_grads = place(
        1, (1, 2), (), 0, later_pieces, (first_grads, second_grads, query_grads, out_grads)
    )
    whole = lambda values: values.reshape(groups, row_count, width)
    return (
        whole(memory),
        whole(decoded),
        whole(source_grad),
        whole(target_grad),
        whole(memory_grad),
        gains,
        shifts,
        final,
        jnp.swapaxes(routers, 1, 2),
        query_grads,
        keyval_grads,
        out_grads,
        first_grads,
        bias_grads,
        second_grads,
        out_biases,
        counts,
    )


def solution(mesh):
    in_specs = (
        P("rows", "ffn", None),
        P("rows", "ffn", None),
        P("rows", "ffn", None),
        P("rows"),
        P("rows"),
        P(None, "rows", "ffn", None),
        P(),
        P(),
        P(),
        P(),
        P(),
        P(),
        P(None, None, "ffn"),
        P(None, "ffn"),
        P(None, "ffn", None),
        P(),
    )
    out_specs = (
        P("rows", "ffn", None),
        P("rows", "ffn", None),
        P("rows", "ffn", None),
        P("rows", "ffn", None),
        P("rows", "ffn", None),
        P(),
        P(),
        P(),
        P(),
        P(),
        P(),
        P(),
        P(None, None, "ffn"),
        P(None, "ffn"),
        P(None, "ffn", None),
        P(),
        P(),
    )
    return jax.shard_map(body, mesh=mesh, in_specs=in_specs, out_specs=out_specs, check_vma=False)
```

```python
import functools
import jax
import jax.numpy as jnp
from jax import lax
from jax.experimental import pallas as pl
from jax.experimental.pallas import tpu as pltpu
from jax.sharding import PartitionSpec as P

EPS = 1e-05
LOW = jnp.bfloat16
FULL = jnp.float32
VMEM_BYTES = 22 * 1024 * 1024
CUT_BYTES = 62 * 1024 * 1024
MICRO = 1 << 29
COSTS = {"cut": 1, "prepare": 1.1, "queries": 1.1, "attend": 3, "encoder_feed": 6, "decoder_feed": 12}
COSTS.update({"attend_back": 4.3, "project_back": 2.8, "encoder_feed_back": 10, "finish": 2.7})
COSTS.update({"finish_pack": 3.5, "prepare_queries": 2, "place": 4})


class Meta:
    def __init__(self, *lengths):
        self.lengths = lengths

    def __getitem__(self, n):
        if n == 0:
            return lax.rem(lax.axis_index("rows"), ways_of())
        if n == 1:
            return lax.axis_index("ffn")
        groups = self.lengths[0].shape[0]
        return self.lengths[(n - 2) // groups][(n - 2) % groups]


def mm(left, right):
    return jnp.dot(left, right, preferred_element_type=FULL)


def mm_nt(left, right):
    return lax.dot_general(left, right, (((1,), (1,)), ((), ())), preferred_element_type=FULL)


def normalise(values):
    center = values - jnp.mean(values, -1, keepdims=True)
    inverse = lax.rsqrt(jnp.mean(center * center, -1, keepdims=True) + EPS)
    return center * inverse, inverse


def norm_back(upstream, normal, inverse, gain_row):
    scaled = upstream * gain_row
    return inverse * (
        scaled
        - jnp.mean(scaled, -1, keepdims=True)
        - normal * jnp.mean(scaled * normal, -1, keepdims=True)
    )


def split_low(values):
    high = values.astype(LOW)
    return high, (values - high.astype(FULL)).astype(LOW)


def gelu_parts(pre):
    c = 0.7978845608028654
    square = pre * pre
    t = jnp.tanh(c * pre * (1.0 + 0.044715 * square))
    half = 0.5 * (1.0 + t)
    act = pre * half
    slope = half + (0.5 * c) * pre * (1.0 - t * t) * (1.0 + 0.134145 * square)
    return act, slope


def call(body, out_shape, args, scratch=(), after=(), name=None, whole=(), alias=None, out_specs=None, smem=0, memory=VMEM_BYTES):
    arrays, specs = [], []
    for n, arg in enumerate(args):
        if isinstance(arg, tuple):
            array, entry = arg
            rest = array.shape[1:]
            specs.append(
                pl.BlockSpec(
                    (None,) + rest,
                    lambda step, entry=entry, rest=rest: (entry,) + (0,) * len(rest),
                    pipeline_mode=pl.Buffered(1),
                )
            )
        else:
            array = arg
            space = pltpu.SMEM if n < smem else pltpu.HBM if n in whole else pltpu.VMEM
            specs.append(pl.BlockSpec(memory_space=space))
        arrays.append(array)
    taken, skipped = len(arrays), len(after)

    def run(*refs):
        body(Meta(*refs[:smem]), *refs[smem:taken], *refs[taken + skipped :])

    return pl.pallas_call(
        run,
        grid=(1,),
        out_shape=out_shape,
        in_specs=specs + [pl.BlockSpec(memory_space=pl.ANY)] * skipped,
        out_specs=out_specs
        or jax.tree.map(lambda _: pl.BlockSpec(memory_space=pltpu.VMEM), out_shape),
        scratch_shapes=list(scratch),
        input_output_aliases=alias or {},
        compiler_params=pltpu.CompilerParams(vmem_limit_bytes=memory),
        cost_estimate=pl.CostEstimate(
            flops=int(COSTS[name] * MICRO), bytes_accessed=1 << 16, transcendentals=0
        ),
        name=name,
    )(*arrays, *after)


def like(shape, dtype):
    return jax.ShapeDtypeStruct(shape, dtype)


def prepare_kernel(row, meta, value, gain, shift, keyval, h_out, kv_out):
    normal, _ = normalise(value[...].astype(FULL))
    h = (normal * gain[row : row + 1] + shift[row : row + 1]).astype(LOW)
    h_out[...] = h
    kv_out[...] = mm(h, keyval[...]).astype(LOW)


def cut_kernel(ways, layer, meta, first, second, bias, mine, biases, semaphores):
    rows = first.shape[1] // ways
    at = pl.ds(pl.multiple_of(meta[0] * rows, rows), rows)
    copies = [
        pltpu.make_async_copy(weight.at[layer, at, :], mine.at[pl.ds(n * rows, rows), :], semaphores.at[n])
        for n, weight in enumerate((first, second))
    ]
    copies.append(pltpu.make_async_copy(bias, biases, semaphores.at[2]))
    for copy in copies:
        copy.start()
    for copy in copies:
        copy.wait()
    mine[2 * rows :] = jnp.broadcast_to(biases[layer : layer + 1, :], (16, biases.shape[1]))


def to_slots(values, groups):
    part = values.shape[1] // groups
    blocks = []
    for g in range(groups):
        block = values[:, g * part : (g + 1) * part]
        blocks += [block, block]
    return jnp.concatenate(blocks, 1)


def slot_queries(h, route, query_proj, router_t, groups, slot_out, gate_out):
    experts = router_t.shape[0]
    queries = mm(h, query_proj).astype(LOW)
    spread = to_slots(queries.T, groups)
    head = spread.shape[0] // experts
    chosen = jnp.zeros((head, spread.shape[1]), LOW)
    for e in range(experts):
        chosen = jnp.where(route == e, spread[e * head : (e + 1) * head], chosen)
    slot_out[...] = chosen * jnp.asarray(float(head) ** -0.5, LOW)
    logits = to_slots(mm_nt(router_t, h), groups)
    ids = lax.broadcasted_iota(jnp.int32, logits.shape, 0)
    picked = jnp.sum(jnp.where(ids == route, logits, 0.0), 0, keepdims=True)
    part = picked.shape[1] // (2 * groups)
    gates = []
    for g in range(groups):
        a = picked[:, 2 * g * part : (2 * g + 1) * part]
        b = picked[:, (2 * g + 1) * part : (2 * g + 2) * part]
        top = jnp.maximum(a, b)
        ea, eb = jnp.exp(a - top), jnp.exp(b - top)
        total = ea + eb
        gates += [ea / total, eb / total]
    gate_out[...] = jnp.concatenate(gates, 1)


def allowed_keys(shape, z, part, planes, length, causal):
    blocks = []
    for k in range(planes):
        position = (z ^ k) * part + lax.broadcasted_iota(jnp.int32, (part, shape[1]), 0)
        ok = position < length
        if causal:
            lane = lax.broadcasted_iota(jnp.int32, (part, shape[1]), 1)
            query = z * part + jnp.where(lane >= part, lane - part, lane)
            ok = ok & (position <= query)
        blocks.append(ok)
    return jnp.concatenate(blocks, 0)


def attend(meta, side, causal, slots, gates, route, kv_refs, out_proj, groups, experts, lse_out, att_out):
    z = meta[1]
    part = kv_refs[0].shape[0] // groups
    planes = len(kv_refs)
    head = slots.shape[0]
    lanes = 2 * part
    columns = []
    for g in range(groups):
        kv = jnp.concatenate([ref[g * part : (g + 1) * part, :] for ref in kv_refs], 0)
        q = slots[:, g * lanes : (g + 1) * lanes]
        padded = jnp.concatenate([q, jnp.zeros_like(q)], 0)
        scores = mm(kv, padded)
        ok = allowed_keys(scores.shape, z, part, planes, meta[2 + 2 * side + g], causal)
        scores = jnp.where(ok, scores, -1e30)
        top = jnp.max(scores, 0, keepdims=True)
        raised = jnp.exp(scores - top)
        total = jnp.sum(raised, 0, keepdims=True)
        lse_out[:, g * lanes : (g + 1) * lanes] = top + jnp.log(total)
        low = (raised * (1.0 / total)).astype(LOW)
        attended = mm(kv.T, low)[head:]
        att_out[:, g * lanes : (g + 1) * lanes] = attended
        gated = attended * gates[:, g * lanes : (g + 1) * lanes]
        ids = route[:, g * lanes : (g + 1) * lanes]
        rows = []
        for e in range(experts):
            first = jnp.where(ids[:, :part] == e, gated[:, :part], 0.0)
            rows.append(jnp.where(ids[:, part:] == e, gated[:, part:], first).astype(LOW))
        columns.append(jnp.concatenate(rows, 0))
    mixed = jnp.concatenate(columns, 1)
    return mixed, mm(mixed.T, out_proj)


def prepare_queries_kernel(groups, row, meta, value, gain, shift, keyval, route, query_proj, router_t, kv_out, slot_out, gate_out):
    normal, _ = normalise(value[...].astype(FULL))
    h = (normal * gain[row : row + 1] + shift[row : row + 1]).astype(LOW)
    kv_out[...] = mm(h, keyval[...]).astype(LOW)
    slot_queries(h, route[...], query_proj[...], router_t[...], groups, slot_out, gate_out)


def queries_kernel(groups, meta, h, route, query_proj, router_t, slot_out, gate_out):
    slot_queries(h[...], route[...], query_proj[...], router_t[...], groups, slot_out, gate_out)


def attend_kernel(groups, side, causal, planes, next_queries, meta, resid, slots, gates, route, *rest):
    kv_refs, rest = rest[:planes], rest[planes:]
    out_proj, rest = rest[0], rest[1:]
    if next_queries:
        (gain, shift, next_route, next_proj, next_router, new_resid, lse_out, att_out, mixed_out, next_slots, next_gates) = rest
    else:
        (new_resid, lse_out, att_out, mixed_out) = rest
    experts = out_proj.shape[0] // slots.shape[0]
    mixed, branch = attend(meta, side, causal, slots, gates, route, kv_refs, out_proj[...], groups, experts, lse_out, att_out)
    mixed_out[...] = mixed
    total = resid[...].astype(FULL) + branch
    new_resid[...] = total
    if next_queries:
        normal, _ = normalise(total)
        h = (normal * gain[3:4] + shift[3:4]).astype(LOW)
        slot_queries(h, next_route[...], next_proj[...], next_router[...], groups, next_slots, next_gates)


def place_weights(meta, own_first, own_second, pieces, first, second):
    r = meta[0]
    first[0] = own_first[...]
    second[0] = own_second[...]
    ways = len(pieces)
    rows = own_first.shape[0] // ways
    for j, piece in enumerate(pieces):
        at = pl.ds(pl.multiple_of((r ^ j) * rows, rows), rows)
        for k in range(1, first.shape[0]):
            first[k, at, :] = piece[k - 1, :rows]
            second[k, at, :] = piece[k - 1, rows:]


def feed_forward_kernel(ways, meta, state, gain, shift, out_bias, bias, keyval, own_first, own_second, *rest):
    pieces, (memory, low_out, kv_out, first, second) = rest[:ways], rest[ways:]
    place_weights(meta, own_first, own_second, pieces, first, second)
    value = state[...]
    normal, _ = normalise(value)
    h = (normal * gain[1:2] + shift[1:2]).astype(LOW)
    memory[...] = value + out_bias[0:1].astype(FULL)

    def step(k, carry):
        pre = mm(h, first[k]) + bias[k]
        act = jax.nn.gelu(pre).astype(LOW)
        memory[...] += mm(act, second[k])
        return carry

    lax.fori_loop(0, first.shape[0], step, 0)
    low = memory[...].astype(LOW)
    low_out[...] = low
    kv_out[...] = mm(low, keyval[...]).astype(LOW)


def feed_backward_core(meta, h, upstream_low, ways, bias, first, second, grad, d_h, kept, sent, bias_grad, state):
    r, z = meta[0], meta[1]
    h_t = h.T
    up_t = upstream_low.T
    d_h[...] = jnp.zeros_like(d_h)
    rows = h.shape[1] // ways

    def step(k, carry):
        w_first, w_second = first[k], second[k]
        pre = mm(h, w_first) + bias[k]
        act, slope = gelu_parts(pre)
        act = act.astype(LOW)
        if state is not None:
            state[...] += mm(act, w_second)
        d_pre_full = (mm_nt(upstream_low, w_second) * slope).astype(LOW)
        d_h[...] += mm_nt(d_pre_full, w_first)
        bias_grad[z ^ k] = jnp.sum(d_pre_full.astype(FULL), 0, keepdims=True)
        for half, product in enumerate((mm(h_t, d_pre_full), mm(up_t, act))):
            grad[...] = product
            for j in range(ways):
                block = grad[pl.ds(pl.multiple_of((r ^ j) * rows, rows), rows), :].astype(LOW)
                target = sent if j & 1 else kept
                target[j // 2, k, half * rows : (half + 1) * rows, :] = block
        return carry

    lax.fori_loop(0, first.shape[0], step, 0)


def decoder_feed_kernel(ways, groups, meta, state_in, cotangent, gain, shift, out_bias, bias, own_first, own_second, *rest):
    pieces, (decoded, state_grad, kept, sent, bias_grad, sums, first, second, grad, d_h) = rest[:ways], rest[ways:]
    place_weights(meta, own_first, own_second, pieces, first, second)
    value = state_in[...]
    normal, inverse = normalise(value)
    h = (normal * gain[4:5] + shift[4:5]).astype(LOW)
    decoded[...] = value + out_bias[1:2].astype(FULL)
    part = value.shape[0] // groups
    seeds = []
    for g in range(groups):
        row = meta[1] * part + lax.broadcasted_iota(jnp.int32, (part, value.shape[1]), 0)
        seeds.append(jnp.where(row < meta[4 + g], cotangent[g * part : (g + 1) * part, :].astype(FULL), 0.0))
    seed = jnp.concatenate(seeds, 0)
    feed_backward_core(meta, h, seed.astype(LOW), ways, bias, first, second, grad, d_h, kept, sent, bias_grad, decoded)
    normal, inverse = normalise(state_in[...])
    upstream = d_h[...]
    state_grad[...] = seed + norm_back(upstream, normal, inverse, gain[4:5])
    sums[0:1] = jnp.sum(upstream * normal, 0, keepdims=True)
    sums[1:2] = jnp.sum(upstream, 0, keepdims=True)
    sums[2:3] = jnp.sum(seed, 0, keepdims=True)
    sums[3:8] = jnp.zeros((5, sums.shape[1]), FULL)


def total_of(blocks):
    total = blocks[0][...].astype(FULL)
    for block in blocks[1:]:
        total = total + block[...].astype(FULL)
    return total.astype(LOW)


def write_pieces(meta, ways, values, scratch, kept, sent):
    scratch[...] = values
    rows = values.shape[0] // ways
    for j in range(ways):
        at = pl.ds(pl.multiple_of((meta[0] ^ j) * rows, rows), rows)
        place = sent if j & 1 else kept
        place[j // 2] = scratch[at, :].astype(LOW)


def encoder_feed_kernel(ways, planes, meta, state_in, memory_low, gain, shift, bias, keyval, *rest):
    blocks, rest = rest[:planes], rest[planes:]
    own_first, own_second = rest[:2]
    pieces, rest = rest[2 : 2 + ways], rest[2 + ways :]
    (memory_grad, state_grad, keyval_kept, keyval_sent, kept, sent, bias_grad, sums, first, second, grad, d_h, keyval_grad) = rest
    place_weights(meta, own_first, own_second, pieces, first, second)
    d_kv = total_of(blocks)
    upstream_in = mm_nt(d_kv, keyval[...])
    memory_grad[...] = upstream_in
    write_pieces(meta, ways, mm(d_kv.T, memory_low[...]), keyval_grad, keyval_kept, keyval_sent)
    normal, inverse = normalise(state_in[...])
    h = (normal * gain[1:2] + shift[1:2]).astype(LOW)
    feed_backward_core(meta, h, upstream_in.astype(LOW), ways, bias, first, second, grad, d_h, kept, sent, bias_grad, None)
    normal, inverse = normalise(state_in[...])
    upstream = d_h[...]
    state_grad[...] = memory_grad[...] + norm_back(upstream, normal, inverse, gain[1:2])
    sums[0:1] = jnp.sum(upstream * normal, 0, keepdims=True)
    sums[1:2] = jnp.sum(upstream, 0, keepdims=True)
    sums[2:3] = jnp.sum(memory_grad[...], 0, keepdims=True)
    sums[3:8] = jnp.zeros((5, sums.shape[1]), FULL)


def attend_back_kernel(groups, side, causal, planes, experts, meta, upstream, slots, gates, route, lse, att, *rest):
    kv_refs, rest = rest[:planes], rest[planes:]
    out_proj, d_kv_kept, d_kv_sent, query_rows_out, logit_out = rest
    z = meta[1]
    head = slots.shape[0]
    branch_grad = upstream[...].astype(LOW)
    part = branch_grad.shape[0] // groups
    lanes = 2 * part
    d_mixed = mm_nt(out_proj[...], branch_grad)
    query_columns, logit_columns = [], []
    for g in range(groups):
        here = slice(g * lanes, (g + 1) * lanes)
        ids = route[:, here]
        gate = gates[:, here]
        attended = att[:, here]
        mine = d_mixed[:, g * part : (g + 1) * part]
        spread = jnp.concatenate([mine, mine], 1)
        slot_grad = jnp.zeros((head, lanes), FULL)
        for e in range(experts):
            slot_grad = jnp.where(ids == e, spread[e * head : (e + 1) * head], slot_grad)
        gate_grad = jnp.sum(attended * slot_grad, 0, keepdims=True)
        weighted = gate * gate_grad
        both = weighted[:, :part] + weighted[:, part:]
        chosen_grad = gate * (gate_grad - jnp.concatenate([both, both], 1))
        att_grad = (gate * slot_grad).astype(LOW)
        inner = jnp.sum(att_grad.astype(FULL) * attended, 0, keepdims=True)
        q = slots[:, here]
        zeros = jnp.zeros_like(q)
        kv = jnp.concatenate([ref[g * part : (g + 1) * part, :] for ref in kv_refs], 0)
        scores = mm(kv, jnp.concatenate([q, zeros], 0))
        ok = allowed_keys(scores.shape, z, part, planes, meta[2 + 2 * side + g], causal)
        probs = jnp.exp(jnp.where(ok, scores, -1e30) - lse[:, here])
        probs_grad = mm(kv, jnp.concatenate([zeros, att_grad], 0))
        score_grad = (probs * (probs_grad - inner)).astype(LOW)
        d_kv = mm(score_grad, jnp.concatenate([q, zeros], 0).T) + mm(
            probs.astype(LOW), jnp.concatenate([zeros, att_grad], 0).T
        )
        for k in range(planes):
            place = d_kv_sent if k & 1 else d_kv_kept
            place[k // 2, g * part : (g + 1) * part, :] = d_kv[k * part : (k + 1) * part].astype(LOW)
        slot_query_grad = mm(kv.T, score_grad)[:head] * (float(head) ** -0.5)
        rows = []
        for e in range(experts):
            first = jnp.where(ids[:, :part] == e, slot_query_grad[:, :part], 0.0)
            rows.append(jnp.where(ids[:, part:] == e, slot_query_grad[:, part:], first).astype(LOW))
        query_columns.append(jnp.concatenate(rows, 0))
        expert = lax.broadcasted_iota(jnp.int32, (experts, part), 0)
        first = jnp.where(ids[:, :part] == expert, chosen_grad[:, :part], 0.0)
        logit_columns.append(jnp.where(ids[:, part:] == expert, chosen_grad[:, part:], first))
    query_rows_out[...] = jnp.concatenate(query_columns, 1)
    logit_out[...] = jnp.concatenate(logit_columns, 1)


def project_back_kernel(ways, norm_row, finish, meta, upstream, state, gain, shift, mixed, query_rows, logit_grad, query_proj, router, result, kept, sent, router_grad, sums, grad):
    normal, inverse = normalise(state[...].astype(FULL))
    h = (normal * gain[norm_row : norm_row + 1] + shift[norm_row : norm_row + 1]).astype(LOW)
    query_grad_rows = query_rows[...]
    high, low = split_low(logit_grad[...])
    router_grad[...] = mm(high, h) + mm(low, h)
    d_h = mm_nt(query_grad_rows.T, query_proj[...])
    d_h = d_h + mm(high.T, router[...]) + mm(low.T, router[...])
    rows_each = grad.shape[0] // ways
    for half in range(2):
        if half == 0:
            grad[...] = mm(query_grad_rows, h)
        else:
            grad[...] = mm(mixed[...], upstream[...].astype(LOW))
        for j in range(ways):
            at = pl.ds(pl.multiple_of((meta[0] ^ j) * rows_each, rows_each), rows_each)
            place = sent if j & 1 else kept
            place[j // 2, half * rows_each : (half + 1) * rows_each, :] = grad[at, :].astype(LOW)
    if finish:
        result[...] = upstream[...] + norm_back(d_h, normal, inverse, gain[norm_row : norm_row + 1])
        sums[0:1] = jnp.sum(d_h * normal, 0, keepdims=True)
        sums[1:2] = jnp.sum(d_h, 0, keepdims=True)
        sums[2:8] = jnp.zeros((6, sums.shape[1]), FULL)
    else:
        result[...] = d_h
        sums[...] = jnp.zeros_like(sums)


def finish_kernel(planes, ways, norm_row, pieces, meta, partial, upstream, state, gain, shift, keyval, *rest):
    blocks, rest = rest[:planes], rest[planes:]
    d_kv = total_of(blocks)
    normal, inverse = normalise(state[...].astype(FULL))
    h = (normal * gain[norm_row : norm_row + 1] + shift[norm_row : norm_row + 1]).astype(LOW)
    keyval_grad = mm(d_kv.T, h)
    if pieces:
        result, keyval_kept, keyval_sent, sums, scratch = rest
        write_pieces(meta, ways, keyval_grad, scratch, keyval_kept, keyval_sent)
    else:
        result, keyval_out, sums = rest
        keyval_out[...] = keyval_grad
    d_h = partial[...] + mm_nt(d_kv, keyval[...])
    result[...] = upstream[...] + norm_back(d_h, normal, inverse, gain[norm_row : norm_row + 1])
    sums[0:1] = jnp.sum(d_h * normal, 0, keepdims=True)
    sums[1:2] = jnp.sum(d_h, 0, keepdims=True)
    sums[2:8] = jnp.zeros((6, sums.shape[1]), FULL)


def finish_pack_kernel(planes, groups, ways, norm_row, meta, partial, upstream, state, gain, shift, keyval, *rest):
    blocks, rest = rest[:planes], rest[planes:]
    (routes, sums_one, sums_two, sums_three, sums_four, router_zero, router_one, router_two, bias_zero, bias_one) = rest[:10]
    result, keyval_kept, keyval_sent, small_kept, small_sent, sums, keyval_scratch, out = rest[10:]
    finish_kernel(planes, ways, norm_row, True, meta, partial, upstream, state, gain, shift, keyval, *blocks, result, keyval_kept, keyval_sent, sums, keyval_scratch)
    experts = router_zero.shape[0]
    count = bias_zero.shape[0]
    width = out.shape[1]
    slots_all = routes.shape[2]
    part = slots_all // (2 * groups)
    for n, ref in enumerate((sums, sums_one, sums_two, sums_three, sums_four)):
        out[8 * n : 8 * n + 8] = ref[...]
    at = 40
    expert = lax.broadcasted_iota(jnp.int32, (experts, slots_all), 0)
    lane = lax.broadcasted_iota(jnp.int32, (experts, slots_all), 1)
    position = meta[1] * part + lane % part
    hits = []
    for j in range(3):
        inside = jnp.zeros((experts, slots_all), jnp.bool_)
        for g in range(groups):
            mine = (lane // (2 * part)) == g
            inside = inside | (mine & (position < meta[2 + g + (groups if j else 0)]))
        hits.append(jnp.where((routes[j] == expert) & inside, 1.0, 0.0))
    hits.append(jnp.zeros((128 - 3 * experts, slots_all), FULL))
    hits = jnp.concatenate(hits, 0).astype(LOW)
    counts = mm_nt(jnp.ones((16, slots_all), LOW), hits).astype(jnp.int32)
    bit = lax.broadcasted_iota(jnp.int32, counts.shape, 0)
    digits = (lax.shift_right_logical(counts, bit) & 1).astype(FULL)
    out[at : at + 16, 128:] = jnp.zeros((16, width - 128), FULL)
    out[at : at + 16, :128] = digits
    at += 16
    rows = [router_zero[...], router_one[...], router_two[...]]
    rows += [bias_zero[k] for k in range(count)] + [bias_one[k] for k in range(count)]
    rows = jnp.concatenate(rows, 0)
    out[at : at + rows.shape[0]] = rows
    at += rows.shape[0]
    out[at:] = jnp.zeros((out.shape[0] - at, width), FULL)
    write_pieces(meta, ways, out[...], out, small_kept, small_sent)


def unpack(meta, total, planes, experts, gain_out, shift_out, final_out, router_out, bias_out, out_bias_out, counts_out):
    sums = [total[8 * n : 8 * n + 8] for n in range(5)]
    gain_out[...] = jnp.concatenate([sums[n][0:1] for n in range(4)], 0)
    shift_out[...] = jnp.concatenate([sums[n][1:2] for n in range(4)], 0)
    final_out[...] = sums[4][0:2]
    out_bias_out[...] = jnp.concatenate([sums[1][2:3], sums[4][2:3]], 0)
    at = 40
    digits = total[at : at + 16, :128]
    weight = lax.shift_left(jnp.int32(1), lax.broadcasted_iota(jnp.int32, digits.shape, 0))
    value = jnp.sum(digits * weight.astype(FULL), 0, keepdims=True).astype(jnp.int32)
    for j in range(3):
        counts_out[j : j + 1, :] = value[:, j * experts : (j + 1) * experts]
    at += 16
    for j in range(3):
        router_out[j] = total[at + j * experts : at + (j + 1) * experts]
    at += 3 * experts
    for layer in range(2):
        bias_out[layer : layer + 1, :] = total[pl.ds(at + layer * planes + meta[1], 1), :]


def swap(values, axis_name, bits):
    size = lax.axis_size(axis_name)
    return lax.ppermute(values, axis_name, [(i, i ^ bits) for i in range(size)])


def ways_of():
    return min(lax.axis_size("rows"), 8)


def bits_of(axis_name, first=1):
    bits, bit = [], first
    while bit < lax.axis_size(axis_name):
        bits.append(bit)
        bit *= 2
    return bits


def entry_of(item):
    return item[0][item[1]] if isinstance(item, tuple) else item


def first_planes(values):
    have = {0: values}
    have.update({bit: swap(values, "ffn", bit) for bit in bits_of("ffn")[::-1]})
    return have


def other_planes(have, received):
    for bit in bits_of("ffn")[::-1]:
        known = {k: part for k, part in received.items() if k & (bit - 1) == 0 and k & ~(2 * bit - 1)}
        received.update({k | bit: swap(part, "ffn", bit) for k, part in known.items() if k | bit not in received})
    return [{**have, **received}[k] for k in range(lax.axis_size("ffn"))]


def even_rows(own):
    return [own] + [swap(own, "rows", k) for k in range(2, ways_of(), 2)]


def all_rows(even):
    return [part for piece in even for part in (piece, swap(piece, "rows", 1))]


def doubled_rows(values, bits):
    return jnp.concatenate([values, swap(values, "rows", bits)])


def cross_rows(parts):
    return [swap(part, "rows", 2 * half + 2) for half, part in enumerate(parts)]


class Joined:
    def __init__(self, upper, lower):
        self.upper, self.lower = upper, lower

    def __getitem__(self, rows):
        count = self.upper.shape[0]
        if rows.stop <= count:
            return self.upper[rows]
        if rows.start >= count:
            return self.lower[rows.start - count : rows.stop - count]
        return jnp.concatenate([self.upper[rows.start :], self.lower[: rows.stop - count]])


def place_kernel(ways, small, small_rows, planes, experts, meta, *refs):
    halves_of, refs = refs[: 2 * ways], refs[2 * ways :]
    pieces = [Joined(*halves_of[2 * j : 2 * j + 2]) for j in range(ways)]
    plain, turned, turn, narrow, semaphores = refs[-5:]
    first_out, second_out, query_out, out_out, keyval_out, *more = refs[:-5]
    r = meta[0]
    rows = turn.shape[0] // ways
    copies = []
    base = 0

    def send(source, place):
        copies.append(pltpu.make_async_copy(source, place, semaphores.at[len(copies)]))
        copies[-1].start()

    def collect(few):
        nonlocal base
        for j, piece in enumerate(pieces):
            at = pl.ds(pl.multiple_of((r ^ j) * few, few), few)
            turn[at, :] = piece[base : base + few].astype(FULL)
        base += few

    def pair(n, flip, plain_out, turned_out):
        nonlocal base
        for j, piece in enumerate(pieces):
            at = pl.ds(pl.multiple_of((r ^ j) * rows, rows), rows)
            halves = [piece[base : base + rows].astype(FULL), piece[base + rows : base + 2 * rows].astype(FULL)]
            plain[n, at, :] = halves[1 if flip else 0]
            turn[at, :] = halves[0 if flip else 1]
        base += 2 * rows
        turned[n] = turn[...].T
        send(plain.at[n], plain_out)
        send(turned.at[n], turned_out)

    pair(0, False, first_out.at[0], second_out.at[0])
    pair(1, True, out_out.at[0], query_out.at[0])
    for n, entry in enumerate(small):
        collect(narrow.shape[2] // ways)
        narrow[n] = turn[: narrow.shape[2]].T
        send(narrow.at[n], keyval_out.at[entry])
    collect(small_rows // ways)
    unpack(meta, turn, planes, experts, *more)
    pair(2, False, first_out.at[1], second_out.at[1])
    for entry in (1, 2):
        pair(2 + entry, True, out_out.at[entry], query_out.at[entry])
    for copy in copies:
        copy.wait()


def body(
    source,
    target,
    cotangent,
    source_lengths,
    target_lengths,
    routes,
    norm_gain,
    norm_shift,
    moa_router,
    moa_query,
    moa_keyval,
    moa_out,
    ffn_in,
    ffn_in_bias,
    ffn_out,
    ffn_out_bias,
):
    groups, row_count, width = source.shape
    tokens = groups * row_count
    planes = lax.axis_size("ffn")
    ways = ways_of()
    experts = moa_router.shape[2]
    both = moa_keyval.shape[2]
    head = both // 2
    hidden = ffn_in.shape[2]
    slots_all = 2 * tokens
    meta = (source_lengths, target_lengths)
    flat = lambda values: values.reshape(tokens, width)
    source, target, cotangent = flat(source), flat(target), flat(cotangent)
    route_rows = jnp.swapaxes(routes, 2, 3).reshape(3, 1, slots_all)
    router_t = jnp.swapaxes(moa_router, 1, 2)
    norms = (norm_gain, norm_shift)

    rows_like = like((tokens, width), FULL)
    low_like = like((tokens, width), LOW)
    kv_like = like((tokens, both), LOW)
    sums_like = like((8, width), FULL)
    slot_like = [like((head, slots_all), LOW), like((1, slots_all), FULL)]

    last = []

    def run(body, out_shape, args, scratch=(), after=(), **more):
        after = tuple(after) + tuple(last)
        results = call(body, out_shape, args, scratch, after, **more)
        flat_results = jax.tree.leaves(results)
        last[:] = [min(flat_results, key=lambda array: array.size)]
        return results

    def hold(*arrays):
        held = lax.optimization_barrier((arrays, tuple(last)))[0]
        return held if len(arrays) > 1 else held[0]

    def mark(*arrays):
        last.extend(jax.tree.leaves(arrays))

    def relay(have):
        keys = [k for k in have if k]
        held = hold(*(have[k] for k in keys))
        mark(held)
        return other_planes(have, dict(zip(keys, held)))

    def sums(*outs):
        results = []
        for slots in outs:
            parts = []
            for slot in slots:
                parts.append(sum(entry_of(arg).astype(FULL) for arg in slot).astype(LOW))
            results.append(parts[0] if len(parts) == 1 else jnp.concatenate(parts))
        return results

    piece_rows = 2 * width // ways

    def cut(layer, after=()):
        return run(
            functools.partial(cut_kernel, ways, layer),
            like((piece_rows + 16, hidden), LOW),
            (ffn_in, ffn_out, ffn_in_bias),
            [pltpu.VMEM(ffn_in_bias.shape, LOW), pltpu.SemaphoreType.DMA((3,))],
            after,
            name="cut",
            whole=(0, 1, 2),
            memory=CUT_BYTES if layer == 0 else VMEM_BYTES,
        )

    def join(parts):
        biases = jnp.stack([part[piece_rows] for part in parts])[:, None].astype(FULL)
        return jnp.stack([part[:piece_rows] for part in parts[1:]]), biases

    def prepare(j, row, value, after=()):
        return run(
            functools.partial(prepare_kernel, row),
            [low_like, kv_like],
            (value, *norms, (moa_keyval, j)),
            after=after,
            name="prepare",
        )

    def prepare_queries(j, row, value):
        kv, *slots = run(
            functools.partial(prepare_queries_kernel, groups, row),
            [kv_like] + slot_like,
            (value, *norms, (moa_keyval, j), (route_rows, j), (moa_query, j), (router_t, j)),
            name="prepare_queries",
        )
        return kv, slots

    def queries(j, h, after=()):
        return run(
            functools.partial(queries_kernel, groups),
            slot_like,
            (h, (route_rows, j), (moa_query, j), (router_t, j)),
            after=after,
            name="queries",
        )

    kept_like = [
        rows_like,
        like((1, slots_all), FULL),
        like((head, slots_all), FULL),
        like((experts * head, tokens), LOW),
    ]

    def attention(j, side, causal, resid, slots, kv_blocks, following, after=()):
        extra, more = (), []
        if following:
            extra = (*norms, (route_rows, 2), (moa_query, 2), (router_t, 2))
            more = slot_like
        return run(
            functools.partial(attend_kernel, groups, side, causal, planes, following),
            kept_like + more,
            (*meta, resid, *slots, (route_rows, j), *kv_blocks, (moa_out, j), *extra),
            after=after,
            smem=2,
            name="attend",
        )

    def attention_back(j, side, causal, upstream, slots, saved, kv_blocks, after=()):
        lse, att, mixed = saved
        return run(
            functools.partial(attend_back_kernel, groups, side, causal, planes, experts),
            [like((planes // 2, tokens, both), LOW)] * 2
            + [like((experts * head, tokens), LOW), like((experts, tokens), FULL)],
            (*meta, upstream, *slots, (route_rows, j), lse, att, *kv_blocks, (moa_out, j)),
            after=after,
            smem=2,
            name="attend_back",
        )

    def project_back(j, norm_row, finish, upstream, state, saved, rows, after=()):
        return run(
            functools.partial(project_back_kernel, ways, norm_row, finish),
            [rows_like]
            + [like((ways // 2, piece_rows, width), LOW)] * 2
            + [like((experts, width), FULL), sums_like],
            (upstream, state, *norms, saved[2], *rows, (moa_query, j), (router_t, j)),
            [pltpu.VMEM((width, width), FULL)],
            after=after,
            name="project_back",
        )

    keyval_like = [like((ways // 2, both // ways, width), LOW)] * 2
    keyval_scratch = [pltpu.VMEM((both, width), FULL)]

    def finish(j, norm_row, partial, upstream, state, blocks, pieces, after=()):
        return run(
            functools.partial(finish_kernel, len(blocks), ways, norm_row, pieces),
            [rows_like] + (keyval_like if pieces else [like((both, width), FULL)]) + [sums_like],
            (partial, upstream, state, *norms, (moa_keyval, j), *blocks),
            keyval_scratch if pieces else [],
            after=after,
            name="finish",
        )

    halves = range(ways // 2)
    near_planes = list(range(1, planes, 2))
    flat_pieces = lambda values: values.reshape(ways // 2, planes * piece_rows, hidden)
    by_plane = lambda values: values.reshape(planes, piece_rows, hidden)
    two = lambda values: values.reshape(planes // 2, -1, values.shape[-1])

    def pairs(*items):
        kept = hold(*(kept for kept, received in items), *(received for kept, received in items))
        kept, received = kept[: len(items)], kept[len(items) :]
        own, *parts = sums(*([[(k, h), (r, h)] for k, r in zip(kept, received)] for h in halves))
        mark(own, parts)
        return [own] + cross_rows(parts)

    def halve(items, bits):
        arrays = hold(*(array for item in items for array in item))
        parts = [arrays[n : n + 2] for n in range(0, len(arrays), 2)]
        count = parts[0][0].shape[0] // 2
        outs = []
        for at in (0, count):
            slots = [[[(k, n), (r, n)] for k, r in parts] for n in range(at, at + count)]
            rows_each = sum(k.shape[1] for k, r in parts)
            joined = [sums(slot)[0] for slot in slots]
            outs.append(jnp.concatenate(joined).reshape(count, rows_each, -1))
        mark(outs)
        return outs[0], swap(outs[1], "rows", bits)

    def feed_pairs(kept, received):
        return pairs((flat_pieces(kept), flat_pieces(received)))

    def feed_near(arrays):
        arrays = hold(*arrays) if len(arrays) > 1 else [hold(arrays[0])]
        arrays = [by_plane(values) for values in arrays]
        slot = lambda k: [(array, k) for array in arrays]
        near, kept = sums([slot(k) for k in near_planes], [slot(k - 1) for k in near_planes])
        mark(near, kept)
        return two(kept), two(swap(near, "ffn", 1))

    def planes_far(kept, near):
        kept, near = hold(kept, near)
        (far,) = sums([[(kept, k), (near, k)] for k in range(1, planes // 2)])
        mark(far)
        rows_each = kept.shape[1]
        return [(kept, 0), (near, 0)] + [
            swap(far[(k - 1) * rows_each : k * rows_each], "ffn", 2 * k) for k in range(1, planes // 2)
        ]

    def total(*slots):
        flat_slots = [arg for slot in slots for arg in slot]
        arrays = hold(*(arg[0] if isinstance(arg, tuple) else arg for arg in flat_slots))
        arrays = [
            (array, arg[1]) if isinstance(arg, tuple) else array
            for array, arg in zip(arrays, flat_slots)
        ]
        taken = []
        for slot in slots:
            taken.append(arrays[: len(slot)])
            arrays = arrays[len(slot) :]
        (result,) = sums(taken)
        mark(result)
        return result

    def over_more_rows(values):
        for bit in bits_of("rows", ways):
            values = total([values, swap(values, "rows", bit)])
        return values

    def join(have, direct=True):
        parts = hold(*have)
        biases = jnp.stack([part[piece_rows] for part in parts])[:, None].astype(FULL)
        own = jnp.stack([part[:piece_rows] for part in parts[1:]])
        mark(own)
        return even_rows(own) if direct else own, biases

    def core(even):
        even = hold(*even)
        mark(even)
        return all_rows(even)

    def widen(values, bits):
        values = doubled_rows(hold(values), bits)
        mark(values)
        return values

    def all_of(even, odd):
        return [(array, n) for n in range(even.shape[0]) for array in (even, odd)]

    def split_first(kept, received):
        kept, received = hold(kept, received)
        both_sums = (kept.astype(FULL) + received.astype(FULL)).astype(LOW)
        rows = both_sums.shape[2] // 2
        left, right = both_sums[:, :, :rows], both_sums[:, :, rows:]
        parts = left[:2], left[2:], right[0::2], right[1::2]
        mark(parts)
        return parts[0], swap(parts[1], "rows", 4), parts[2], swap(parts[3], "rows", 2)

    def split_second(left, left_in, right, right_in):
        left, left_in, right, right_in = hold(left, left_in, right, right_in)
        left = (left.astype(FULL) + left_in.astype(FULL)).astype(LOW)
        right = (right.astype(FULL) + right_in.astype(FULL)).astype(LOW)
        parts = left[0], left[1], right[0], right[1]
        mark(parts)
        return parts[0], swap(parts[1], "rows", 2), parts[2], swap(parts[3], "rows", 4)

    def split_near(left, left_in, right, right_in):
        left, left_in, right, right_in = hold(left, left_in, right, right_in)
        left = left.astype(FULL) + left_in.astype(FULL)
        right = right.astype(FULL) + right_in.astype(FULL)
        whole = jnp.concatenate([left, right], 1).astype(LOW)
        kept, near = whole[0::2], whole[1::2]
        mark(kept, near)
        return kept, swap(near, "ffn", 1)

    weights_zero = first_planes(cut(0))
    h_source, kv_source = prepare(0, 0, source)
    kv_zero = first_planes(kv_source)
    weights_zero = relay(weights_zero)
    slots_zero = queries(0, h_source)
    even_zero, bias_zero = join(weights_zero)
    kv_zero = relay(kv_zero)
    mine_one = cut(1)
    weights_one = first_planes(mine_one)
    kv_target, slots_one = prepare_queries(1, 2, target)
    middle, *saved_zero = attention(0, 0, False, source, slots_zero, kv_zero, False)
    weights_one = relay(weights_one)
    kv_one = first_planes(hold(kv_target))
    pieces_zero = core(even_zero)
    weight_scratch = [pltpu.VMEM((planes, width, hidden), LOW), pltpu.VMEM((planes, hidden, width), LOW)]
    memory, memory_low, kv_memory = run(
        functools.partial(feed_forward_kernel, ways),
        [rows_like, low_like, kv_like],
        (middle, *norms, ffn_out_bias, bias_zero, (moa_keyval, 2))
        + ((ffn_in, 0), (ffn_out, 0), *pieces_zero),
        weight_scratch,
        name="encoder_feed",
    )
    kv_two = first_planes(kv_memory)
    kv_one = relay(kv_one)
    even_one, bias_one = join(weights_one)
    first_state, *saved_one, next_slots, next_gates = attention(
        1, 1, True, target, slots_one, kv_one, True
    )
    slots_two = (next_slots, next_gates)
    kv_two = relay(kv_two)
    pieces_one = core(even_one)
    second_state, *saved_two = attention(2, 0, False, first_state, slots_two, kv_two, False)

    back_scratch = weight_scratch + [pltpu.VMEM((width, hidden), FULL), pltpu.VMEM((tokens, width), FULL)]
    feed_like = [like((ways // 2, planes, piece_rows, hidden), LOW)] * 2
    feed_like += [like((planes, 1, hidden), FULL), sums_like]
    decoded, second_grad, one_kept, one_sent, bias_grad_one, sums_four = run(
        functools.partial(decoder_feed_kernel, ways, groups),
        [rows_like, rows_like] + feed_like,
        (*meta, second_state, cotangent, *norms, ffn_out_bias, bias_one)
        + ((ffn_in, 1), (ffn_out, 1), *pieces_one),
        back_scratch,
        smem=2,
        name="decoder_feed",
    )
    one_received = swap(one_sent, "rows", 1)
    d_kv_kept_two, d_kv_sent, *rows_two = attention_back(
        2, 0, False, second_grad, slots_two, saved_two, kv_two
    )
    d_kv_near_two = swap(d_kv_sent, "ffn", 1)
    one = halve([(flat_pieces(one_kept), flat_pieces(one_received))], 4)
    first_grad, kept_two, sent_two, router_two, sums_three = project_back(
        2, 3, True, second_grad, first_state, saved_two, rows_two
    )
    d_kv_two = planes_far(d_kv_kept_two, d_kv_near_two)
    d_kv_kept_one, d_kv_sent, *rows_one = attention_back(
        1, 1, True, first_grad, slots_one, saved_one, kv_one
    )
    d_kv_near_one = swap(d_kv_sent, "ffn", 1)
    self_grad, kept_one, sent_one, router_one, unused = project_back(
        1, 2, False, first_grad, target, saved_one, rows_one
    )
    later_sent = jnp.concatenate([sent_one, sent_two], 1)
    mark(later_sent)
    later_received = swap(later_sent, "rows", 1)
    (memory_grad, middle_grad, keyval_kept_two, keyval_sent_two, zero_kept, zero_sent, bias_grad_zero, sums_one) = run(
        functools.partial(encoder_feed_kernel, ways, len(d_kv_two)),
        [rows_like, rows_like] + keyval_like + feed_like,
        (middle, memory_low, *norms, bias_zero, (moa_keyval, 2), *d_kv_two)
        + ((ffn_in, 0), (ffn_out, 0), *pieces_zero),
        back_scratch + keyval_scratch,
        name="encoder_feed_back",
    )
    zero_received = swap(zero_sent, "rows", 1)
    d_kv_one = planes_far(d_kv_kept_one, d_kv_near_one)
    one = halve([one], 2)
    later = halve([(jnp.concatenate([kept_one, kept_two], 1), later_received)], 4)
    d_kv_kept_zero, d_kv_sent, *rows_zero = attention_back(
        0, 0, False, middle_grad, slots_zero, saved_zero, kv_zero
    )
    d_kv_zero = [(d_kv_kept_zero, 0)]
    d_kv_zero += [
        swap((d_kv_sent if k & 1 else d_kv_kept_zero)[k // 2], "ffn", k)
        for k in range(planes - 1, 0, -1)
    ]
    zero = halve([(flat_pieces(zero_kept), flat_pieces(zero_received))], 4)
    encoder_grad, kept_zero, sent_zero, router_zero, unused = project_back(
        0, 0, False, middle_grad, source, saved_zero, rows_zero
    )
    target_grad, keyval_kept_one, keyval_sent_one, sums_two = finish(
        1, 2, self_grad, first_grad, target, d_kv_one, True
    )
    later = halve([later], 2)
    small_rows = 40 + 16 + 3 * experts + 2 * planes
    small_rows = (small_rows + 127) // 128 * 128
    small_like = [like((ways // 2, small_rows // ways, width), LOW)] * 2
    (source_grad, keyval_kept_zero, keyval_sent_zero, small_kept, small_sent, sums_zero) = run(
        functools.partial(finish_pack_kernel, len(d_kv_zero), groups, ways, 0),
        [rows_like] + keyval_like + small_like + [sums_like],
        (*meta, encoder_grad, middle_grad, source, *norms, (moa_keyval, 0), *d_kv_zero)
        + (route_rows, sums_one, sums_two, sums_three, sums_four)
        + (router_zero, router_one, router_two, bias_grad_zero, bias_grad_one),
        keyval_scratch + [pltpu.VMEM((small_rows, width), FULL)],
        name="finish_pack",
        smem=2,
    )
    first_sent = jnp.concatenate(
        [sent_zero, keyval_sent_zero, keyval_sent_one, keyval_sent_two, small_sent], 1
    )
    first_kept = jnp.concatenate(
        [kept_zero, keyval_kept_zero, keyval_kept_one, keyval_kept_two, small_kept], 1
    )
    mark(first_sent)
    first_received = swap(first_sent, "rows", 1)
    one = total([(one[0], 0), (one[1], 0)])
    one_kept, one_near = feed_near([one])
    first_part = pairs((first_kept, first_received))
    zero = halve([zero], 2)
    later = total([(later[0], 0), (later[1], 0)])
    later_next = swap(later, "ffn", 1)
    one_parts = planes_far(one_kept, one_near)
    first_part = total(first_part)
    first_next = swap(first_part, "ffn", 1)
    zero = total([(zero[0], 0), (zero[1], 0)])
    zero_kept, zero_near = feed_near([zero])
    later = total([later, later_next])
    later_next = swap(later, "ffn", 2)
    first_part = total([first_part, first_next])
    first_next = swap(first_part, "ffn", 2)
    zero_parts = planes_far(zero_kept, zero_near)
    own = total(zero_parts, [first_part, first_next], one_parts, [later, later_next])
    own = over_more_rows(own)[None]
    half = own.shape[1] // 2
    left, right = own[:, :half], own[:, half:]
    mark(left, right)
    left, right = doubled_rows(left, 4), doubled_rows(right, 2)
    left, right = hold(left, right)
    mark(left, right)
    left, right = doubled_rows(left, 2), doubled_rows(right, 4)
    left, right = hold(left, right)
    mark(left, right)
    lefts, rights = (left, swap(left, "rows", 1)), (right, swap(right, "rows", 1))
    order = (0, 2, 1, 3)
    final_pieces = [
        [(lefts[j & 1], order[j // 2]), (rights[j & 1], j // 2)] for j in range(ways)
    ]
    grads_like = [like((2, width, hidden), FULL), like((2, hidden, width), FULL)]
    grads_like += [like((3, width, experts * head), FULL), like((3, experts * head, width), FULL)]
    grads_like += [like((3, width, both), FULL)]
    small_outs = [like((4, width), FULL), like((4, width), FULL), like((2, width), FULL)]
    small_outs += [like((3, experts, width), FULL), like((2, hidden), FULL), like((2, width), FULL)]
    small_outs += [like((3, experts), jnp.int32)]
    stay = pl.BlockSpec(memory_space=pl.ANY)
    lies = pl.BlockSpec(memory_space=pltpu.VMEM)

    outs = grads_like + small_outs
    (first_grads, second_grads, query_grads, out_grads, keyval_grads, *smalls) = run(
        functools.partial(place_kernel, ways, (0, 1, 2), small_rows, planes, experts),
        outs,
        tuple(piece for pair in final_pieces for piece in pair),
        [pltpu.VMEM((5, width, width), FULL)] * 2
        + [pltpu.VMEM((width, width), FULL), pltpu.VMEM((3, width, both), FULL)]
        + [pltpu.SemaphoreType.DMA((13,))],
        name="place",
        out_specs=[stay] * 5 + [lies] * (len(outs) - 5),
        memory=32 * 1024 * 1024,
    )
    gains, shifts, final, routers, bias_grads, out_biases, counts = smalls
    whole = lambda values: values.reshape(groups, row_count, width)
    return (
        whole(memory),
        whole(decoded),
        whole(source_grad),
        whole(target_grad),
        whole(memory_grad),
        gains,
        shifts,
        final,
        jnp.swapaxes(routers, 1, 2),
        query_grads,
        keyval_grads,
        out_grads,
        first_grads,
        bias_grads,
        second_grads,
        out_biases,
        counts,
    )


def solution(mesh):
    in_specs = (
        P("rows", "ffn", None),
        P("rows", "ffn", None),
        P("rows", "ffn", None),
        P("rows"),
        P("rows"),
        P(None, "rows", "ffn", None),
        P(),
        P(),
        P(),
        P(),
        P(),
        P(),
        P(None, None, "ffn"),
        P(None, "ffn"),
        P(None, "ffn", None),
        P(),
    )
    out_specs = (
        P("rows", "ffn", None),
        P("rows", "ffn", None),
        P("rows", "ffn", None),
        P("rows", "ffn", None),
        P("rows", "ffn", None),
        P(),
        P(),
        P(),
        P(),
        P(),
        P(),
        P(),
        P(None, None, "ffn"),
        P(None, "ffn"),
        P(None, "ffn", None),
        P(),
        P(),
    )
    return jax.shard_map(body, mesh=mesh, in_specs=in_specs, out_specs=out_specs, check_vma=False)
```

```python
import functools
import jax
import jax.numpy as jnp
from jax import lax
from jax.experimental import pallas as pl
from jax.experimental.pallas import tpu as pltpu
from jax.sharding import PartitionSpec as P

EPS = 1e-05
LOW = jnp.bfloat16
FULL = jnp.float32
VMEM_BYTES = 22 * 1024 * 1024
CUT_BYTES = 62 * 1024 * 1024
MICRO = 1 << 29
COSTS = {"cut": 1, "prepare": 1.1, "queries": 1.1, "attend": 3, "encoder_feed": 6, "decoder_feed": 12}
COSTS.update({"attend_back": 4.3, "project_back": 2.8, "encoder_feed_back": 10, "finish": 2.7})
COSTS.update({"finish_pack": 3.5, "prepare_queries": 2, "place": 4})


class Meta:
    def __init__(self, *lengths):
        self.lengths = lengths

    def __getitem__(self, n):
        if n == 0:
            return lax.rem(lax.axis_index("rows"), ways_of())
        if n == 1:
            return lax.axis_index("ffn")
        groups = self.lengths[0].shape[0]
        return self.lengths[(n - 2) // groups][(n - 2) % groups]


def mm(left, right):
    return jnp.dot(left, right, preferred_element_type=FULL)


def mm_nt(left, right):
    return lax.dot_general(left, right, (((1,), (1,)), ((), ())), preferred_element_type=FULL)


def normalise(values):
    center = values - jnp.mean(values, -1, keepdims=True)
    inverse = lax.rsqrt(jnp.mean(center * center, -1, keepdims=True) + EPS)
    return center * inverse, inverse


def norm_back(upstream, normal, inverse, gain_row):
    scaled = upstream * gain_row
    return inverse * (
        scaled
        - jnp.mean(scaled, -1, keepdims=True)
        - normal * jnp.mean(scaled * normal, -1, keepdims=True)
    )


def split_low(values):
    high = values.astype(LOW)
    return high, (values - high.astype(FULL)).astype(LOW)


def gelu_parts(pre):
    c = 0.7978845608028654
    square = pre * pre
    t = jnp.tanh(c * pre * (1.0 + 0.044715 * square))
    half = 0.5 * (1.0 + t)
    act = pre * half
    slope = half + (0.5 * c) * pre * (1.0 - t * t) * (1.0 + 0.134145 * square)
    return act, slope


def call(body, out_shape, args, scratch=(), after=(), name=None, whole=(), alias=None, out_specs=None, smem=0, memory=VMEM_BYTES):
    arrays, specs = [], []
    for n, arg in enumerate(args):
        if isinstance(arg, tuple):
            array, entry = arg
            rest = array.shape[1:]
            specs.append(
                pl.BlockSpec(
                    (None,) + rest,
                    lambda step, entry=entry, rest=rest: (entry,) + (0,) * len(rest),
                    pipeline_mode=pl.Buffered(1),
                )
            )
        else:
            array = arg
            space = pltpu.SMEM if n < smem else pltpu.HBM if n in whole else pltpu.VMEM
            specs.append(pl.BlockSpec(memory_space=space))
        arrays.append(array)
    taken, skipped = len(arrays), len(after)

    def run(*refs):
        body(Meta(*refs[:smem]), *refs[smem:taken], *refs[taken + skipped :])

    return pl.pallas_call(
        run,
        grid=(1,),
        out_shape=out_shape,
        in_specs=specs + [pl.BlockSpec(memory_space=pl.ANY)] * skipped,
        out_specs=out_specs
        or jax.tree.map(lambda _: pl.BlockSpec(memory_space=pltpu.VMEM), out_shape),
        scratch_shapes=list(scratch),
        input_output_aliases=alias or {},
        compiler_params=pltpu.CompilerParams(vmem_limit_bytes=memory),
        cost_estimate=pl.CostEstimate(
            flops=int(COSTS[name] * MICRO), bytes_accessed=1 << 16, transcendentals=0
        ),
        name=name,
    )(*arrays, *after)


def like(shape, dtype):
    return jax.ShapeDtypeStruct(shape, dtype)


def prepare_kernel(row, meta, value, gain, shift, keyval, h_out, kv_out):
    normal, _ = normalise(value[...].astype(FULL))
    h = (normal * gain[row : row + 1] + shift[row : row + 1]).astype(LOW)
    h_out[...] = h
    kv_out[...] = mm(h, keyval[...]).astype(LOW)


def cut_kernel(ways, layer, meta, first, second, bias, mine, biases, semaphores):
    rows = first.shape[1] // ways
    at = pl.ds(pl.multiple_of(meta[0] * rows, rows), rows)
    copies = [
        pltpu.make_async_copy(weight.at[layer, at, :], mine.at[pl.ds(n * rows, rows), :], semaphores.at[n])
        for n, weight in enumerate((first, second))
    ]
    copies.append(pltpu.make_async_copy(bias, biases, semaphores.at[2]))
    for copy in copies:
        copy.start()
    for copy in copies:
        copy.wait()
    mine[2 * rows :] = jnp.broadcast_to(biases[layer : layer + 1, :], (16, biases.shape[1]))


def to_slots(values, groups):
    part = values.shape[1] // groups
    blocks = []
    for g in range(groups):
        block = values[:, g * part : (g + 1) * part]
        blocks += [block, block]
    return jnp.concatenate(blocks, 1)


def slot_queries(h, route, query_proj, router_t, groups, slot_out, gate_out):
    experts = router_t.shape[0]
    queries = mm(h, query_proj).astype(LOW)
    spread = to_slots(queries.T, groups)
    head = spread.shape[0] // experts
    chosen = jnp.zeros((head, spread.shape[1]), LOW)
    for e in range(experts):
        chosen = jnp.where(route == e, spread[e * head : (e + 1) * head], chosen)
    slot_out[...] = chosen * jnp.asarray(float(head) ** -0.5, LOW)
    logits = to_slots(mm_nt(router_t, h), groups)
    ids = lax.broadcasted_iota(jnp.int32, logits.shape, 0)
    picked = jnp.sum(jnp.where(ids == route, logits, 0.0), 0, keepdims=True)
    part = picked.shape[1] // (2 * groups)
    gates = []
    for g in range(groups):
        a = picked[:, 2 * g * part : (2 * g + 1) * part]
        b = picked[:, (2 * g + 1) * part : (2 * g + 2) * part]
        top = jnp.maximum(a, b)
        ea, eb = jnp.exp(a - top), jnp.exp(b - top)
        total = ea + eb
        gates += [ea / total, eb / total]
    gate_out[...] = jnp.concatenate(gates, 1)


def allowed_keys(shape, z, part, planes, length, causal):
    blocks = []
    for k in range(planes):
        position = (z ^ k) * part + lax.broadcasted_iota(jnp.int32, (part, shape[1]), 0)
        ok = position < length
        if causal:
            lane = lax.broadcasted_iota(jnp.int32, (part, shape[1]), 1)
            query = z * part + jnp.where(lane >= part, lane - part, lane)
            ok = ok & (position <= query)
        blocks.append(ok)
    return jnp.concatenate(blocks, 0)


def attend(meta, side, causal, slots, gates, route, kv_refs, out_proj, groups, experts, lse_out, att_out):
    z = meta[1]
    part = kv_refs[0].shape[0] // groups
    planes = len(kv_refs)
    head = slots.shape[0]
    lanes = 2 * part
    columns = []
    for g in range(groups):
        kv = jnp.concatenate([ref[g * part : (g + 1) * part, :] for ref in kv_refs], 0)
        q = slots[:, g * lanes : (g + 1) * lanes]
        padded = jnp.concatenate([q, jnp.zeros_like(q)], 0)
        scores = mm(kv, padded)
        ok = allowed_keys(scores.shape, z, part, planes, meta[2 + 2 * side + g], causal)
        scores = jnp.where(ok, scores, -1e30)
        top = jnp.max(scores, 0, keepdims=True)
        raised = jnp.exp(scores - top)
        total = jnp.sum(raised, 0, keepdims=True)
        lse_out[:, g * lanes : (g + 1) * lanes] = top + jnp.log(total)
        low = (raised * (1.0 / total)).astype(LOW)
        attended = mm(kv.T, low)[head:]
        att_out[:, g * lanes : (g + 1) * lanes] = attended
        gated = attended * gates[:, g * lanes : (g + 1) * lanes]
        ids = route[:, g * lanes : (g + 1) * lanes]
        rows = []
        for e in range(experts):
            first = jnp.where(ids[:, :part] == e, gated[:, :part], 0.0)
            rows.append(jnp.where(ids[:, part:] == e, gated[:, part:], first).astype(LOW))
        columns.append(jnp.concatenate(rows, 0))
    mixed = jnp.concatenate(columns, 1)
    return mixed, mm(mixed.T, out_proj)


def prepare_queries_kernel(groups, row, meta, value, gain, shift, keyval, route, query_proj, router_t, kv_out, slot_out, gate_out):
    normal, _ = normalise(value[...].astype(FULL))
    h = (normal * gain[row : row + 1] + shift[row : row + 1]).astype(LOW)
    kv_out[...] = mm(h, keyval[...]).astype(LOW)
    slot_queries(h, route[...], query_proj[...], router_t[...], groups, slot_out, gate_out)


def queries_kernel(groups, meta, h, route, query_proj, router_t, slot_out, gate_out):
    slot_queries(h[...], route[...], query_proj[...], router_t[...], groups, slot_out, gate_out)


def attend_kernel(groups, side, causal, planes, next_queries, meta, resid, slots, gates, route, *rest):
    kv_refs, rest = rest[:planes], rest[planes:]
    out_proj, rest = rest[0], rest[1:]
    if next_queries:
        (gain, shift, next_route, next_proj, next_router, new_resid, lse_out, att_out, mixed_out, next_slots, next_gates) = rest
    else:
        (new_resid, lse_out, att_out, mixed_out) = rest
    experts = out_proj.shape[0] // slots.shape[0]
    mixed, branch = attend(meta, side, causal, slots, gates, route, kv_refs, out_proj[...], groups, experts, lse_out, att_out)
    mixed_out[...] = mixed
    total = resid[...].astype(FULL) + branch
    new_resid[...] = total
    if next_queries:
        normal, _ = normalise(total)
        h = (normal * gain[3:4] + shift[3:4]).astype(LOW)
        slot_queries(h, next_route[...], next_proj[...], next_router[...], groups, next_slots, next_gates)


def place_weights(meta, own_first, own_second, pieces, first, second):
    r = meta[0]
    first[0] = own_first[...]
    second[0] = own_second[...]
    ways = len(pieces)
    rows = own_first.shape[0] // ways
    for j, piece in enumerate(pieces):
        at = pl.ds(pl.multiple_of((r ^ j) * rows, rows), rows)
        for k in range(1, first.shape[0]):
            first[k, at, :] = piece[k - 1, :rows]
            second[k, at, :] = piece[k - 1, rows:]


def feed_forward_kernel(ways, meta, state, gain, shift, out_bias, bias, keyval, own_first, own_second, *rest):
    pieces, (memory, low_out, kv_out, first, second) = rest[:ways], rest[ways:]
    place_weights(meta, own_first, own_second, pieces, first, second)
    value = state[...]
    normal, _ = normalise(value)
    h = (normal * gain[1:2] + shift[1:2]).astype(LOW)
    memory[...] = value + out_bias[0:1].astype(FULL)

    def step(k, carry):
        pre = mm(h, first[k]) + bias[k]
        act = jax.nn.gelu(pre).astype(LOW)
        memory[...] += mm(act, second[k])
        return carry

    lax.fori_loop(0, first.shape[0], step, 0, unroll=True)
    low = memory[...].astype(LOW)
    low_out[...] = low
    kv_out[...] = mm(low, keyval[...]).astype(LOW)


def feed_backward_core(meta, h, upstream_low, ways, bias, first, second, grad, d_h, kept, sent, bias_grad, state):
    r, z = meta[0], meta[1]
    h_t = h.T
    up_t = upstream_low.T
    d_h[...] = jnp.zeros_like(d_h)
    rows = h.shape[1] // ways

    def step(k, carry):
        w_first, w_second = first[k], second[k]
        pre = mm(h, w_first) + bias[k]
        act, slope = gelu_parts(pre)
        act = act.astype(LOW)
        if state is not None:
            state[...] += mm(act, w_second)
        d_pre_full = (mm_nt(upstream_low, w_second) * slope).astype(LOW)
        d_h[...] += mm_nt(d_pre_full, w_first)
        bias_grad[z ^ k] = jnp.sum(d_pre_full.astype(FULL), 0, keepdims=True)
        for half, product in enumerate((mm(h_t, d_pre_full), mm(up_t, act))):
            grad[...] = product.astype(LOW)
            for j in range(ways):
                block = grad[pl.ds(pl.multiple_of((r ^ j) * rows, rows), rows), :]
                target = sent if j & 1 else kept
                target[j // 2, k, half * rows : (half + 1) * rows, :] = block
        return carry

    lax.fori_loop(0, first.shape[0], step, 0, unroll=True)


def decoder_feed_kernel(ways, groups, meta, state_in, cotangent, gain, shift, out_bias, bias, own_first, own_second, *rest):
    pieces, (decoded, state_grad, kept, sent, bias_grad, sums, first, second, grad, d_h) = rest[:ways], rest[ways:]
    place_weights(meta, own_first, own_second, pieces, first, second)
    value = state_in[...]
    normal, inverse = normalise(value)
    h = (normal * gain[4:5] + shift[4:5]).astype(LOW)
    decoded[...] = value + out_bias[1:2].astype(FULL)
    part = value.shape[0] // groups
    seeds = []
    for g in range(groups):
        row = meta[1] * part + lax.broadcasted_iota(jnp.int32, (part, value.shape[1]), 0)
        seeds.append(jnp.where(row < meta[4 + g], cotangent[g * part : (g + 1) * part, :].astype(FULL), 0.0))
    seed = jnp.concatenate(seeds, 0)
    feed_backward_core(meta, h, seed.astype(LOW), ways, bias, first, second, grad, d_h, kept, sent, bias_grad, decoded)
    normal, inverse = normalise(state_in[...])
    upstream = d_h[...]
    state_grad[...] = seed + norm_back(upstream, normal, inverse, gain[4:5])
    sums[0:1] = jnp.sum(upstream * normal, 0, keepdims=True)
    sums[1:2] = jnp.sum(upstream, 0, keepdims=True)
    sums[2:3] = jnp.sum(seed, 0, keepdims=True)
    sums[3:8] = jnp.zeros((5, sums.shape[1]), FULL)


def total_of(blocks):
    total = blocks[0][...].astype(FULL)
    for block in blocks[1:]:
        total = total + block[...].astype(FULL)
    return total.astype(LOW)


def write_pieces(meta, ways, values, scratch, kept, sent):
    scratch[...] = values
    rows = values.shape[0] // ways
    for j in range(ways):
        at = pl.ds(pl.multiple_of((meta[0] ^ j) * rows, rows), rows)
        place = sent if j & 1 else kept
        place[j // 2] = scratch[at, :].astype(LOW)


def encoder_feed_kernel(ways, planes, meta, state_in, memory_low, gain, shift, bias, keyval, *rest):
    blocks, rest = rest[:planes], rest[planes:]
    own_first, own_second = rest[:2]
    pieces, rest = rest[2 : 2 + ways], rest[2 + ways :]
    (memory_grad, state_grad, keyval_kept, keyval_sent, kept, sent, bias_grad, sums, first, second, grad, d_h, keyval_grad) = rest
    place_weights(meta, own_first, own_second, pieces, first, second)
    d_kv = total_of(blocks)
    upstream_in = mm_nt(d_kv, keyval[...])
    memory_grad[...] = upstream_in
    write_pieces(meta, ways, mm(d_kv.T, memory_low[...]), keyval_grad, keyval_kept, keyval_sent)
    normal, inverse = normalise(state_in[...])
    h = (normal * gain[1:2] + shift[1:2]).astype(LOW)
    feed_backward_core(meta, h, upstream_in.astype(LOW), ways, bias, first, second, grad, d_h, kept, sent, bias_grad, None)
    normal, inverse = normalise(state_in[...])
    upstream = d_h[...]
    state_grad[...] = memory_grad[...] + norm_back(upstream, normal, inverse, gain[1:2])
    sums[0:1] = jnp.sum(upstream * normal, 0, keepdims=True)
    sums[1:2] = jnp.sum(upstream, 0, keepdims=True)
    sums[2:3] = jnp.sum(memory_grad[...], 0, keepdims=True)
    sums[3:8] = jnp.zeros((5, sums.shape[1]), FULL)


def attend_back_kernel(groups, side, causal, planes, experts, meta, upstream, slots, gates, route, lse, att, *rest):
    kv_refs, rest = rest[:planes], rest[planes:]
    out_proj, d_kv_kept, d_kv_sent, query_rows_out, logit_out = rest
    z = meta[1]
    head = slots.shape[0]
    branch_grad = upstream[...].astype(LOW)
    part = branch_grad.shape[0] // groups
    lanes = 2 * part
    d_mixed = mm_nt(out_proj[...], branch_grad)
    query_columns, logit_columns = [], []
    for g in range(groups):
        here = slice(g * lanes, (g + 1) * lanes)
        ids = route[:, here]
        gate = gates[:, here]
        attended = att[:, here]
        mine = d_mixed[:, g * part : (g + 1) * part]
        spread = jnp.concatenate([mine, mine], 1)
        slot_grad = jnp.zeros((head, lanes), FULL)
        for e in range(experts):
            slot_grad = jnp.where(ids == e, spread[e * head : (e + 1) * head], slot_grad)
        gate_grad = jnp.sum(attended * slot_grad, 0, keepdims=True)
        weighted = gate * gate_grad
        both = weighted[:, :part] + weighted[:, part:]
        chosen_grad = gate * (gate_grad - jnp.concatenate([both, both], 1))
        att_grad = (gate * slot_grad).astype(LOW)
        inner = jnp.sum(att_grad.astype(FULL) * attended, 0, keepdims=True)
        q = slots[:, here]
        zeros = jnp.zeros_like(q)
        kv = jnp.concatenate([ref[g * part : (g + 1) * part, :] for ref in kv_refs], 0)
        scores = mm(kv, jnp.concatenate([q, zeros], 0))
        ok = allowed_keys(scores.shape, z, part, planes, meta[2 + 2 * side + g], causal)
        probs = jnp.exp(jnp.where(ok, scores, -1e30) - lse[:, here])
        probs_grad = mm(kv, jnp.concatenate([zeros, att_grad], 0))
        score_grad = (probs * (probs_grad - inner)).astype(LOW)
        d_kv = mm(score_grad, jnp.concatenate([q, zeros], 0).T) + mm(
            probs.astype(LOW), jnp.concatenate([zeros, att_grad], 0).T
        )
        for k in range(planes):
            place = d_kv_sent if k & 1 else d_kv_kept
            place[k // 2, g * part : (g + 1) * part, :] = d_kv[k * part : (k + 1) * part].astype(LOW)
        slot_query_grad = mm(kv.T, score_grad)[:head] * (float(head) ** -0.5)
        rows = []
        for e in range(experts):
            first = jnp.where(ids[:, :part] == e, slot_query_grad[:, :part], 0.0)
            rows.append(jnp.where(ids[:, part:] == e, slot_query_grad[:, part:], first).astype(LOW))
        query_columns.append(jnp.concatenate(rows, 0))
        expert = lax.broadcasted_iota(jnp.int32, (experts, part), 0)
        first = jnp.where(ids[:, :part] == expert, chosen_grad[:, :part], 0.0)
        logit_columns.append(jnp.where(ids[:, part:] == expert, chosen_grad[:, part:], first))
    query_rows_out[...] = jnp.concatenate(query_columns, 1)
    logit_out[...] = jnp.concatenate(logit_columns, 1)


def project_back_kernel(ways, norm_row, finish, meta, upstream, state, gain, shift, mixed, query_rows, logit_grad, query_proj, router, result, kept, sent, router_grad, sums, grad):
    normal, inverse = normalise(state[...].astype(FULL))
    h = (normal * gain[norm_row : norm_row + 1] + shift[norm_row : norm_row + 1]).astype(LOW)
    query_grad_rows = query_rows[...]
    high, low = split_low(logit_grad[...])
    router_grad[...] = mm(high, h) + mm(low, h)
    d_h = mm_nt(query_grad_rows.T, query_proj[...])
    d_h = d_h + mm(high.T, router[...]) + mm(low.T, router[...])
    rows_each = grad.shape[0] // ways
    for half in range(2):
        if half == 0:
            grad[...] = mm(query_grad_rows, h).astype(LOW)
        else:
            grad[...] = mm(mixed[...], upstream[...].astype(LOW)).astype(LOW)
        for j in range(ways):
            at = pl.ds(pl.multiple_of((meta[0] ^ j) * rows_each, rows_each), rows_each)
            place = sent if j & 1 else kept
            place[j // 2, half * rows_each : (half + 1) * rows_each, :] = grad[at, :]
    if finish:
        result[...] = upstream[...] + norm_back(d_h, normal, inverse, gain[norm_row : norm_row + 1])
        sums[0:1] = jnp.sum(d_h * normal, 0, keepdims=True)
        sums[1:2] = jnp.sum(d_h, 0, keepdims=True)
        sums[2:8] = jnp.zeros((6, sums.shape[1]), FULL)
    else:
        result[...] = d_h
        sums[...] = jnp.zeros_like(sums)


def finish_kernel(planes, ways, norm_row, pieces, meta, partial, upstream, state, gain, shift, keyval, *rest):
    blocks, rest = rest[:planes], rest[planes:]
    d_kv = total_of(blocks)
    normal, inverse = normalise(state[...].astype(FULL))
    h = (normal * gain[norm_row : norm_row + 1] + shift[norm_row : norm_row + 1]).astype(LOW)
    keyval_grad = mm(d_kv.T, h)
    if pieces:
        result, keyval_kept, keyval_sent, sums, scratch = rest
        write_pieces(meta, ways, keyval_grad, scratch, keyval_kept, keyval_sent)
    else:
        result, keyval_out, sums = rest
        keyval_out[...] = keyval_grad
    d_h = partial[...] + mm_nt(d_kv, keyval[...])
    result[...] = upstream[...] + norm_back(d_h, normal, inverse, gain[norm_row : norm_row + 1])
    sums[0:1] = jnp.sum(d_h * normal, 0, keepdims=True)
    sums[1:2] = jnp.sum(d_h, 0, keepdims=True)
    sums[2:8] = jnp.zeros((6, sums.shape[1]), FULL)


def finish_pack_kernel(planes, groups, ways, norm_row, meta, partial, upstream, state, gain, shift, keyval, *rest):
    blocks, rest = rest[:planes], rest[planes:]
    (routes, sums_one, sums_two, sums_three, sums_four, router_zero, router_one, router_two, bias_zero, bias_one) = rest[:10]
    result, keyval_kept, keyval_sent, small_kept, small_sent, sums, keyval_scratch, out = rest[10:]
    finish_kernel(planes, ways, norm_row, True, meta, partial, upstream, state, gain, shift, keyval, *blocks, result, keyval_kept, keyval_sent, sums, keyval_scratch)
    experts = router_zero.shape[0]
    count = bias_zero.shape[0]
    width = out.shape[1]
    slots_all = routes.shape[2]
    part = slots_all // (2 * groups)
    for n, ref in enumerate((sums, sums_one, sums_two, sums_three, sums_four)):
        out[8 * n : 8 * n + 8] = ref[...]
    at = 40
    expert = lax.broadcasted_iota(jnp.int32, (experts, slots_all), 0)
    lane = lax.broadcasted_iota(jnp.int32, (experts, slots_all), 1)
    position = meta[1] * part + lane % part
    hits = []
    for j in range(3):
        inside = jnp.zeros((experts, slots_all), jnp.bool_)
        for g in range(groups):
            mine = (lane // (2 * part)) == g
            inside = inside | (mine & (position < meta[2 + g + (groups if j else 0)]))
        hits.append(jnp.where((routes[j] == expert) & inside, 1.0, 0.0))
    hits.append(jnp.zeros((128 - 3 * experts, slots_all), FULL))
    hits = jnp.concatenate(hits, 0).astype(LOW)
    counts = mm_nt(jnp.ones((16, slots_all), LOW), hits).astype(jnp.int32)
    bit = lax.broadcasted_iota(jnp.int32, counts.shape, 0)
    digits = (lax.shift_right_logical(counts, bit) & 1).astype(FULL)
    out[at : at + 16, 128:] = jnp.zeros((16, width - 128), FULL)
    out[at : at + 16, :128] = digits
    at += 16
    rows = [router_zero[...], router_one[...], router_two[...]]
    rows += [bias_zero[k] for k in range(count)] + [bias_one[k] for k in range(count)]
    rows = jnp.concatenate(rows, 0)
    out[at : at + rows.shape[0]] = rows
    at += rows.shape[0]
    out[at:] = jnp.zeros((out.shape[0] - at, width), FULL)
    write_pieces(meta, ways, out[...], out, small_kept, small_sent)


def unpack(meta, total, planes, experts, gain_out, shift_out, final_out, router_out, bias_out, out_bias_out, counts_out):
    sums = [total[8 * n : 8 * n + 8] for n in range(5)]
    gain_out[...] = jnp.concatenate([sums[n][0:1] for n in range(4)], 0)
    shift_out[...] = jnp.concatenate([sums[n][1:2] for n in range(4)], 0)
    final_out[...] = sums[4][0:2]
    out_bias_out[...] = jnp.concatenate([sums[1][2:3], sums[4][2:3]], 0)
    at = 40
    digits = total[at : at + 16, :128]
    weight = lax.shift_left(jnp.int32(1), lax.broadcasted_iota(jnp.int32, digits.shape, 0))
    value = jnp.sum(digits * weight.astype(FULL), 0, keepdims=True).astype(jnp.int32)
    for j in range(3):
        counts_out[j : j + 1, :] = value[:, j * experts : (j + 1) * experts]
    at += 16
    for j in range(3):
        router_out[j] = total[at + j * experts : at + (j + 1) * experts]
    at += 3 * experts
    for layer in range(2):
        bias_out[layer : layer + 1, :] = total[pl.ds(at + layer * planes + meta[1], 1), :]


def swap(values, axis_name, bits):
    size = lax.axis_size(axis_name)
    return lax.ppermute(values, axis_name, [(i, i ^ bits) for i in range(size)])


def ways_of():
    return min(lax.axis_size("rows"), 8)


def bits_of(axis_name, first=1):
    bits, bit = [], first
    while bit < lax.axis_size(axis_name):
        bits.append(bit)
        bit *= 2
    return bits


def entry_of(item):
    return item[0][item[1]] if isinstance(item, tuple) else item


def first_planes(values):
    have = {0: values}
    have.update({bit: swap(values, "ffn", bit) for bit in bits_of("ffn")[::-1]})
    return have


def other_planes(have, received):
    for bit in bits_of("ffn")[::-1]:
        known = {k: part for k, part in received.items() if k & (bit - 1) == 0 and k & ~(2 * bit - 1)}
        received.update({k | bit: swap(part, "ffn", bit) for k, part in known.items() if k | bit not in received})
    return [{**have, **received}[k] for k in range(lax.axis_size("ffn"))]


def even_rows(own):
    return [own] + [swap(own, "rows", k) for k in range(2, ways_of(), 2)]


def all_rows(even):
    return [part for piece in even for part in (piece, swap(piece, "rows", 1))]


def doubled_rows(values, bits):
    return jnp.concatenate([values, swap(values, "rows", bits)])


def cross_rows(parts):
    return [swap(part, "rows", 2 * half + 2) for half, part in enumerate(parts)]


class Joined:
    def __init__(self, upper, lower):
        self.upper, self.lower = upper, lower

    def __getitem__(self, rows):
        count = self.upper.shape[0]
        if rows.stop <= count:
            return self.upper[rows]
        if rows.start >= count:
            return self.lower[rows.start - count : rows.stop - count]
        return jnp.concatenate([self.upper[rows.start :], self.lower[: rows.stop - count]])


def place_kernel(ways, small, small_rows, planes, experts, meta, *refs):
    halves_of, refs = refs[: 2 * ways], refs[2 * ways :]
    pieces = [Joined(*halves_of[2 * j : 2 * j + 2]) for j in range(ways)]
    plain, turned, turn, narrow, semaphores = refs[-5:]
    first_out, second_out, query_out, out_out, keyval_out, *more = refs[:-5]
    r = meta[0]
    rows = turn.shape[0] // ways
    copies = []
    base = 0

    def send(source, place):
        copies.append(pltpu.make_async_copy(source, place, semaphores.at[len(copies)]))
        copies[-1].start()

    def collect(few):
        nonlocal base
        for j, piece in enumerate(pieces):
            at = pl.ds(pl.multiple_of((r ^ j) * few, few), few)
            turn[at, :] = piece[base : base + few].astype(FULL)
        base += few

    def pair(n, flip, plain_out, turned_out):
        nonlocal base
        for j, piece in enumerate(pieces):
            at = pl.ds(pl.multiple_of((r ^ j) * rows, rows), rows)
            halves = [piece[base : base + rows].astype(FULL), piece[base + rows : base + 2 * rows].astype(FULL)]
            plain[n, at, :] = halves[1 if flip else 0]
            turn[at, :] = halves[0 if flip else 1]
        base += 2 * rows
        turned[n] = turn[...].T
        send(plain.at[n], plain_out)
        send(turned.at[n], turned_out)

    pair(0, False, first_out.at[0], second_out.at[0])
    pair(1, True, out_out.at[0], query_out.at[0])
    for n, entry in enumerate(small):
        collect(narrow.shape[2] // ways)
        narrow[n] = turn[: narrow.shape[2]].T
        send(narrow.at[n], keyval_out.at[entry])
    collect(small_rows // ways)
    unpack(meta, turn, planes, experts, *more)
    pair(2, False, first_out.at[1], second_out.at[1])
    for entry in (1, 2):
        pair(2 + entry, True, out_out.at[entry], query_out.at[entry])
    for copy in copies:
        copy.wait()


def body(
    source,
    target,
    cotangent,
    source_lengths,
    target_lengths,
    routes,
    norm_gain,
    norm_shift,
    moa_router,
    moa_query,
    moa_keyval,
    moa_out,
    ffn_in,
    ffn_in_bias,
    ffn_out,
    ffn_out_bias,
):
    groups, row_count, width = source.shape
    tokens = groups * row_count
    planes = lax.axis_size("ffn")
    ways = ways_of()
    experts = moa_router.shape[2]
    both = moa_keyval.shape[2]
    head = both // 2
    hidden = ffn_in.shape[2]
    slots_all = 2 * tokens
    meta = (source_lengths, target_lengths)
    flat = lambda values: values.reshape(tokens, width)
    source, target, cotangent = flat(source), flat(target), flat(cotangent)
    route_rows = jnp.swapaxes(routes, 2, 3).reshape(3, 1, slots_all)
    router_t = jnp.swapaxes(moa_router, 1, 2)
    norms = (norm_gain, norm_shift)

    rows_like = like((tokens, width), FULL)
    low_like = like((tokens, width), LOW)
    kv_like = like((tokens, both), LOW)
    sums_like = like((8, width), FULL)
    slot_like = [like((head, slots_all), LOW), like((1, slots_all), FULL)]

    last = []

    def run(body, out_shape, args, scratch=(), after=(), **more):
        after = tuple(after) + tuple(last)
        results = call(body, out_shape, args, scratch, after, **more)
        flat_results = jax.tree.leaves(results)
        last[:] = [min(flat_results, key=lambda array: array.size)]
        return results

    def hold(*arrays):
        held = lax.optimization_barrier((arrays, tuple(last)))[0]
        return held if len(arrays) > 1 else held[0]

    def mark(*arrays):
        last.extend(jax.tree.leaves(arrays))

    def relay(have):
        keys = [k for k in have if k]
        held = hold(*(have[k] for k in keys))
        mark(held)
        return other_planes(have, dict(zip(keys, held)))

    def sums(*outs):
        results = []
        for slots in outs:
            parts = []
            for slot in slots:
                parts.append(sum(entry_of(arg).astype(FULL) for arg in slot).astype(LOW))
            results.append(parts[0] if len(parts) == 1 else jnp.concatenate(parts))
        return results

    piece_rows = 2 * width // ways

    def cut(layer, after=()):
        return run(
            functools.partial(cut_kernel, ways, layer),
            like((piece_rows + 16, hidden), LOW),
            (ffn_in, ffn_out, ffn_in_bias),
            [pltpu.VMEM(ffn_in_bias.shape, LOW), pltpu.SemaphoreType.DMA((3,))],
            after,
            name="cut",
            whole=(0, 1, 2),
            memory=CUT_BYTES if layer == 0 else VMEM_BYTES,
        )

    def join(parts):
        biases = jnp.stack([part[piece_rows] for part in parts])[:, None].astype(FULL)
        return jnp.stack([part[:piece_rows] for part in parts[1:]]), biases

    def prepare(j, row, value, after=()):
        return run(
            functools.partial(prepare_kernel, row),
            [low_like, kv_like],
            (value, *norms, (moa_keyval, j)),
            after=after,
            name="prepare",
            memory=CUT_BYTES,
        )

    def prepare_queries(j, row, value):
        kv, *slots = run(
            functools.partial(prepare_queries_kernel, groups, row),
            [kv_like] + slot_like,
            (value, *norms, (moa_keyval, j), (route_rows, j), (moa_query, j), (router_t, j)),
            name="prepare_queries",
        )
        return kv, slots

    def queries(j, h, after=()):
        return run(
            functools.partial(queries_kernel, groups),
            slot_like,
            (h, (route_rows, j), (moa_query, j), (router_t, j)),
            after=after,
            name="queries",
        )

    kept_like = [
        rows_like,
        like((1, slots_all), FULL),
        like((head, slots_all), FULL),
        like((experts * head, tokens), LOW),
    ]

    def attention(j, side, causal, resid, slots, kv_blocks, following, after=()):
        extra, more = (), []
        if following:
            extra = (*norms, (route_rows, 2), (moa_query, 2), (router_t, 2))
            more = slot_like
        return run(
            functools.partial(attend_kernel, groups, side, causal, planes, following),
            kept_like + more,
            (*meta, resid, *slots, (route_rows, j), *kv_blocks, (moa_out, j), *extra),
            after=after,
            smem=2,
            name="attend",
        )

    def attention_back(j, side, causal, upstream, slots, saved, kv_blocks, after=()):
        lse, att, mixed = saved
        return run(
            functools.partial(attend_back_kernel, groups, side, causal, planes, experts),
            [like((planes // 2, tokens, both), LOW)] * 2
            + [like((experts * head, tokens), LOW), like((experts, tokens), FULL)],
            (*meta, upstream, *slots, (route_rows, j), lse, att, *kv_blocks, (moa_out, j)),
            after=after,
            smem=2,
            name="attend_back",
        )

    def project_back(j, norm_row, finish, upstream, state, saved, rows, after=()):
        return run(
            functools.partial(project_back_kernel, ways, norm_row, finish),
            [rows_like]
            + [like((ways // 2, piece_rows, width), LOW)] * 2
            + [like((experts, width), FULL), sums_like],
            (upstream, state, *norms, saved[2], *rows, (moa_query, j), (router_t, j)),
            [pltpu.VMEM((width, width), LOW)],
            after=after,
            name="project_back",
        )

    keyval_like = [like((ways // 2, both // ways, width), LOW)] * 2
    keyval_scratch = [pltpu.VMEM((both, width), FULL)]

    def finish(j, norm_row, partial, upstream, state, blocks, pieces, after=()):
        return run(
            functools.partial(finish_kernel, len(blocks), ways, norm_row, pieces),
            [rows_like] + (keyval_like if pieces else [like((both, width), FULL)]) + [sums_like],
            (partial, upstream, state, *norms, (moa_keyval, j), *blocks),
            keyval_scratch if pieces else [],
            after=after,
            name="finish",
        )

    halves = range(ways // 2)
    near_planes = list(range(1, planes, 2))
    flat_pieces = lambda values: values.reshape(ways // 2, planes * piece_rows, hidden)
    by_plane = lambda values: values.reshape(planes, piece_rows, hidden)
    two = lambda values: values.reshape(planes // 2, -1, values.shape[-1])

    def pairs(*items):
        kept = hold(*(kept for kept, received in items), *(received for kept, received in items))
        kept, received = kept[: len(items)], kept[len(items) :]
        own, *parts = sums(*([[(k, h), (r, h)] for k, r in zip(kept, received)] for h in halves))
        mark(own, parts)
        return [own] + cross_rows(parts)

    def halve(items, bits):
        arrays = hold(*(array for item in items for array in item))
        parts = [arrays[n : n + 2] for n in range(0, len(arrays), 2)]
        count = parts[0][0].shape[0]
        numbers = range(count)
        if bits == 4:
            numbers = numbers[: count // 2], numbers[count // 2 :]
        else:
            numbers = numbers[0::2], numbers[1::2]
        outs = []
        for mine in numbers:
            joined = [sums([[(k, n), (r, n)] for k, r in parts])[0] for n in mine]
            outs.append(jnp.concatenate(joined).reshape(count // 2, -1, parts[0][0].shape[2]))
        mark(outs)
        return outs[0], swap(outs[1], "rows", bits)

    def straight(kept, sent):
        return [(kept, 0)] + [
            swap((sent if k & 1 else kept)[k // 2], "ffn", k) for k in range(planes - 1, 0, -1)
        ]

    def feed_pairs(kept, received):
        return pairs((flat_pieces(kept), flat_pieces(received)))

    def feed_near(arrays):
        arrays = hold(*arrays) if len(arrays) > 1 else [hold(arrays[0])]
        arrays = [by_plane(values) for values in arrays]
        slot = lambda k: [(array, k) for array in arrays]
        near, kept = sums([slot(k) for k in near_planes], [slot(k - 1) for k in near_planes])
        mark(near, kept)
        return two(kept), two(swap(near, "ffn", 1))

    def planes_far(kept, near):
        kept, near = hold(kept, near)
        (far,) = sums([[(kept, k), (near, k)] for k in range(1, planes // 2)])
        mark(far)
        rows_each = kept.shape[1]
        return [(kept, 0), (near, 0)] + [
            swap(far[(k - 1) * rows_each : k * rows_each], "ffn", 2 * k) for k in range(1, planes // 2)
        ]

    def total(*slots):
        flat_slots = [arg for slot in slots for arg in slot]
        arrays = hold(*(arg[0] if isinstance(arg, tuple) else arg for arg in flat_slots))
        arrays = [
            (array, arg[1]) if isinstance(arg, tuple) else array
            for array, arg in zip(arrays, flat_slots)
        ]
        taken = []
        for slot in slots:
            taken.append(arrays[: len(slot)])
            arrays = arrays[len(slot) :]
        (result,) = sums(taken)
        mark(result)
        return result

    def over_more_rows(values):
        for bit in bits_of("rows", ways):
            values = total([values, swap(values, "rows", bit)])
        return values

    def join(have, direct=True):
        parts = hold(*have)
        biases = jnp.stack([part[piece_rows] for part in parts])[:, None].astype(FULL)
        own = jnp.stack([part[:piece_rows] for part in parts[1:]])
        mark(own)
        return even_rows(own) if direct else own, biases

    def core(even):
        even = hold(*even)
        mark(even)
        return all_rows(even)

    def widen(values, bits):
        values = doubled_rows(hold(values), bits)
        mark(values)
        return values

    def all_of(even, odd):
        return [(array, n) for n in range(even.shape[0]) for array in (even, odd)]

    def split_first(kept, received):
        kept, received = hold(kept, received)
        both_sums = (kept.astype(FULL) + received.astype(FULL)).astype(LOW)
        rows = both_sums.shape[2] // 2
        left, right = both_sums[:, :, :rows], both_sums[:, :, rows:]
        parts = left[:2], left[2:], right[0::2], right[1::2]
        mark(parts)
        return parts[0], swap(parts[1], "rows", 4), parts[2], swap(parts[3], "rows", 2)

    def split_second(left, left_in, right, right_in):
        left, left_in, right, right_in = hold(left, left_in, right, right_in)
        left = (left.astype(FULL) + left_in.astype(FULL)).astype(LOW)
        right = (right.astype(FULL) + right_in.astype(FULL)).astype(LOW)
        parts = left[0], left[1], right[0], right[1]
        mark(parts)
        return parts[0], swap(parts[1], "rows", 2), parts[2], swap(parts[3], "rows", 4)

    def split_near(left, left_in, right, right_in):
        left, left_in, right, right_in = hold(left, left_in, right, right_in)
        left = left.astype(FULL) + left_in.astype(FULL)
        right = right.astype(FULL) + right_in.astype(FULL)
        whole = jnp.concatenate([left, right], 1).astype(LOW)
        kept, near = whole[0::2], whole[1::2]
        mark(kept, near)
        return kept, swap(near, "ffn", 1)

    weights_zero = first_planes(cut(0))
    h_source, kv_source = prepare(0, 0, source)
    kv_zero = first_planes(kv_source)
    weights_zero = relay(weights_zero)
    slots_zero = queries(0, h_source)
    even_zero, bias_zero = join(weights_zero)
    kv_zero = relay(kv_zero)
    mine_one = cut(1)
    weights_one = first_planes(mine_one)
    kv_target, slots_one = prepare_queries(1, 2, target)
    middle, *saved_zero = attention(0, 0, False, source, slots_zero, kv_zero, False)
    weights_one = relay(weights_one)
    kv_one = first_planes(hold(kv_target))
    pieces_zero = core(even_zero)
    weight_scratch = [pltpu.VMEM((planes, width, hidden), LOW), pltpu.VMEM((planes, hidden, width), LOW)]
    memory, memory_low, kv_memory = run(
        functools.partial(feed_forward_kernel, ways),
        [rows_like, low_like, kv_like],
        (middle, *norms, ffn_out_bias, bias_zero, (moa_keyval, 2))
        + ((ffn_in, 0), (ffn_out, 0), *pieces_zero),
        weight_scratch,
        name="encoder_feed",
    )
    kv_two = first_planes(kv_memory)
    kv_one = relay(kv_one)
    even_one, bias_one = join(weights_one)
    first_state, *saved_one, next_slots, next_gates = attention(
        1, 1, True, target, slots_one, kv_one, True
    )
    slots_two = (next_slots, next_gates)
    kv_two = relay(kv_two)
    pieces_one = core(even_one)
    second_state, *saved_two = attention(2, 0, False, first_state, slots_two, kv_two, False)

    back_scratch = weight_scratch + [pltpu.VMEM((width, hidden), LOW), pltpu.VMEM((tokens, width), FULL)]
    feed_like = [like((ways // 2, planes, piece_rows, hidden), LOW)] * 2
    feed_like += [like((planes, 1, hidden), FULL), sums_like]
    decoded, second_grad, one_kept, one_sent, bias_grad_one, sums_four = run(
        functools.partial(decoder_feed_kernel, ways, groups),
        [rows_like, rows_like] + feed_like,
        (*meta, second_state, cotangent, *norms, ffn_out_bias, bias_one)
        + ((ffn_in, 1), (ffn_out, 1), *pieces_one),
        back_scratch,
        smem=2,
        name="decoder_feed",
    )
    one_received = swap(one_sent, "rows", 1)
    d_kv_kept_two, d_kv_sent, *rows_two = attention_back(
        2, 0, False, second_grad, slots_two, saved_two, kv_two
    )
    d_kv_two = straight(d_kv_kept_two, d_kv_sent)
    one = halve([(flat_pieces(one_kept), flat_pieces(one_received))], 4)
    first_grad, kept_two, sent_two, router_two, sums_three = project_back(
        2, 3, True, second_grad, first_state, saved_two, rows_two
    )
    d_kv_kept_one, d_kv_sent, *rows_one = attention_back(
        1, 1, True, first_grad, slots_one, saved_one, kv_one
    )
    d_kv_near_one = swap(d_kv_sent, "ffn", 1)
    self_grad, kept_one, sent_one, router_one, unused = project_back(
        1, 2, False, first_grad, target, saved_one, rows_one
    )
    later_sent = jnp.concatenate([sent_one, sent_two], 1)
    mark(later_sent)
    later_received = swap(later_sent, "rows", 1)
    (memory_grad, middle_grad, keyval_kept_two, keyval_sent_two, zero_kept, zero_sent, bias_grad_zero, sums_one) = run(
        functools.partial(encoder_feed_kernel, ways, len(d_kv_two)),
        [rows_like, rows_like] + keyval_like + feed_like,
        (middle, memory_low, *norms, bias_zero, (moa_keyval, 2), *d_kv_two)
        + ((ffn_in, 0), (ffn_out, 0), *pieces_zero),
        back_scratch + keyval_scratch,
        name="encoder_feed_back",
    )
    zero_received = swap(zero_sent, "rows", 1)
    one = halve([one], 2)
    later = halve([(jnp.concatenate([kept_one, kept_two], 1), later_received)], 4)
    d_kv_one = planes_far(d_kv_kept_one, d_kv_near_one)
    d_kv_kept_zero, d_kv_sent, *rows_zero = attention_back(
        0, 0, False, middle_grad, slots_zero, saved_zero, kv_zero
    )
    d_kv_zero = [(d_kv_kept_zero, 0)]
    d_kv_zero += [
        swap((d_kv_sent if k & 1 else d_kv_kept_zero)[k // 2], "ffn", k)
        for k in range(planes - 1, 0, -1)
    ]
    zero = halve([(flat_pieces(zero_kept), flat_pieces(zero_received))], 4)
    encoder_grad, kept_zero, sent_zero, router_zero, unused = project_back(
        0, 0, False, middle_grad, source, saved_zero, rows_zero
    )
    one = total([(one[0], 0), (one[1], 0)])
    one_kept, one_near = feed_near([one])
    target_grad, keyval_kept_one, keyval_sent_one, sums_two = finish(
        1, 2, self_grad, first_grad, target, d_kv_one, True
    )
    later = halve([later], 2)
    small_rows = 40 + 16 + 3 * experts + 2 * planes
    small_rows = (small_rows + 127) // 128 * 128
    small_like = [like((ways // 2, small_rows // ways, width), LOW)] * 2
    (source_grad, keyval_kept_zero, keyval_sent_zero, small_kept, small_sent, sums_zero) = run(
        functools.partial(finish_pack_kernel, len(d_kv_zero), groups, ways, 0),
        [rows_like] + keyval_like + small_like + [sums_like],
        (*meta, encoder_grad, middle_grad, source, *norms, (moa_keyval, 0), *d_kv_zero)
        + (route_rows, sums_one, sums_two, sums_three, sums_four)
        + (router_zero, router_one, router_two, bias_grad_zero, bias_grad_one),
        keyval_scratch + [pltpu.VMEM((small_rows, width), FULL)],
        name="finish_pack",
        smem=2,
    )
    first_sent = jnp.concatenate(
        [sent_zero, keyval_sent_zero, keyval_sent_one, keyval_sent_two, small_sent], 1
    )
    first_kept = jnp.concatenate(
        [kept_zero, keyval_kept_zero, keyval_kept_one, keyval_kept_two, small_kept], 1
    )
    mark(first_sent)
    first_received = swap(first_sent, "rows", 1)
    first_part = pairs((first_kept, first_received))
    zero = halve([zero], 2)
    later = total([(later[0], 0), (later[1], 0)])
    later_next = swap(later, "ffn", 1)
    one_parts = planes_far(one_kept, one_near)
    first_part = total(first_part)
    first_next = swap(first_part, "ffn", 1)
    zero = total([(zero[0], 0), (zero[1], 0)])
    zero_kept, zero_near = feed_near([zero])
    later = total([later, later_next])
    later_next = swap(later, "ffn", 2)
    first_part = total([first_part, first_next])
    first_next = swap(first_part, "ffn", 2)
    zero_parts = planes_far(zero_kept, zero_near)
    own = total(zero_parts, [first_part, first_next], one_parts, [later, later_next])
    own = over_more_rows(own)[None]
    half = own.shape[1] // 2
    left, right = own[:, :half], own[:, half:]
    mark(left, right)
    left, right = doubled_rows(left, 4), doubled_rows(right, 2)
    left, right = hold(left, right)
    mark(left, right)
    left, right = doubled_rows(left, 2), doubled_rows(right, 4)
    left, right = hold(left, right)
    mark(left, right)
    lefts, rights = (left, swap(left, "rows", 1)), (right, swap(right, "rows", 1))
    order = (0, 2, 1, 3)
    final_pieces = [
        [(lefts[j & 1], order[j // 2]), (rights[j & 1], j // 2)] for j in range(ways)
    ]
    grads_like = [like((2, width, hidden), FULL), like((2, hidden, width), FULL)]
    grads_like += [like((3, width, experts * head), FULL), like((3, experts * head, width), FULL)]
    grads_like += [like((3, width, both), FULL)]
    small_outs = [like((4, width), FULL), like((4, width), FULL), like((2, width), FULL)]
    small_outs += [like((3, experts, width), FULL), like((2, hidden), FULL), like((2, width), FULL)]
    small_outs += [like((3, experts), jnp.int32)]
    stay = pl.BlockSpec(memory_space=pl.ANY)
    lies = pl.BlockSpec(memory_space=pltpu.VMEM)

    outs = grads_like + small_outs
    (first_grads, second_grads, query_grads, out_grads, keyval_grads, *smalls) = run(
        functools.partial(place_kernel, ways, (0, 1, 2), small_rows, planes, experts),
        outs,
        tuple(piece for pair in final_pieces for piece in pair),
        [pltpu.VMEM((5, width, width), FULL)] * 2
        + [pltpu.VMEM((width, width), FULL), pltpu.VMEM((3, width, both), FULL)]
        + [pltpu.SemaphoreType.DMA((13,))],
        name="place",
        out_specs=[stay] * 5 + [lies] * (len(outs) - 5),
        memory=32 * 1024 * 1024,
    )
    gains, shifts, final, routers, bias_grads, out_biases, counts = smalls
    whole = lambda values: values.reshape(groups, row_count, width)
    return (
        whole(memory),
        whole(decoded),
        whole(source_grad),
        whole(target_grad),
        whole(memory_grad),
        gains,
        shifts,
        final,
        jnp.swapaxes(routers, 1, 2),
        query_grads,
        keyval_grads,
        out_grads,
        first_grads,
        bias_grads,
        second_grads,
        out_biases,
        counts,
    )


def solution(mesh):
    in_specs = (
        P("rows", "ffn", None),
        P("rows", "ffn", None),
        P("rows", "ffn", None),
        P("rows"),
        P("rows"),
        P(None, "rows", "ffn", None),
        P(),
        P(),
        P(),
        P(),
        P(),
        P(),
        P(None, None, "ffn"),
        P(None, "ffn"),
        P(None, "ffn", None),
        P(),
    )
    out_specs = (
        P("rows", "ffn", None),
        P("rows", "ffn", None),
        P("rows", "ffn", None),
        P("rows", "ffn", None),
        P("rows", "ffn", None),
        P(),
        P(),
        P(),
        P(),
        P(),
        P(),
        P(),
        P(None, None, "ffn"),
        P(None, "ffn"),
        P(None, "ffn", None),
        P(),
        P(),
    )
    return jax.shard_map(body, mesh=mesh, in_specs=in_specs, out_specs=out_specs, check_vma=False)
```

```python
import functools
import jax
import jax.numpy as jnp
from jax import lax
from jax.experimental import pallas as pl
from jax.experimental.pallas import tpu as pltpu
from jax.sharding import PartitionSpec as P

EPS = 1e-05
LOW = jnp.bfloat16
FULL = jnp.float32
VMEM_BYTES = 22 * 1024 * 1024
CUT_BYTES = 62 * 1024 * 1024
MICRO = 1 << 29
COSTS = {"cut": 1, "prepare": 1.1, "queries": 1.1, "attend": 3, "encoder_feed": 6, "decoder_feed": 12}
COSTS.update({"attend_back": 4.3, "project_back": 2.8, "encoder_feed_back": 10, "finish": 2.7})
COSTS.update({"finish_pack": 3.5, "prepare_queries": 2, "place": 4})


class Meta:
    def __init__(self, *lengths):
        self.lengths = lengths

    def __getitem__(self, n):
        if n == 0:
            return lax.rem(lax.axis_index("rows"), ways_of())
        if n == 1:
            return lax.axis_index("ffn")
        groups = self.lengths[0].shape[0]
        return self.lengths[(n - 2) // groups][(n - 2) % groups]


def mm(left, right):
    return jnp.dot(left, right, preferred_element_type=FULL)


def mm_nt(left, right):
    return lax.dot_general(left, right, (((1,), (1,)), ((), ())), preferred_element_type=FULL)


def normalise(values):
    center = values - jnp.mean(values, -1, keepdims=True)
    inverse = lax.rsqrt(jnp.mean(center * center, -1, keepdims=True) + EPS)
    return center * inverse, inverse


def norm_back(upstream, normal, inverse, gain_row):
    scaled = upstream * gain_row
    return inverse * (
        scaled
        - jnp.mean(scaled, -1, keepdims=True)
        - normal * jnp.mean(scaled * normal, -1, keepdims=True)
    )


def split_low(values):
    high = values.astype(LOW)
    return high, (values - high.astype(FULL)).astype(LOW)


def gelu_parts(pre):
    c = 0.7978845608028654
    square = pre * pre
    t = jnp.tanh(c * pre * (1.0 + 0.044715 * square))
    half = 0.5 * (1.0 + t)
    act = pre * half
    slope = half + (0.5 * c) * pre * (1.0 - t * t) * (1.0 + 0.134145 * square)
    return act, slope


def call(body, out_shape, args, scratch=(), after=(), name=None, whole=(), alias=None, out_specs=None, smem=0, memory=VMEM_BYTES):
    arrays, specs = [], []
    for n, arg in enumerate(args):
        if isinstance(arg, tuple):
            array, entry = arg
            rest = array.shape[1:]
            specs.append(
                pl.BlockSpec(
                    (None,) + rest,
                    lambda step, entry=entry, rest=rest: (entry,) + (0,) * len(rest),
                    pipeline_mode=pl.Buffered(1),
                )
            )
        else:
            array = arg
            space = pltpu.SMEM if n < smem else pltpu.HBM if n in whole else pltpu.VMEM
            specs.append(pl.BlockSpec(memory_space=space))
        arrays.append(array)
    taken, skipped = len(arrays), len(after)

    def run(*refs):
        body(Meta(*refs[:smem]), *refs[smem:taken], *refs[taken + skipped :])

    return pl.pallas_call(
        run,
        grid=(1,),
        out_shape=out_shape,
        in_specs=specs + [pl.BlockSpec(memory_space=pl.ANY)] * skipped,
        out_specs=out_specs
        or jax.tree.map(lambda _: pl.BlockSpec(memory_space=pltpu.VMEM), out_shape),
        scratch_shapes=list(scratch),
        input_output_aliases=alias or {},
        compiler_params=pltpu.CompilerParams(vmem_limit_bytes=memory),
        cost_estimate=pl.CostEstimate(
            flops=int(COSTS[name] * MICRO), bytes_accessed=1 << 16, transcendentals=0
        ),
        name=name,
    )(*arrays, *after)


def like(shape, dtype):
    return jax.ShapeDtypeStruct(shape, dtype)


def prepare_kernel(row, meta, value, gain, shift, keyval, h_out, kv_out):
    normal, _ = normalise(value[...].astype(FULL))
    h = (normal * gain[row : row + 1] + shift[row : row + 1]).astype(LOW)
    h_out[...] = h
    kv_out[...] = mm(h, keyval[...]).astype(LOW)


def cut_kernel(ways, layer, meta, first, second, bias, mine, biases, semaphores):
    rows = first.shape[1] // ways
    at = pl.ds(pl.multiple_of(meta[0] * rows, rows), rows)
    copies = [
        pltpu.make_async_copy(weight.at[layer, at, :], mine.at[pl.ds(n * rows, rows), :], semaphores.at[n])
        for n, weight in enumerate((first, second))
    ]
    copies.append(pltpu.make_async_copy(bias, biases, semaphores.at[2]))
    for copy in copies:
        copy.start()
    for copy in copies:
        copy.wait()
    mine[2 * rows :] = jnp.broadcast_to(biases[layer : layer + 1, :], (16, biases.shape[1]))


def to_slots(values, groups):
    part = values.shape[1] // groups
    blocks = []
    for g in range(groups):
        block = values[:, g * part : (g + 1) * part]
        blocks += [block, block]
    return jnp.concatenate(blocks, 1)


def slot_queries(h, route, query_proj, router_t, groups, slot_out, gate_out):
    experts = router_t.shape[0]
    queries = mm(h, query_proj).astype(LOW)
    spread = to_slots(queries.T, groups)
    head = spread.shape[0] // experts
    chosen = jnp.zeros((head, spread.shape[1]), LOW)
    for e in range(experts):
        chosen = jnp.where(route == e, spread[e * head : (e + 1) * head], chosen)
    slot_out[...] = chosen * jnp.asarray(float(head) ** -0.5, LOW)
    logits = to_slots(mm_nt(router_t, h), groups)
    ids = lax.broadcasted_iota(jnp.int32, logits.shape, 0)
    picked = jnp.sum(jnp.where(ids == route, logits, 0.0), 0, keepdims=True)
    part = picked.shape[1] // (2 * groups)
    gates = []
    for g in range(groups):
        a = picked[:, 2 * g * part : (2 * g + 1) * part]
        b = picked[:, (2 * g + 1) * part : (2 * g + 2) * part]
        top = jnp.maximum(a, b)
        ea, eb = jnp.exp(a - top), jnp.exp(b - top)
        total = ea + eb
        gates += [ea / total, eb / total]
    gate_out[...] = jnp.concatenate(gates, 1)


def allowed_keys(shape, z, part, planes, length, causal):
    blocks = []
    for k in range(planes):
        position = (z ^ k) * part + lax.broadcasted_iota(jnp.int32, (part, shape[1]), 0)
        ok = position < length
        if causal:
            lane = lax.broadcasted_iota(jnp.int32, (part, shape[1]), 1)
            query = z * part + jnp.where(lane >= part, lane - part, lane)
            ok = ok & (position <= query)
        blocks.append(ok)
    return jnp.concatenate(blocks, 0)


def attend(meta, side, causal, slots, gates, route, kv_refs, out_proj, groups, experts, lse_out, att_out):
    z = meta[1]
    part = kv_refs[0].shape[0] // groups
    planes = len(kv_refs)
    head = slots.shape[0]
    lanes = 2 * part
    columns = []
    for g in range(groups):
        kv = jnp.concatenate([ref[g * part : (g + 1) * part, :] for ref in kv_refs], 0)
        q = slots[:, g * lanes : (g + 1) * lanes]
        padded = jnp.concatenate([q, jnp.zeros_like(q)], 0)
        scores = mm(kv, padded)
        ok = allowed_keys(scores.shape, z, part, planes, meta[2 + 2 * side + g], causal)
        scores = jnp.where(ok, scores, -1e30)
        top = jnp.max(scores, 0, keepdims=True)
        raised = jnp.exp(scores - top)
        total = jnp.sum(raised, 0, keepdims=True)
        lse_out[:, g * lanes : (g + 1) * lanes] = top + jnp.log(total)
        low = (raised * (1.0 / total)).astype(LOW)
        attended = mm(kv.T, low)[head:]
        att_out[:, g * lanes : (g + 1) * lanes] = attended
        gated = attended * gates[:, g * lanes : (g + 1) * lanes]
        ids = route[:, g * lanes : (g + 1) * lanes]
        rows = []
        for e in range(experts):
            first = jnp.where(ids[:, :part] == e, gated[:, :part], 0.0)
            rows.append(jnp.where(ids[:, part:] == e, gated[:, part:], first).astype(LOW))
        columns.append(jnp.concatenate(rows, 0))
    mixed = jnp.concatenate(columns, 1)
    return mixed, mm(mixed.T, out_proj)


def prepare_queries_kernel(groups, row, meta, value, gain, shift, keyval, route, query_proj, router_t, kv_out, slot_out, gate_out):
    normal, _ = normalise(value[...].astype(FULL))
    h = (normal * gain[row : row + 1] + shift[row : row + 1]).astype(LOW)
    kv_out[...] = mm(h, keyval[...]).astype(LOW)
    slot_queries(h, route[...], query_proj[...], router_t[...], groups, slot_out, gate_out)


def queries_kernel(groups, meta, h, route, query_proj, router_t, slot_out, gate_out):
    slot_queries(h[...], route[...], query_proj[...], router_t[...], groups, slot_out, gate_out)


def attend_kernel(groups, side, causal, planes, next_queries, meta, resid, slots, gates, route, *rest):
    kv_refs, rest = rest[:planes], rest[planes:]
    out_proj, rest = rest[0], rest[1:]
    if next_queries:
        (gain, shift, next_route, next_proj, next_router, new_resid, lse_out, att_out, mixed_out, next_slots, next_gates) = rest
    else:
        (new_resid, lse_out, att_out, mixed_out) = rest
    experts = out_proj.shape[0] // slots.shape[0]
    mixed, branch = attend(meta, side, causal, slots, gates, route, kv_refs, out_proj[...], groups, experts, lse_out, att_out)
    mixed_out[...] = mixed
    total = resid[...].astype(FULL) + branch
    new_resid[...] = total
    if next_queries:
        normal, _ = normalise(total)
        h = (normal * gain[3:4] + shift[3:4]).astype(LOW)
        slot_queries(h, next_route[...], next_proj[...], next_router[...], groups, next_slots, next_gates)


def place_weights(meta, own_first, own_second, pieces, first, second):
    r = meta[0]
    first[0] = own_first[...]
    second[0] = own_second[...]
    ways = len(pieces)
    rows = own_first.shape[0] // ways
    for j, piece in enumerate(pieces):
        at = pl.ds(pl.multiple_of((r ^ j) * rows, rows), rows)
        for k in range(1, first.shape[0]):
            first[k, at, :] = piece[k - 1, :rows]
            second[k, at, :] = piece[k - 1, rows:]


def feed_forward_kernel(ways, meta, state, gain, shift, out_bias, bias, keyval, own_first, own_second, *rest):
    pieces, (memory, low_out, kv_out, first, second) = rest[:ways], rest[ways:]
    place_weights(meta, own_first, own_second, pieces, first, second)
    value = state[...]
    normal, _ = normalise(value)
    h = (normal * gain[1:2] + shift[1:2]).astype(LOW)
    memory[...] = value + out_bias[0:1].astype(FULL)

    def step(k, carry):
        pre = mm(h, first[k]) + bias[k]
        act = jax.nn.gelu(pre).astype(LOW)
        memory[...] += mm(act, second[k])
        return carry

    lax.fori_loop(0, first.shape[0], step, 0)
    low = memory[...].astype(LOW)
    low_out[...] = low
    kv_out[...] = mm(low, keyval[...]).astype(LOW)


def feed_backward_core(meta, h, upstream_low, ways, bias, first, second, grad, d_h, kept, sent, bias_grad, state):
    r, z = meta[0], meta[1]
    h_t = h.T
    up_t = upstream_low.T
    d_h[...] = jnp.zeros_like(d_h)
    rows = h.shape[1] // ways

    def step(k, carry):
        w_first, w_second = first[k], second[k]
        pre = mm(h, w_first) + bias[k]
        act, slope = gelu_parts(pre)
        act = act.astype(LOW)
        if state is not None:
            state[...] += mm(act, w_second)
        d_pre_full = (mm_nt(upstream_low, w_second) * slope).astype(LOW)
        d_h[...] += mm_nt(d_pre_full, w_first)
        bias_grad[z ^ k] = jnp.sum(d_pre_full.astype(FULL), 0, keepdims=True)
        for half, product in enumerate((mm(h_t, d_pre_full), mm(up_t, act))):
            grad[...] = product.astype(LOW)
            for j in range(ways):
                block = grad[pl.ds(pl.multiple_of((r ^ j) * rows, rows), rows), :]
                target = sent if j & 1 else kept
                target[j // 2, k, half * rows : (half + 1) * rows, :] = block
        return carry

    lax.fori_loop(0, first.shape[0], step, 0, unroll=state is not None)


def decoder_feed_kernel(ways, groups, meta, state_in, cotangent, gain, shift, out_bias, bias, own_first, own_second, *rest):
    pieces, (decoded, state_grad, kept, sent, bias_grad, sums, first, second, grad, d_h) = rest[:ways], rest[ways:]
    place_weights(meta, own_first, own_second, pieces, first, second)
    value = state_in[...]
    normal, inverse = normalise(value)
    h = (normal * gain[4:5] + shift[4:5]).astype(LOW)
    decoded[...] = value + out_bias[1:2].astype(FULL)
    part = value.shape[0] // groups
    seeds = []
    for g in range(groups):
        row = meta[1] * part + lax.broadcasted_iota(jnp.int32, (part, value.shape[1]), 0)
        seeds.append(jnp.where(row < meta[4 + g], cotangent[g * part : (g + 1) * part, :].astype(FULL), 0.0))
    seed = jnp.concatenate(seeds, 0)
    feed_backward_core(meta, h, seed.astype(LOW), ways, bias, first, second, grad, d_h, kept, sent, bias_grad, decoded)
    normal, inverse = normalise(state_in[...])
    upstream = d_h[...]
    state_grad[...] = seed + norm_back(upstream, normal, inverse, gain[4:5])
    sums[0:1] = jnp.sum(upstream * normal, 0, keepdims=True)
    sums[1:2] = jnp.sum(upstream, 0, keepdims=True)
    sums[2:3] = jnp.sum(seed, 0, keepdims=True)
    sums[3:8] = jnp.zeros((5, sums.shape[1]), FULL)


def total_of(blocks):
    total = blocks[0][...].astype(FULL)
    for block in blocks[1:]:
        total = total + block[...].astype(FULL)
    return total.astype(LOW)


def write_pieces(meta, ways, values, scratch, kept, sent):
    scratch[...] = values
    rows = values.shape[0] // ways
    for j in range(ways):
        at = pl.ds(pl.multiple_of((meta[0] ^ j) * rows, rows), rows)
        place = sent if j & 1 else kept
        place[j // 2] = scratch[at, :].astype(LOW)


def encoder_feed_kernel(ways, planes, meta, state_in, memory_low, gain, shift, bias, keyval, *rest):
    blocks, rest = rest[:planes], rest[planes:]
    own_first, own_second = rest[:2]
    pieces, rest = rest[2 : 2 + ways], rest[2 + ways :]
    (memory_grad, state_grad, keyval_kept, keyval_sent, kept, sent, bias_grad, sums, first, second, grad, d_h, keyval_grad) = rest
    place_weights(meta, own_first, own_second, pieces, first, second)
    d_kv = total_of(blocks)
    upstream_in = mm_nt(d_kv, keyval[...])
    memory_grad[...] = upstream_in
    write_pieces(meta, ways, mm(d_kv.T, memory_low[...]), keyval_grad, keyval_kept, keyval_sent)
    normal, inverse = normalise(state_in[...])
    h = (normal * gain[1:2] + shift[1:2]).astype(LOW)
    feed_backward_core(meta, h, upstream_in.astype(LOW), ways, bias, first, second, grad, d_h, kept, sent, bias_grad, None)
    normal, inverse = normalise(state_in[...])
    upstream = d_h[...]
    state_grad[...] = memory_grad[...] + norm_back(upstream, normal, inverse, gain[1:2])
    sums[0:1] = jnp.sum(upstream * normal, 0, keepdims=True)
    sums[1:2] = jnp.sum(upstream, 0, keepdims=True)
    sums[2:3] = jnp.sum(memory_grad[...], 0, keepdims=True)
    sums[3:8] = jnp.zeros((5, sums.shape[1]), FULL)


def attend_back_kernel(groups, side, causal, planes, experts, meta, upstream, slots, gates, route, lse, att, *rest):
    kv_refs, rest = rest[:planes], rest[planes:]
    out_proj, d_kv_kept, d_kv_sent, query_rows_out, logit_out = rest
    z = meta[1]
    head = slots.shape[0]
    branch_grad = upstream[...].astype(LOW)
    part = branch_grad.shape[0] // groups
    lanes = 2 * part
    d_mixed = mm_nt(out_proj[...], branch_grad)
    query_columns, logit_columns = [], []
    for g in range(groups):
        here = slice(g * lanes, (g + 1) * lanes)
        ids = route[:, here]
        gate = gates[:, here]
        attended = att[:, here]
        mine = d_mixed[:, g * part : (g + 1) * part]
        spread = jnp.concatenate([mine, mine], 1)
        slot_grad = jnp.zeros((head, lanes), FULL)
        for e in range(experts):
            slot_grad = jnp.where(ids == e, spread[e * head : (e + 1) * head], slot_grad)
        gate_grad = jnp.sum(attended * slot_grad, 0, keepdims=True)
        weighted = gate * gate_grad
        both = weighted[:, :part] + weighted[:, part:]
        chosen_grad = gate * (gate_grad - jnp.concatenate([both, both], 1))
        att_grad = (gate * slot_grad).astype(LOW)
        inner = jnp.sum(att_grad.astype(FULL) * attended, 0, keepdims=True)
        q = slots[:, here]
        zeros = jnp.zeros_like(q)
        kv = jnp.concatenate([ref[g * part : (g + 1) * part, :] for ref in kv_refs], 0)
        scores = mm(kv, jnp.concatenate([q, zeros], 0))
        ok = allowed_keys(scores.shape, z, part, planes, meta[2 + 2 * side + g], causal)
        probs = jnp.exp(jnp.where(ok, scores, -1e30) - lse[:, here])
        probs_grad = mm(kv, jnp.concatenate([zeros, att_grad], 0))
        score_grad = (probs * (probs_grad - inner)).astype(LOW)
        d_kv = mm(score_grad, jnp.concatenate([q, zeros], 0).T) + mm(
            probs.astype(LOW), jnp.concatenate([zeros, att_grad], 0).T
        )
        for k in range(planes):
            place = d_kv_sent if k & 1 else d_kv_kept
            place[k // 2, g * part : (g + 1) * part, :] = d_kv[k * part : (k + 1) * part].astype(LOW)
        slot_query_grad = mm(kv.T, score_grad)[:head] * (float(head) ** -0.5)
        rows = []
        for e in range(experts):
            first = jnp.where(ids[:, :part] == e, slot_query_grad[:, :part], 0.0)
            rows.append(jnp.where(ids[:, part:] == e, slot_query_grad[:, part:], first).astype(LOW))
        query_columns.append(jnp.concatenate(rows, 0))
        expert = lax.broadcasted_iota(jnp.int32, (experts, part), 0)
        first = jnp.where(ids[:, :part] == expert, chosen_grad[:, :part], 0.0)
        logit_columns.append(jnp.where(ids[:, part:] == expert, chosen_grad[:, part:], first))
    query_rows_out[...] = jnp.concatenate(query_columns, 1)
    logit_out[...] = jnp.concatenate(logit_columns, 1)


def project_back_kernel(ways, norm_row, finish, meta, upstream, state, gain, shift, mixed, query_rows, logit_grad, query_proj, router, result, kept, sent, router_grad, sums, grad):
    normal, inverse = normalise(state[...].astype(FULL))
    h = (normal * gain[norm_row : norm_row + 1] + shift[norm_row : norm_row + 1]).astype(LOW)
    query_grad_rows = query_rows[...]
    high, low = split_low(logit_grad[...])
    router_grad[...] = mm(high, h) + mm(low, h)
    d_h = mm_nt(query_grad_rows.T, query_proj[...])
    d_h = d_h + mm(high.T, router[...]) + mm(low.T, router[...])
    rows_each = grad.shape[0] // ways
    for half in range(2):
        if half == 0:
            grad[...] = mm(query_grad_rows, h).astype(LOW)
        else:
            grad[...] = mm(mixed[...], upstream[...].astype(LOW)).astype(LOW)
        for j in range(ways):
            at = pl.ds(pl.multiple_of((meta[0] ^ j) * rows_each, rows_each), rows_each)
            place = sent if j & 1 else kept
            place[j // 2, half * rows_each : (half + 1) * rows_each, :] = grad[at, :]
    if finish:
        result[...] = upstream[...] + norm_back(d_h, normal, inverse, gain[norm_row : norm_row + 1])
        sums[0:1] = jnp.sum(d_h * normal, 0, keepdims=True)
        sums[1:2] = jnp.sum(d_h, 0, keepdims=True)
        sums[2:8] = jnp.zeros((6, sums.shape[1]), FULL)
    else:
        result[...] = d_h
        sums[...] = jnp.zeros_like(sums)


def finish_kernel(planes, ways, norm_row, pieces, meta, partial, upstream, state, gain, shift, keyval, *rest):
    blocks, rest = rest[:planes], rest[planes:]
    d_kv = total_of(blocks)
    normal, inverse = normalise(state[...].astype(FULL))
    h = (normal * gain[norm_row : norm_row + 1] + shift[norm_row : norm_row + 1]).astype(LOW)
    keyval_grad = mm(d_kv.T, h)
    if pieces:
        result, keyval_kept, keyval_sent, sums, scratch = rest
        write_pieces(meta, ways, keyval_grad, scratch, keyval_kept, keyval_sent)
    else:
        result, keyval_out, sums = rest
        keyval_out[...] = keyval_grad
    d_h = partial[...] + mm_nt(d_kv, keyval[...])
    result[...] = upstream[...] + norm_back(d_h, normal, inverse, gain[norm_row : norm_row + 1])
    sums[0:1] = jnp.sum(d_h * normal, 0, keepdims=True)
    sums[1:2] = jnp.sum(d_h, 0, keepdims=True)
    sums[2:8] = jnp.zeros((6, sums.shape[1]), FULL)


def finish_pack_kernel(planes, groups, ways, norm_row, meta, partial, upstream, state, gain, shift, keyval, *rest):
    blocks, rest = rest[:planes], rest[planes:]
    (routes, sums_one, sums_two, sums_three, sums_four, router_zero, router_one, router_two, bias_zero, bias_one) = rest[:10]
    result, keyval_kept, keyval_sent, small_kept, small_sent, sums, keyval_scratch, out = rest[10:]
    finish_kernel(planes, ways, norm_row, True, meta, partial, upstream, state, gain, shift, keyval, *blocks, result, keyval_kept, keyval_sent, sums, keyval_scratch)
    experts = router_zero.shape[0]
    count = bias_zero.shape[0]
    width = out.shape[1]
    slots_all = routes.shape[2]
    part = slots_all // (2 * groups)
    for n, ref in enumerate((sums, sums_one, sums_two, sums_three, sums_four)):
        out[8 * n : 8 * n + 8] = ref[...]
    at = 40
    expert = lax.broadcasted_iota(jnp.int32, (experts, slots_all), 0)
    lane = lax.broadcasted_iota(jnp.int32, (experts, slots_all), 1)
    position = meta[1] * part + lane % part
    hits = []
    for j in range(3):
        inside = jnp.zeros((experts, slots_all), jnp.bool_)
        for g in range(groups):
            mine = (lane // (2 * part)) == g
            inside = inside | (mine & (position < meta[2 + g + (groups if j else 0)]))
        hits.append(jnp.where((routes[j] == expert) & inside, 1.0, 0.0))
    hits.append(jnp.zeros((128 - 3 * experts, slots_all), FULL))
    hits = jnp.concatenate(hits, 0).astype(LOW)
    counts = mm_nt(jnp.ones((16, slots_all), LOW), hits).astype(jnp.int32)
    bit = lax.broadcasted_iota(jnp.int32, counts.shape, 0)
    digits = (lax.shift_right_logical(counts, bit) & 1).astype(FULL)
    out[at : at + 16, 128:] = jnp.zeros((16, width - 128), FULL)
    out[at : at + 16, :128] = digits
    at += 16
    rows = [router_zero[...], router_one[...], router_two[...]]
    rows += [bias_zero[k] for k in range(count)] + [bias_one[k] for k in range(count)]
    rows = jnp.concatenate(rows, 0)
    out[at : at + rows.shape[0]] = rows
    at += rows.shape[0]
    out[at:] = jnp.zeros((out.shape[0] - at, width), FULL)
    write_pieces(meta, ways, out[...], out, small_kept, small_sent)


def unpack(meta, total, planes, experts, gain_out, shift_out, final_out, router_out, bias_out, out_bias_out, counts_out):
    sums = [total[8 * n : 8 * n + 8] for n in range(5)]
    gain_out[...] = jnp.concatenate([sums[n][0:1] for n in range(4)], 0)
    shift_out[...] = jnp.concatenate([sums[n][1:2] for n in range(4)], 0)
    final_out[...] = sums[4][0:2]
    out_bias_out[...] = jnp.concatenate([sums[1][2:3], sums[4][2:3]], 0)
    at = 40
    digits = total[at : at + 16, :128]
    weight = lax.shift_left(jnp.int32(1), lax.broadcasted_iota(jnp.int32, digits.shape, 0))
    value = jnp.sum(digits * weight.astype(FULL), 0, keepdims=True).astype(jnp.int32)
    for j in range(3):
        counts_out[j : j + 1, :] = value[:, j * experts : (j + 1) * experts]
    at += 16
    for j in range(3):
        router_out[j] = total[at + j * experts : at + (j + 1) * experts]
    at += 3 * experts
    for layer in range(2):
        bias_out[layer : layer + 1, :] = total[pl.ds(at + layer * planes + meta[1], 1), :]


def swap(values, axis_name, bits):
    size = lax.axis_size(axis_name)
    return lax.ppermute(values, axis_name, [(i, i ^ bits) for i in range(size)])


def ways_of():
    return min(lax.axis_size("rows"), 8)


def bits_of(axis_name, first=1):
    bits, bit = [], first
    while bit < lax.axis_size(axis_name):
        bits.append(bit)
        bit *= 2
    return bits


def entry_of(item):
    return item[0][item[1]] if isinstance(item, tuple) else item


def first_planes(values):
    have = {0: values}
    have.update({bit: swap(values, "ffn", bit) for bit in bits_of("ffn")[::-1]})
    return have


def other_planes(have, received):
    for bit in bits_of("ffn")[::-1]:
        known = {k: part for k, part in received.items() if k & (bit - 1) == 0 and k & ~(2 * bit - 1)}
        received.update({k | bit: swap(part, "ffn", bit) for k, part in known.items() if k | bit not in received})
    return [{**have, **received}[k] for k in range(lax.axis_size("ffn"))]


def even_rows(own):
    return [own] + [swap(own, "rows", k) for k in range(2, ways_of(), 2)]


def all_rows(even):
    return [part for piece in even for part in (piece, swap(piece, "rows", 1))]


def doubled_rows(values, bits):
    return jnp.concatenate([values, swap(values, "rows", bits)])


def cross_rows(parts):
    return [swap(part, "rows", 2 * half + 2) for half, part in enumerate(parts)]


class Joined:
    def __init__(self, upper, lower):
        self.upper, self.lower = upper, lower

    def __getitem__(self, rows):
        count = self.upper.shape[0]
        if rows.stop <= count:
            return self.upper[rows]
        if rows.start >= count:
            return self.lower[rows.start - count : rows.stop - count]
        return jnp.concatenate([self.upper[rows.start :], self.lower[: rows.stop - count]])


def place_kernel(ways, small, small_rows, planes, experts, meta, *refs):
    halves_of, refs = refs[: 2 * ways], refs[2 * ways :]
    pieces = [Joined(*halves_of[2 * j : 2 * j + 2]) for j in range(ways)]
    plain, turned, turn, narrow, semaphores = refs[-5:]
    first_out, second_out, query_out, out_out, keyval_out, *more = refs[:-5]
    r = meta[0]
    rows = turn.shape[0] // ways
    copies = []
    base = 0

    def send(source, place):
        copies.append(pltpu.make_async_copy(source, place, semaphores.at[len(copies)]))
        copies[-1].start()

    def collect(few):
        nonlocal base
        for j, piece in enumerate(pieces):
            at = pl.ds(pl.multiple_of((r ^ j) * few, few), few)
            turn[at, :] = piece[base : base + few].astype(FULL)
        base += few

    def pair(n, flip, plain_out, turned_out):
        nonlocal base
        for j, piece in enumerate(pieces):
            at = pl.ds(pl.multiple_of((r ^ j) * rows, rows), rows)
            halves = [piece[base : base + rows].astype(FULL), piece[base + rows : base + 2 * rows].astype(FULL)]
            plain[n, at, :] = halves[1 if flip else 0]
            turn[at, :] = halves[0 if flip else 1]
        base += 2 * rows
        turned[n] = turn[...].T
        send(plain.at[n], plain_out)
        send(turned.at[n], turned_out)

    pair(0, False, first_out.at[0], second_out.at[0])
    pair(1, True, out_out.at[0], query_out.at[0])
    for n, entry in enumerate(small):
        collect(narrow.shape[2] // ways)
        narrow[n] = turn[: narrow.shape[2]].T
        send(narrow.at[n], keyval_out.at[entry])
    collect(small_rows // ways)
    unpack(meta, turn, planes, experts, *more)
    pair(2, False, first_out.at[1], second_out.at[1])
    for entry in (1, 2):
        pair(2 + entry, True, out_out.at[entry], query_out.at[entry])
    for copy in copies:
        copy.wait()


def body(
    source,
    target,
    cotangent,
    source_lengths,
    target_lengths,
    routes,
    norm_gain,
    norm_shift,
    moa_router,
    moa_query,
    moa_keyval,
    moa_out,
    ffn_in,
    ffn_in_bias,
    ffn_out,
    ffn_out_bias,
):
    groups, row_count, width = source.shape
    tokens = groups * row_count
    planes = lax.axis_size("ffn")
    ways = ways_of()
    experts = moa_router.shape[2]
    both = moa_keyval.shape[2]
    head = both // 2
    hidden = ffn_in.shape[2]
    slots_all = 2 * tokens
    meta = (source_lengths, target_lengths)
    flat = lambda values: values.reshape(tokens, width)
    source, target, cotangent = flat(source), flat(target), flat(cotangent)
    route_rows = jnp.swapaxes(routes, 2, 3).reshape(3, 1, slots_all)
    router_t = jnp.swapaxes(moa_router, 1, 2)
    norms = (norm_gain, norm_shift)

    rows_like = like((tokens, width), FULL)
    low_like = like((tokens, width), LOW)
    kv_like = like((tokens, both), LOW)
    sums_like = like((8, width), FULL)
    slot_like = [like((head, slots_all), LOW), like((1, slots_all), FULL)]

    last = []

    def run(body, out_shape, args, scratch=(), after=(), **more):
        after = tuple(after) + tuple(last)
        results = call(body, out_shape, args, scratch, after, **more)
        flat_results = jax.tree.leaves(results)
        last[:] = [min(flat_results, key=lambda array: array.size)]
        return results

    def hold(*arrays):
        held = lax.optimization_barrier((arrays, tuple(last)))[0]
        return held if len(arrays) > 1 else held[0]

    def mark(*arrays):
        last.extend(jax.tree.leaves(arrays))

    def relay(have):
        keys = [k for k in have if k]
        held = hold(*(have[k] for k in keys))
        mark(held)
        return other_planes(have, dict(zip(keys, held)))

    def sums(*outs):
        results = []
        for slots in outs:
            parts = []
            for slot in slots:
                parts.append(sum(entry_of(arg).astype(FULL) for arg in slot).astype(LOW))
            results.append(parts[0] if len(parts) == 1 else jnp.concatenate(parts))
        return results

    piece_rows = 2 * width // ways

    def cut(layer, after=()):
        return run(
            functools.partial(cut_kernel, ways, layer),
            like((piece_rows + 16, hidden), LOW),
            (ffn_in, ffn_out, ffn_in_bias),
            [pltpu.VMEM(ffn_in_bias.shape, LOW), pltpu.SemaphoreType.DMA((3,))],
            after,
            name="cut",
            whole=(0, 1, 2),
            memory=CUT_BYTES if layer == 0 else VMEM_BYTES,
        )

    def join(parts):
        biases = jnp.stack([part[piece_rows] for part in parts])[:, None].astype(FULL)
        return jnp.stack([part[:piece_rows] for part in parts[1:]]), biases

    def prepare(j, row, value, after=()):
        return run(
            functools.partial(prepare_kernel, row),
            [low_like, kv_like],
            (value, *norms, (moa_keyval, j)),
            after=after,
            name="prepare",
            memory=CUT_BYTES,
        )

    def prepare_queries(j, row, value):
        kv, *slots = run(
            functools.partial(prepare_queries_kernel, groups, row),
            [kv_like] + slot_like,
            (value, *norms, (moa_keyval, j), (route_rows, j), (moa_query, j), (router_t, j)),
            name="prepare_queries",
        )
        return kv, slots

    def queries(j, h, after=()):
        return run(
            functools.partial(queries_kernel, groups),
            slot_like,
            (h, (route_rows, j), (moa_query, j), (router_t, j)),
            after=after,
            name="queries",
        )

    kept_like = [
        rows_like,
        like((1, slots_all), FULL),
        like((head, slots_all), FULL),
        like((experts * head, tokens), LOW),
    ]

    def attention(j, side, causal, resid, slots, kv_blocks, following, after=()):
        extra, more = (), []
        if following:
            extra = (*norms, (route_rows, 2), (moa_query, 2), (router_t, 2))
            more = slot_like
        return run(
            functools.partial(attend_kernel, groups, side, causal, planes, following),
            kept_like + more,
            (*meta, resid, *slots, (route_rows, j), *kv_blocks, (moa_out, j), *extra),
            after=after,
            smem=2,
            name="attend",
        )

    def attention_back(j, side, causal, upstream, slots, saved, kv_blocks, after=()):
        lse, att, mixed = saved
        return run(
            functools.partial(attend_back_kernel, groups, side, causal, planes, experts),
            [like((planes // 2, tokens, both), LOW)] * 2
            + [like((experts * head, tokens), LOW), like((experts, tokens), FULL)],
            (*meta, upstream, *slots, (route_rows, j), lse, att, *kv_blocks, (moa_out, j)),
            after=after,
            smem=2,
            name="attend_back",
        )

    def project_back(j, norm_row, finish, upstream, state, saved, rows, after=()):
        return run(
            functools.partial(project_back_kernel, ways, norm_row, finish),
            [rows_like]
            + [like((ways // 2, piece_rows, width), LOW)] * 2
            + [like((experts, width), FULL), sums_like],
            (upstream, state, *norms, saved[2], *rows, (moa_query, j), (router_t, j)),
            [pltpu.VMEM((width, width), LOW)],
            after=after,
            name="project_back",
        )

    keyval_like = [like((ways // 2, both // ways, width), LOW)] * 2
    keyval_scratch = [pltpu.VMEM((both, width), FULL)]

    def finish(j, norm_row, partial, upstream, state, blocks, pieces, after=()):
        return run(
            functools.partial(finish_kernel, len(blocks), ways, norm_row, pieces),
            [rows_like] + (keyval_like if pieces else [like((both, width), FULL)]) + [sums_like],
            (partial, upstream, state, *norms, (moa_keyval, j), *blocks),
            keyval_scratch if pieces else [],
            after=after,
            name="finish",
        )

    halves = range(ways // 2)
    near_planes = list(range(1, planes, 2))
    flat_pieces = lambda values: values.reshape(ways // 2, planes * piece_rows, hidden)
    by_plane = lambda values: values.reshape(planes, piece_rows, hidden)
    two = lambda values: values.reshape(planes // 2, -1, values.shape[-1])

    def pairs(*items):
        kept = hold(*(kept for kept, received in items), *(received for kept, received in items))
        kept, received = kept[: len(items)], kept[len(items) :]
        own, *parts = sums(*([[(k, h), (r, h)] for k, r in zip(kept, received)] for h in halves))
        mark(own, parts)
        return [own] + cross_rows(parts)

    def halve(items, bits):
        arrays = hold(*(array for item in items for array in item))
        parts = [arrays[n : n + 2] for n in range(0, len(arrays), 2)]
        count = parts[0][0].shape[0]
        numbers = range(count)
        if bits == 4:
            numbers = numbers[: count // 2], numbers[count // 2 :]
        else:
            numbers = numbers[0::2], numbers[1::2]
        outs = []
        for mine in numbers:
            joined = [sums([[(k, n), (r, n)] for k, r in parts])[0] for n in mine]
            outs.append(jnp.concatenate(joined).reshape(count // 2, -1, parts[0][0].shape[2]))
        mark(outs)
        return outs[0], swap(outs[1], "rows", bits)

    def straight(kept, sent):
        return [(kept, 0)] + [
            swap((sent if k & 1 else kept)[k // 2], "ffn", k) for k in range(planes - 1, 0, -1)
        ]

    def feed_pairs(kept, received):
        return pairs((flat_pieces(kept), flat_pieces(received)))

    def feed_near(arrays):
        arrays = hold(*arrays) if len(arrays) > 1 else [hold(arrays[0])]
        arrays = [by_plane(values) for values in arrays]
        slot = lambda k: [(array, k) for array in arrays]
        near, kept = sums([slot(k) for k in near_planes], [slot(k - 1) for k in near_planes])
        mark(near, kept)
        return two(kept), two(swap(near, "ffn", 1))

    def planes_far(kept, near):
        kept, near = hold(kept, near)
        (far,) = sums([[(kept, k), (near, k)] for k in range(1, planes // 2)])
        mark(far)
        rows_each = kept.shape[1]
        return [(kept, 0), (near, 0)] + [
            swap(far[(k - 1) * rows_each : k * rows_each], "ffn", 2 * k) for k in range(1, planes // 2)
        ]

    def total(*slots):
        flat_slots = [arg for slot in slots for arg in slot]
        arrays = hold(*(arg[0] if isinstance(arg, tuple) else arg for arg in flat_slots))
        arrays = [
            (array, arg[1]) if isinstance(arg, tuple) else array
            for array, arg in zip(arrays, flat_slots)
        ]
        taken = []
        for slot in slots:
            taken.append(arrays[: len(slot)])
            arrays = arrays[len(slot) :]
        (result,) = sums(taken)
        mark(result)
        return result

    def over_more_rows(values):
        for bit in bits_of("rows", ways):
            values = total([values, swap(values, "rows", bit)])
        return values

    def join(have, direct=True):
        parts = hold(*have)
        biases = jnp.stack([part[piece_rows] for part in parts])[:, None].astype(FULL)
        own = jnp.stack([part[:piece_rows] for part in parts[1:]])
        mark(own)
        return even_rows(own) if direct else own, biases

    def core(even):
        even = hold(*even)
        mark(even)
        return all_rows(even)

    def widen(values, bits):
        values = doubled_rows(hold(values), bits)
        mark(values)
        return values

    def all_of(even, odd):
        return [(array, n) for n in range(even.shape[0]) for array in (even, odd)]

    def split_first(kept, received):
        kept, received = hold(kept, received)
        both_sums = (kept.astype(FULL) + received.astype(FULL)).astype(LOW)
        rows = both_sums.shape[2] // 2
        left, right = both_sums[:, :, :rows], both_sums[:, :, rows:]
        parts = left[:2], left[2:], right[0::2], right[1::2]
        mark(parts)
        return parts[0], swap(parts[1], "rows", 4), parts[2], swap(parts[3], "rows", 2)

    def split_second(left, left_in, right, right_in):
        left, left_in, right, right_in = hold(left, left_in, right, right_in)
        left = (left.astype(FULL) + left_in.astype(FULL)).astype(LOW)
        right = (right.astype(FULL) + right_in.astype(FULL)).astype(LOW)
        parts = left[0], left[1], right[0], right[1]
        mark(parts)
        return parts[0], swap(parts[1], "rows", 2), parts[2], swap(parts[3], "rows", 4)

    def split_near(left, left_in, right, right_in):
        left, left_in, right, right_in = hold(left, left_in, right, right_in)
        left = left.astype(FULL) + left_in.astype(FULL)
        right = right.astype(FULL) + right_in.astype(FULL)
        whole = jnp.concatenate([left, right], 1).astype(LOW)
        kept, near = whole[0::2], whole[1::2]
        mark(kept, near)
        return kept, swap(near, "ffn", 1)

    weights_zero = first_planes(cut(0))
    h_source, kv_source = prepare(0, 0, source)
    kv_zero = first_planes(kv_source)
    weights_zero = relay(weights_zero)
    slots_zero = queries(0, h_source)
    even_zero, bias_zero = join(weights_zero)
    kv_zero = relay(kv_zero)
    mine_one = cut(1)
    weights_one = first_planes(mine_one)
    kv_target, slots_one = prepare_queries(1, 2, target)
    middle, *saved_zero = attention(0, 0, False, source, slots_zero, kv_zero, False)
    weights_one = relay(weights_one)
    kv_one = first_planes(hold(kv_target))
    pieces_zero = core(even_zero)
    weight_scratch = [pltpu.VMEM((planes, width, hidden), LOW), pltpu.VMEM((planes, hidden, width), LOW)]
    memory, memory_low, kv_memory = run(
        functools.partial(feed_forward_kernel, ways),
        [rows_like, low_like, kv_like],
        (middle, *norms, ffn_out_bias, bias_zero, (moa_keyval, 2))
        + ((ffn_in, 0), (ffn_out, 0), *pieces_zero),
        weight_scratch,
        name="encoder_feed",
    )
    kv_two = first_planes(kv_memory)
    kv_one = relay(kv_one)
    even_one, bias_one = join(weights_one)
    first_state, *saved_one, next_slots, next_gates = attention(
        1, 1, True, target, slots_one, kv_one, True
    )
    slots_two = (next_slots, next_gates)
    kv_two = relay(kv_two)
    pieces_one = core(even_one)
    second_state, *saved_two = attention(2, 0, False, first_state, slots_two, kv_two, False)

    back_scratch = weight_scratch + [pltpu.VMEM((width, hidden), LOW), pltpu.VMEM((tokens, width), FULL)]
    feed_like = [like((ways // 2, planes, piece_rows, hidden), LOW)] * 2
    feed_like += [like((planes, 1, hidden), FULL), sums_like]
    decoded, second_grad, one_kept, one_sent, bias_grad_one, sums_four = run(
        functools.partial(decoder_feed_kernel, ways, groups),
        [rows_like, rows_like] + feed_like,
        (*meta, second_state, cotangent, *norms, ffn_out_bias, bias_one)
        + ((ffn_in, 1), (ffn_out, 1), *pieces_one),
        back_scratch,
        smem=2,
        name="decoder_feed",
    )
    one_received = swap(one_sent, "rows", 1)
    d_kv_kept_two, d_kv_sent, *rows_two = attention_back(
        2, 0, False, second_grad, slots_two, saved_two, kv_two
    )
    d_kv_two = straight(d_kv_kept_two, d_kv_sent)
    one = halve([(flat_pieces(one_kept), flat_pieces(one_received))], 4)
    first_grad, kept_two, sent_two, router_two, sums_three = project_back(
        2, 3, True, second_grad, first_state, saved_two, rows_two
    )
    d_kv_kept_one, d_kv_sent, *rows_one = attention_back(
        1, 1, True, first_grad, slots_one, saved_one, kv_one
    )
    d_kv_near_one = swap(d_kv_sent, "ffn", 1)
    self_grad, kept_one, sent_one, router_one, unused = project_back(
        1, 2, False, first_grad, target, saved_one, rows_one
    )
    later_sent = jnp.concatenate([sent_one, sent_two], 1)
    mark(later_sent)
    later_received = swap(later_sent, "rows", 1)
    (memory_grad, middle_grad, keyval_kept_two, keyval_sent_two, zero_kept, zero_sent, bias_grad_zero, sums_one) = run(
        functools.partial(encoder_feed_kernel, ways, len(d_kv_two)),
        [rows_like, rows_like] + keyval_like + feed_like,
        (middle, memory_low, *norms, bias_zero, (moa_keyval, 2), *d_kv_two)
        + ((ffn_in, 0), (ffn_out, 0), *pieces_zero),
        back_scratch + keyval_scratch,
        name="encoder_feed_back",
    )
    zero_received = swap(zero_sent, "rows", 1)
    one = halve([one], 2)
    later = halve([(jnp.concatenate([kept_one, kept_two], 1), later_received)], 4)
    d_kv_one = planes_far(d_kv_kept_one, d_kv_near_one)
    d_kv_kept_zero, d_kv_sent, *rows_zero = attention_back(
        0, 0, False, middle_grad, slots_zero, saved_zero, kv_zero
    )
    d_kv_zero = [(d_kv_kept_zero, 0)]
    d_kv_zero += [
        swap((d_kv_sent if k & 1 else d_kv_kept_zero)[k // 2], "ffn", k)
        for k in range(planes - 1, 0, -1)
    ]
    zero = halve([(flat_pieces(zero_kept), flat_pieces(zero_received))], 4)
    encoder_grad, kept_zero, sent_zero, router_zero, unused = project_back(
        0, 0, False, middle_grad, source, saved_zero, rows_zero
    )
    one = total([(one[0], 0), (one[1], 0)])
    one_kept, one_near = feed_near([one])
    target_grad, keyval_kept_one, keyval_sent_one, sums_two = finish(
        1, 2, self_grad, first_grad, target, d_kv_one, True
    )
    later = halve([later], 2)
    small_rows = 40 + 16 + 3 * experts + 2 * planes
    small_rows = (small_rows + 127) // 128 * 128
    small_like = [like((ways // 2, small_rows // ways, width), LOW)] * 2
    (source_grad, keyval_kept_zero, keyval_sent_zero, small_kept, small_sent, sums_zero) = run(
        functools.partial(finish_pack_kernel, len(d_kv_zero), groups, ways, 0),
        [rows_like] + keyval_like + small_like + [sums_like],
        (*meta, encoder_grad, middle_grad, source, *norms, (moa_keyval, 0), *d_kv_zero)
        + (route_rows, sums_one, sums_two, sums_three, sums_four)
        + (router_zero, router_one, router_two, bias_grad_zero, bias_grad_one),
        keyval_scratch + [pltpu.VMEM((small_rows, width), FULL)],
        name="finish_pack",
        smem=2,
    )
    first_sent = jnp.concatenate(
        [sent_zero, keyval_sent_zero, keyval_sent_one, keyval_sent_two, small_sent], 1
    )
    first_kept = jnp.concatenate(
        [kept_zero, keyval_kept_zero, keyval_kept_one, keyval_kept_two, small_kept], 1
    )
    mark(first_sent)
    first_received = swap(first_sent, "rows", 1)
    first_part = pairs((first_kept, first_received))
    zero = halve([zero], 2)
    later = total([(later[0], 0), (later[1], 0)])
    later_next = swap(later, "ffn", 1)
    one_parts = planes_far(one_kept, one_near)
    first_part = total(first_part)
    first_next = swap(first_part, "ffn", 1)
    zero = total([(zero[0], 0), (zero[1], 0)])
    zero_kept, zero_near = feed_near([zero])
    later = total([later, later_next])
    later_next = swap(later, "ffn", 2)
    first_part = total([first_part, first_next])
    first_next = swap(first_part, "ffn", 2)
    zero_parts = planes_far(zero_kept, zero_near)
    own = total(zero_parts, [first_part, first_next], one_parts, [later, later_next])
    own = over_more_rows(own)[None]
    half = own.shape[1] // 2
    left, right = own[:, :half], own[:, half:]
    mark(left, right)
    left, right = doubled_rows(left, 4), doubled_rows(right, 2)
    left, right = hold(left, right)
    mark(left, right)
    left, right = doubled_rows(left, 2), doubled_rows(right, 4)
    left, right = hold(left, right)
    mark(left, right)
    lefts, rights = (left, swap(left, "rows", 1)), (right, swap(right, "rows", 1))
    order = (0, 2, 1, 3)
    final_pieces = [
        [(lefts[j & 1], order[j // 2]), (rights[j & 1], j // 2)] for j in range(ways)
    ]
    grads_like = [like((2, width, hidden), FULL), like((2, hidden, width), FULL)]
    grads_like += [like((3, width, experts * head), FULL), like((3, experts * head, width), FULL)]
    grads_like += [like((3, width, both), FULL)]
    small_outs = [like((4, width), FULL), like((4, width), FULL), like((2, width), FULL)]
    small_outs += [like((3, experts, width), FULL), like((2, hidden), FULL), like((2, width), FULL)]
    small_outs += [like((3, experts), jnp.int32)]
    stay = pl.BlockSpec(memory_space=pl.ANY)
    lies = pl.BlockSpec(memory_space=pltpu.VMEM)

    outs = grads_like + small_outs
    (first_grads, second_grads, query_grads, out_grads, keyval_grads, *smalls) = run(
        functools.partial(place_kernel, ways, (0, 1, 2), small_rows, planes, experts),
        outs,
        tuple(piece for pair in final_pieces for piece in pair),
        [pltpu.VMEM((5, width, width), FULL)] * 2
        + [pltpu.VMEM((width, width), FULL), pltpu.VMEM((3, width, both), FULL)]
        + [pltpu.SemaphoreType.DMA((13,))],
        name="place",
        out_specs=[stay] * 5 + [lies] * (len(outs) - 5),
        memory=32 * 1024 * 1024,
    )
    gains, shifts, final, routers, bias_grads, out_biases, counts = smalls
    whole = lambda values: values.reshape(groups, row_count, width)
    return (
        whole(memory),
        whole(decoded),
        whole(source_grad),
        whole(target_grad),
        whole(memory_grad),
        gains,
        shifts,
        final,
        jnp.swapaxes(routers, 1, 2),
        query_grads,
        keyval_grads,
        out_grads,
        first_grads,
        bias_grads,
        second_grads,
        out_biases,
        counts,
    )


def solution(mesh):
    in_specs = (
        P("rows", "ffn", None),
        P("rows", "ffn", None),
        P("rows", "ffn", None),
        P("rows"),
        P("rows"),
        P(None, "rows", "ffn", None),
        P(),
        P(),
        P(),
        P(),
        P(),
        P(),
        P(None, None, "ffn"),
        P(None, "ffn"),
        P(None, "ffn", None),
        P(),
    )
    out_specs = (
        P("rows", "ffn", None),
        P("rows", "ffn", None),
        P("rows", "ffn", None),
        P("rows", "ffn", None),
        P("rows", "ffn", None),
        P(),
        P(),
        P(),
        P(),
        P(),
        P(),
        P(),
        P(None, None, "ffn"),
        P(None, "ffn"),
        P(None, "ffn", None),
        P(),
        P(),
    )
    return jax.shard_map(body, mesh=mesh, in_specs=in_specs, out_specs=out_specs, check_vma=False)
```
